128 devices in a mesh: rep: 4 (over x), space: 32 (over z, y, core).
Axes of the slice: x: 4, y: 4, z: 4, core: 2. Of those that a mesh axis runs over, the one named last changes fastest.
Arguments:
- latents: bfloat16 [512, 512, 256], P(('rep', 'space')), may hold values from -6 to 6
- cotangent: bfloat16 [512, 512, 256], P(('rep', 'space')), may hold values from -6 to 6
- w_up: bfloat16 [2, 256, 1024], replicated, may hold values from -0.375 to 0.375
- w_down: bfloat16 [2, 1024, 256], replicated, may hold values from -0.1875 to 0.1875
- depth_w: float32 [2, 7, 256], replicated, may hold values from -2 to 2
- time_table: float32 [1000, 256], replicated, may hold values from -6 to 6
- timesteps: int32 [4], P('rep'), may hold values from 0 to 999
- brick_counts: int32 [128], P(('rep', 'space')), may hold values from 1 to 4, as said below
- send_list: int32 [128, 2, 2], P(('rep', 'space')), may hold values from 0 to 13, as said below
- recv_list: int32 [512, 4], P(('rep', 'space')), may hold values from 0 to 20, as said below
Outputs:
- d_latents: bfloat16 [512, 512, 256], P(('rep', 'space'))
- grad_up: float32 [2, 256, 1024], P(None, None, 'rep')
- grad_down: float32 [2, 1024, 256], P(None, 'rep')
- grad_depth: float32 [2, 7, 256], P(None, None, 'rep')
The draws below stay inside these ranges and needn't reach their ends.
Inputs may be any that keep to these rules, and one draw needn't show every extreme that they name: `brick_counts`: some device of every scene holds 4 bricks and some holds one. `send_list`: entry 4 s + f names face f of local slot s; list 0 goes to the device below along space, list 1 to the device above. `recv_list`: 0 means no neighbour, 1 + 4 s + f face f of local slot s, 17 + e entry e received from the device below, 19 + e entry e from the device above. Empty slots have 0 on every side. Whenever a slot names a face across a side, the brick of that face names this slot's facing face across the opposite side.
All inputs are finite; a program needn't handle non-finite values.
Results may differ from the reference program's by a relative error of at most 0.035.
Values may be sent and summed in bfloat16 or wider, within the bound.
A program may use at most 128 MiB of HBM per device.

```python
import math
import jax
import jax.numpy as jnp
from jax import lax

C = 256
HID = 1024
E = 8
B_CAP = 4
FACE_CAP = 2
NB = 2
STEPS = 1000
SCENES = 4
OWNERS = 32
SLOTS = 512
VOX = 512


def layout(key):
    key_occ = jax.random.fold_in(key, 101)
    key_pair = jax.random.fold_in(key, 102)
    key_single = jax.random.fold_in(key, 103)
    random_occ = jax.random.randint(key_occ, (SCENES, OWNERS, B_CAP), 0, 5) < 3
    pick = jax.random.randint(key_single, (SCENES, OWNERS), 0, B_CAP)
    places = jnp.arange(B_CAP, dtype=jnp.int32)
    single = places[None, None, :] == pick[:, :, None]
    occ = random_occ | single
    first = jax.random.randint(key_pair, (SCENES,), 0, OWNERS - 1)
    owner = jnp.arange(OWNERS, dtype=jnp.int32)
    lone = owner[None, :] == (first[:, None] + OWNERS // 2) % OWNERS
    occ = jnp.where(lone[:, :, None], single, occ)
    full = (owner[None, :] == first[:, None]) | (owner[None, :] == first[:, None] + 1)
    occ = occ | full[:, :, None]
    occ_int = occ.astype(jnp.int32)
    slot = jnp.cumsum(occ_int, axis=2) - 1
    return (occ_int, slot)


def draw_brick_counts(key, part):
    occ_int, slot = layout(key)
    return jnp.sum(occ_int, axis=2).reshape(SCENES * OWNERS).astype(jnp.int32)


def draw_send_list(key, part):
    occ_int, slot = layout(key)
    downward = occ_int[:, :, 0:2] * (slot[:, :, 0:2] * 4)
    upward = occ_int[:, :, 2:4] * (slot[:, :, 2:4] * 4 + 1)
    lists = jnp.stack([downward, upward], axis=2)
    return lists.reshape(SCENES * OWNERS, 2, FACE_CAP).astype(jnp.int32)


def draw_recv_list(key, part):
    occ_int, slot = layout(key)
    base = 1 + 4 * B_CAP
    padded = jnp.pad(occ_int, ((0, 0), (1, 1), (0, 0)))
    lower = padded[:, :-2]
    upper = padded[:, 2:]
    zero = jnp.zeros_like(occ_int[:, :, 0])

    def local_code(place, face):
        return occ_int[:, :, place] * (1 + slot[:, :, place] * 4 + face)
    rows = []
    for place in range(4):
        level_x = place // 2
        level_y = place % 2
        if level_x == 0:
            side_lx = lower[:, :, 2 + level_y] * (base + level_y)
            side_ux = local_code(2 + level_y, 0)
        else:
            side_lx = local_code(level_y, 1)
            side_ux = upper[:, :, level_y] * (base + FACE_CAP + level_y)
        if level_y == 0:
            side_ly = zero
            side_uy = local_code(place + 1, 2)
        else:
            side_ly = local_code(place - 1, 3)
            side_uy = zero
        codes = jnp.stack([side_lx, side_ux, side_ly, side_uy], axis=-1)
        rows.append(codes * occ_int[:, :, place][:, :, None])
    by_place = jnp.stack(rows, axis=2)
    onehot = ((slot[:, :, :, None] == jnp.arange(B_CAP, dtype=jnp.int32)) & (occ_int[:, :, :, None] == 1)).astype(jnp.int32)
    by_slot = jnp.sum(onehot[:, :, :, :, None] * by_place[:, :, :, None, :], axis=2)
    return by_slot.reshape(SCENES * OWNERS * B_CAP, 4).astype(jnp.int32)


def touch_ends(result, stream_key, least, top_value):
    shape = result.shape
    index_at = [jax.random.randint(jax.random.fold_in(stream_key, axis), (), 0, shape[axis]) for axis in range(len(shape))]
    result = result.at[tuple(index_at)].set(least)
    longest = shape.index(max(shape))
    index_at[longest] = (index_at[longest] + 1) % shape[longest]
    return result.at[tuple(index_at)].set(top_value)


def block_scale(own_key, dims, shards, least, top_value):
    level, own = 1.0, jax.random.fold_in(own_key, 6)
    for axis_at, parts in shards:
        heights = jnp.exp(jax.random.uniform(jax.random.fold_in(own, axis_at), (parts,), jnp.float32, least / len(shards), top_value / len(shards)))
        level = level * jnp.repeat(heights, dims[axis_at] // parts).reshape([-1 if axis == axis_at else 1 for axis in range(len(dims))])
    return level


def scatter_about(own_key, extent, spread, bound, cuts=(), kind=jnp.bfloat16):
    level = block_scale(own_key, extent, cuts, -0.22, 0.18) if cuts else 1.0
    drawn = jax.random.normal(own_key, extent, jnp.float32) * spread * level
    return jnp.minimum(jnp.maximum(drawn, -bound), bound).astype(kind)


def setup_inputs(seed: int = 0) -> dict:
    splits = jax.random.split(jax.random.key(seed), 11)
    return {
        "latents": scatter_about(splits[0], (SLOTS, VOX, C), 1.0, 6.0, ((0, 128),)),
        "cotangent": scatter_about(splits[1], (SLOTS, VOX, C), 1.0, 6.0, ((0, 128),)),
        "w_up": scatter_about(splits[2], (NB, C, HID), C ** -0.5, 0.375),
        "w_down": scatter_about(splits[3], (NB, HID, C), HID ** -0.5, 0.1875),
        "depth_w": scatter_about(splits[4], (NB, 7, C), 0.4, 2.0, (), jnp.float32),
        "time_table": scatter_about(splits[5], (STEPS, C), 1.0, 6.0, (), jnp.float32),
        "timesteps": touch_ends(jax.random.randint(splits[6], (SCENES,), 0, STEPS), jax.random.fold_in(splits[6], 1), 0, STEPS - 1).astype(jnp.int32),
        "brick_counts": draw_brick_counts(jax.random.fold_in(splits[10], 71), 0),
        "send_list": draw_send_list(jax.random.fold_in(splits[10], 71), 0),
        "recv_list": draw_recv_list(jax.random.fold_in(splits[10], 71), 0),
    }


CUBIC = 0.044715
ROOT = math.sqrt(2.0 / math.pi)
FORWARD_ORDER = (0, 1, 2, 3, 4, 5, 6)
MIRROR_ORDER = (0, 2, 1, 4, 3, 6, 5)

def gelu_tanh(values):
    return 0.5 * values * (1.0 + jnp.tanh(ROOT * (values + CUBIC * values * values * values)))

def gelu_slope(values):
    inner = jnp.tanh(ROOT * (values + CUBIC * values * values * values))
    return 0.5 * (1.0 + inner) + 0.5 * values * (1.0 - inner * inner) * ROOT * (1.0 + 3.0 * CUBIC * values * values)

def planes_of(fields):
    count = fields.shape[0]
    cube = fields.reshape(count, E, E, E, fields.shape[-1])
    stacked = jnp.stack([cube[:, 0], cube[:, E - 1], cube[:, :, 0], cube[:, :, E - 1]], axis=1)
    return stacked.reshape(count * 4, E * E, fields.shape[-1])

def neighbours(field, ghosts):
    count = field.shape[0]
    width = field.shape[-1]
    cube = field.reshape(count, E, E, E, width).astype(jnp.float32)
    sides = ghosts.reshape(count, 4, E, E, width).astype(jnp.float32)
    along_x = jnp.concatenate([sides[:, 0:1], cube, sides[:, 1:2]], axis=1)
    along_y = jnp.concatenate([sides[:, 2][:, :, None], cube, sides[:, 3][:, :, None]], axis=2)
    along_z = jnp.pad(cube, ((0, 0), (0, 0), (0, 0), (1, 1), (0, 0)))
    pieces = [cube, along_x[:, :-2], along_x[:, 2:], along_y[:, :, :-2], along_y[:, :, 2:], along_z[:, :, :, :-2], along_z[:, :, :, 2:]]
    return [piece.reshape(-1, width) for piece in pieces]

def combine(fields, weights, order):
    total = weights[order[0]][None, :] * fields[0]
    for index in range(1, 7):
        total = total + weights[order[index]][None, :] * fields[index]
    return total

def scene_ghosts(field, sends, recvs):
    planes = planes_of(field).reshape(OWNERS, B_CAP * 4, E * E, C)
    outgoing = jax.vmap(lambda plane_set, picks: plane_set[picks.reshape(-1)])(planes, sends)
    outgoing = outgoing.reshape(OWNERS, 2, FACE_CAP, E * E, C)
    empty = jnp.zeros((1, FACE_CAP, E * E, C), jnp.bfloat16)
    from_lower = jnp.concatenate([empty, outgoing[:-1, 1]], axis=0)
    from_upper = jnp.concatenate([outgoing[1:, 0], empty], axis=0)
    blank = jnp.zeros((OWNERS, 1, E * E, C), jnp.bfloat16)
    face_pool = jnp.concatenate([blank, planes, from_lower, from_upper], axis=1)
    ghosts = jax.vmap(lambda rows_all, picks: rows_all[picks.reshape(-1)])(face_pool, recvs.reshape(OWNERS, B_CAP * 4))
    return ghosts.reshape(OWNERS * B_CAP, 4, E * E, C)

def reference(latents, cotangent, w_up, w_down, depth_w, time_table, timesteps, brick_counts, send_list, recv_list):
    per_scene = OWNERS * B_CAP
    grads_in = []
    sum_up = jnp.zeros((NB, C, HID), jnp.float32)
    sum_down = jnp.zeros((NB, HID, C), jnp.float32)
    sum_depth = jnp.zeros((NB, 7, C), jnp.float32)
    for scene in range(SCENES):
        first = scene * per_scene
        counts = jnp.repeat(brick_counts[scene * OWNERS:(scene + 1) * OWNERS], B_CAP)
        occupied = (jnp.arange(per_scene, dtype=jnp.int32) % B_CAP < counts).astype(jnp.float32)[:, None, None]
        sends = send_list[scene * OWNERS:(scene + 1) * OWNERS]
        recvs = recv_list[first:first + per_scene]
        time_shift = time_table[timesteps[scene]]
        field = (latents[first:first + per_scene].astype(jnp.float32) * occupied).astype(jnp.bfloat16)
        saved = []
        for block in range(NB):
            ghosts = scene_ghosts(field, sends, recvs)
            near = neighbours(field, ghosts)
            activation = (combine(near, depth_w[block], FORWARD_ORDER) + time_shift[None, :]).astype(jnp.bfloat16)
            preact = jnp.dot(activation, w_up[block], preferred_element_type=jnp.float32)
            hidden = gelu_tanh(preact).astype(jnp.bfloat16)
            summed = field.reshape(-1, C).astype(jnp.float32) + jnp.dot(hidden, w_down[block], preferred_element_type=jnp.float32)
            saved.append((field, ghosts, activation, preact, hidden))
            field = (summed.reshape(per_scene, VOX, C) * occupied).astype(jnp.bfloat16)
        grad = (cotangent[first:first + per_scene].astype(jnp.float32) * occupied).astype(jnp.bfloat16)
        for block in range(NB - 1, -1, -1):
            field_in, ghosts_in, activation, preact, hidden = saved[block]
            flat_grad = grad.reshape(-1, C)
            sum_down = sum_down.at[block].add(jnp.dot(hidden.T, flat_grad, preferred_element_type=jnp.float32))
            d_hidden = jnp.dot(flat_grad, w_down[block].T, preferred_element_type=jnp.float32)
            d_preact = (d_hidden * gelu_slope(preact)).astype(jnp.bfloat16)
            sum_up = sum_up.at[block].add(jnp.dot(activation.T, d_preact, preferred_element_type=jnp.float32))
            d_act = jnp.dot(d_preact, w_up[block].T, preferred_element_type=jnp.float32).astype(jnp.bfloat16)
            d_field = d_act.reshape(per_scene, VOX, C)
            near_in = neighbours(field_in, ghosts_in)
            d_wide = d_act.astype(jnp.float32)
            sum_depth = sum_depth.at[block].add(jnp.stack([lax.optimization_barrier(jnp.sum(piece * d_wide, axis=0)) for piece in near_in]))
            near_grad = neighbours(d_field, scene_ghosts(d_field, sends, recvs))
            back = combine(near_grad, depth_w[block], MIRROR_ORDER)
            total = flat_grad.astype(jnp.float32) + back
            grad = (total.reshape(per_scene, VOX, C) * occupied).astype(jnp.bfloat16)
        grads_in.append(grad)
    scale = 1.0 / math.sqrt(SLOTS * VOX)
    return (jnp.concatenate(grads_in, axis=0), sum_up * scale, sum_down * scale, sum_depth * scale)
```

```python
import functools
import math

import jax
import jax.numpy as jnp
from jax import lax
from jax.experimental import pallas as pl
from jax.experimental.pallas import tpu as pltpu
from jax.sharding import PartitionSpec as P

MESH = pl.DeviceIdType.MESH
BF = jnp.bfloat16
F32 = jnp.float32
CUBIC = 0.044715
ROOT = math.sqrt(2.0 / math.pi)
NT = (((1,), (1,)), ((), ()))


def gelu_pair(u):
    square = u * u
    gate = 0.5 + 0.5 * jnp.tanh(u * (ROOT + (ROOT * CUBIC) * square))
    hidden = u * gate
    slope = gate + hidden * (1.0 - gate) * (2.0 * ROOT + (6.0 * ROOT * CUBIC) * square)
    return hidden, slope


def dot(a, b):
    return jnp.dot(a, b, preferred_element_type=F32)


def dot_nt(a, b):
    return lax.dot_general(a, b, NT, preferred_element_type=F32)


def kernel(
    scale,
    lat_hbm, cot_hbm, wu_hbm, wd_hbm, dw_ref, tt_hbm, ts_ref, cnt_ref, snd_ref, rcv_ref,
    out_hbm, gup_ref, gdn_ref, dep_ref,
    latv, cotv, wu, wd, tt, field, act, hid, slo, dp, dact, turn_g, turn_a, grad, pool, ghost,
    fsend, flow, fupp, k1, s1, r1, s2, r2, s3, u3, r3, r5, r6, dacc, ds1, dr1, dr2, ds3, dr3, ds2,
    in_sem, out_sem, fs_sem, fr_sem, c1s, c1r, c2s, c2r, c3s, c3r, c5s, c5r, c6s, c6r, e_s, e_r,
):
    me_x = lax.axis_index("rep")
    me_p = lax.axis_index("space")
    core = lax.rem(me_p, 2)
    me_q = me_p // 2
    twin = {"rep": me_x, "space": me_p + 1 - 2 * core}
    below = {"rep": me_x, "space": lax.rem(me_p + 31, 32)}
    above = {"rep": me_x, "space": lax.rem(me_p + 1, 32)}

    def along_x(d):
        return {"rep": lax.rem(me_x + d, 4), "space": me_p}

    def along_q(d):
        return {"rep": me_x, "space": lax.rem(me_q + d, 16) * 2 + core}

    loads = [
        pltpu.make_async_copy(a, b, in_sem.at[i])
        for i, (a, b) in enumerate(
            ((lat_hbm, latv), (wu_hbm, wu), (tt_hbm, tt), (wd_hbm, wd), (cot_hbm, cotv))
        )
    ]
    for copy in loads:
        copy.start()

    barrier = pltpu.get_barrier_semaphore()
    for peer in [twin, below, above] + [along_x(d) for d in (1, 2, 3)]:
        pl.semaphore_signal(barrier, inc=1, device_id=peer, device_id_type=MESH)

    @pl.loop(1, 16)
    def _(d):
        pl.semaphore_signal(barrier, inc=1, device_id=along_q(d), device_id_type=MESH)

    def rows_of(s):
        return pl.ds(pl.multiple_of(s * 512, 512), 512)

    def occupied(s):
        return jnp.minimum(jnp.maximum(cnt_ref[0] - s, 0), 1).astype(F32)

    def remote(src, dst, send, recv, peer):
        return pltpu.make_async_remote_copy(
            src_ref=src, dst_ref=dst, send_sem=send, recv_sem=recv, device_id=peer, device_id_type=MESH
        )

    def pool_faces(src):
        @pl.loop(0, 4)
        def _(s):
            for x in range(8):
                plane = src[pl.ds(pl.multiple_of(s * 512 + x * 64, 64), 64), :].astype(F32)
                if x == 0:
                    pool[1 + 4 * s] = plane
                if x == 7:
                    pool[2 + 4 * s] = plane
                pool[3 + 4 * s, x * 8:x * 8 + 8] = plane[:8]
                pool[4 + 4 * s, x * 8:x * 8 + 8] = plane[56:]

    def face_copies(turn):
        return (
            remote(fsend.at[turn, 1], flow.at[turn], fs_sem.at[turn, 1], fr_sem.at[turn, 1], above),
            remote(fsend.at[turn, 0], fupp.at[turn], fs_sem.at[turn, 0], fr_sem.at[turn, 0], below),
        )

    def send_faces(turn):
        for k in range(2):
            for e in range(2):
                fsend[turn, k, e] = pool[1 + snd_ref[0, k, e]].astype(BF)
        for copy in face_copies(turn):
            copy.start()

    def take_faces(turn):
        for copy in face_copies(turn):
            copy.wait()
        lower = jnp.where(me_p > 0, 1.0, 0.0).astype(F32)
        upper = jnp.where(me_p < 31, 1.0, 0.0).astype(F32)
        for e in range(2):
            pool[17 + e] = flow[turn, e].astype(F32) * lower
            pool[19 + e] = fupp[turn, e].astype(F32) * upper

        @pl.loop(0, 4)
        def _(s):
            for side in range(4):
                ghost[s, side] = pool[rcv_ref[s, side]]

    zed = lax.broadcasted_iota(jnp.int32, (8, 128), 0)

    def taps(src, s, cols):
        def plane(x):
            rows = pl.ds(pl.multiple_of(s * 512 + x * 64, 64), 64)
            return src[rows, cols].astype(F32).reshape(8, 8, 128)

        before = ghost[s, 0, :, cols].reshape(8, 8, 128)
        here = plane(0)
        for x in range(8):
            after = plane(x + 1) if x < 7 else ghost[s, 1, :, cols].reshape(8, 8, 128)
            y_low = jnp.concatenate([ghost[s, 2, x * 8:x * 8 + 8, cols][None], here[:7]], axis=0)
            y_upp = jnp.concatenate([here[1:], ghost[s, 3, x * 8:x * 8 + 8, cols][None]], axis=0)
            z_low = pltpu.roll(here, 1, 1)
            z_upp = pltpu.roll(here, 7, 1)
            yield x, (here, before, after, y_low, y_upp, z_low, z_upp)
            before, here = here, after

    def tap_weights(b, cols, order):
        w = [jnp.broadcast_to(dw_ref[b, i:i + 1, cols], (8, 128)) for i in range(7)]
        if order:
            w[5] = jnp.where(zed == 0, 0.0, w[5])
            w[6] = jnp.where(zed == 7, 0.0, w[6])
        else:
            w[5] = jnp.where(zed == 7, 0.0, w[5])
            w[6] = jnp.where(zed == 0, 0.0, w[6])
        return w

    def conv_forward(b):
        for lane in range(2):
            cols = slice(lane * 128, lane * 128 + 128)
            w = tap_weights(b, cols, True)
            shift = jnp.broadcast_to(moment[:, cols], (8, 128))

            @pl.loop(0, 4)
            def _(s):
                for x, near in taps(field.at[b], s, cols):
                    total = shift[None]
                    for i in range(7):
                        total = total + w[i][None] * near[i]
                    rows = pl.ds(pl.multiple_of(s * 512 + x * 64, 64), 64)
                    act[b, rows, cols] = total.reshape(64, 128).astype(BF)

    mirror = (0, 2, 1, 4, 3, 6, 5)

    def conv_backward(b):
        for lane in range(2):
            cols = slice(lane * 128, lane * 128 + 128)
            w = tap_weights(b, cols, False)

            def slot(s, sums):
                occ = occupied(s)
                sums = list(sums)
                for x, near in taps(dact, s, cols):
                    rows = pl.ds(pl.multiple_of(s * 512 + x * 64, 64), 64)
                    total = grad[rows, cols].astype(F32).reshape(8, 8, 128)
                    value = field[b, rows, cols].astype(F32).reshape(8, 8, 128)
                    for i in range(7):
                        total = total + w[i][None] * near[mirror[i]]
                        sums[i] = sums[i] + jnp.sum(value * near[mirror[i]], axis=0)
                    grad[rows, cols] = (total * occ).reshape(64, 128).astype(BF)
                return tuple(sums)

            sums = list(lax.fori_loop(0, 4, slot, tuple(jnp.zeros((8, 128), F32) for _ in range(7))))
            sums[5] = jnp.where(zed == 7, 0.0, sums[5])
            sums[6] = jnp.where(zed == 0, 0.0, sums[6])
            for i in range(7):
                dacc[7 * b + i:7 * b + i + 1, cols] = jnp.sum(sums[i], axis=0, keepdims=True)

    def c1(b, kind):
        return remote(s1.at[b, kind], r1.at[b, kind], c1s.at[b, kind], c1r.at[b, kind], twin)

    def weight_grad(b, kind, left, right):
        @pl.loop(0, 4)
        def _(j):
            tile = dot(left[...], right[:, pl.ds(pl.multiple_of(j * 256, 256), 256)])
            k1[b, kind, j] = tile.reshape(2, 128, 256)
            s1[b, kind, j] = k1[b, kind, j, 1 - core].astype(BF)

        c1(b, kind).start()

    def c2(b, kind, d):
        to = lax.rem(me_x + d, 4)
        return remote(s2.at[b, kind, to], r2.at[b, kind, d - 1], c2s.at[b, kind, d - 1], c2r.at[b, kind, d - 1], along_x(d))

    def step2(b, kind):
        c1(b, kind).wait()
        for d in (2, 1, 3):
            to = lax.rem(me_x + d, 4)
            s2[b, kind, to] = (k1[b, kind, to, core] + r1[b, kind, to].astype(F32)).astype(BF)
            c2(b, kind, d).start()

    def c3(b, d):
        to = lax.rem(me_q + d, 16)
        return remote(s3.at[b, to], r3.at[b, d - 1], c3s.at[b], c3r.at[b], along_q(d))

    def step3(b):
        for kind in range(2):
            for d in (1, 2, 3):
                c2(b, kind, d).wait()
            total = k1[b, kind, me_x, core] + r1[b, kind, me_x].astype(F32)
            for d in range(3):
                total = total + r2[b, kind, d].astype(F32)
            u3[b, kind * 8:kind * 8 + 8] = total.reshape(8, 16, 256)
            s3[b, kind * 8:kind * 8 + 8] = total.reshape(8, 16, 256).astype(BF)

        @pl.loop(1, 16)
        def _(d):
            c3(b, d).start()

    def wait_all(ref, send, recv):
        pltpu.make_async_copy(ref, ref, send).wait()
        pltpu.make_async_copy(ref, ref, recv).wait()

    def c5(b, d):
        return remote(r5.at[b, me_q], r5.at[b, me_q], c5s.at[b], c5r.at[b], along_q(d))

    def step5(b):
        wait_all(r3.at[b], c3s.at[b], c3r.at[b])
        total = u3[b, me_q]
        for d in range(15):
            total = total + r3[b, d].astype(F32)
        r5[b, me_q] = total.astype(BF)

        @pl.loop(1, 16)
        def _(d):
            c5(b, d).start()

    def c6(b):
        return remote(r5.at[b], r6.at[b], c6s.at[b], c6r.at[b], twin)

    def step6(b):
        wait_all(r3.at[b], c5s.at[b], c5r.at[b])
        c6(b).start()

    def finish(b):
        c6(b).wait()
        for side, ref in ((core, r5), (1 - core, r6)):
            at = pl.ds(pl.multiple_of(side * 128, 128), 128)
            gup_ref[b, at, :] = ref[b, 8:].reshape(128, 256).astype(F32) * scale
            gdn_ref[b, :, at] = (ref[b, :8].reshape(128, 256).astype(F32) * scale).T

    def e1():
        return remote(ds1, dr1, e_s.at[0], e_r.at[0], twin)

    def e2(d):
        return remote(ds2, dr2.at[d - 1], e_s.at[d], e_r.at[d], along_x(d))

    def e3(d):
        return remote(ds3, dr3.at[d - 1], e_s.at[4], e_r.at[4], along_q(d))

    loads[0].wait()

    @pl.loop(0, 4)
    def _(s):
        field[0, rows_of(s), :] = (latv[rows_of(s), :].astype(F32) * occupied(s)).astype(BF)

    pool[0] = jnp.zeros((64, 256), F32)
    pool_faces(field.at[0])
    pl.semaphore_wait(barrier, 21)
    send_faces(0)
    loads[2].wait()
    table_row = lax.broadcasted_iota(jnp.int32, (1000, 256), 0)
    moment = jnp.sum(jnp.where(table_row == ts_ref[0], tt[...], 0.0), axis=0, keepdims=True)
    take_faces(0)
    conv_forward(0)
    loads[1].wait()
    loads[3].wait()

    @pl.loop(0, 4)
    def _(s):
        rows = rows_of(s)
        value = act[0, rows, :]
        total = field[0, rows, :].astype(F32)
        for n in range(4):
            part = slice(n * 256, n * 256 + 256)
            hidden, slope = gelu_pair(dot(value, wu[0, :, part]))
            hidden = hidden.astype(BF)
            hid[0, rows, part] = hidden
            slo[rows, part] = slope.astype(BF)
            total = total + dot(hidden, wd[0, part, :])
        field[1, rows, :] = (total * occupied(s)).astype(BF)

    pool_faces(field.at[1])
    send_faces(1)
    loads[4].wait()

    @pl.loop(0, 4)
    def _(s):
        rows = rows_of(s)
        value = (cotv[rows, :].astype(F32) * occupied(s)).astype(BF)
        grad[rows, :] = value
        turn_g[:, rows] = value.T

    take_faces(1)
    conv_forward(1)

    @pl.loop(0, 4)
    def _(s):
        rows = rows_of(s)
        value = act[1, rows, :]
        turn_a[:, rows] = value.T
        down = grad[rows, :]
        total = jnp.zeros((512, 256), F32)
        for n in range(4):
            part = slice(n * 256, n * 256 + 256)
            hidden, slope = gelu_pair(dot(value, wu[1, :, part]))
            hid[1, rows, part] = hidden.astype(BF)
            back = (dot_nt(down, wd[1, part, :]) * slope).astype(BF)
            dp[rows, part] = back
            total = total + dot_nt(back, wu[1, :, part])
        dact[rows, :] = total.astype(BF)

    pool_faces(dact)
    send_faces(2)
    weight_grad(1, 0, turn_g, hid.at[1])
    weight_grad(1, 1, turn_a, dp)
    take_faces(2)
    step2(1, 0)
    step2(1, 1)
    conv_backward(1)

    @pl.loop(0, 4)
    def _(s):
        rows = rows_of(s)
        turn_g[:, rows] = grad[rows, :].T
        turn_a[:, rows] = act[0, rows, :].T

    weight_grad(0, 0, turn_g, hid.at[0])
    step3(1)

    @pl.loop(0, 4)
    def _(s):
        rows = rows_of(s)
        down = grad[rows, :]
        total = jnp.zeros((512, 256), F32)
        for n in range(4):
            part = slice(n * 256, n * 256 + 256)
            back = (dot_nt(down, wd[0, part, :]) * slo[rows, part].astype(F32)).astype(BF)
            dp[rows, part] = back
            total = total + dot_nt(back, wu[0, :, part])
        dact[rows, :] = total.astype(BF)

    pool_faces(dact)
    send_faces(3)
    step2(0, 0)
    weight_grad(0, 1, turn_a, dp)
    step5(1)
    take_faces(3)
    step2(0, 1)
    dacc[14:16] = jnp.zeros((2, 256), F32)
    conv_backward(0)
    out = pltpu.make_async_copy(grad, out_hbm, out_sem)
    out.start()
    ds1[...] = dacc[...].astype(BF)
    e1().start()
    step6(1)
    e1().wait()
    dsum = dacc[...] + dr1[...].astype(F32)
    ds2[...] = dsum.astype(BF)
    for d in (1, 2, 3):
        e2(d).start()
    step3(0)
    for d in (1, 2, 3):
        e2(d).wait()
    for d in range(3):
        dsum = dsum + dr2[d].astype(F32)
    ds3[...] = dsum.astype(BF)

    @pl.loop(1, 16)
    def _(d):
        e3(d).start()

    finish(1)
    step5(0)
    wait_all(dr3, e_s.at[4], e_r.at[4])
    for d in range(15):
        dsum = dsum + dr3[d].astype(F32)
    dsum = dsum * scale
    share = jnp.zeros((16, 64), F32)
    for j in range(4):
        share = jnp.where(me_x == j, dsum[:, j * 64:j * 64 + 64], share)
    dep_ref[0] = share[0:7]
    dep_ref[1] = share[7:14]
    step6(0)
    finish(0)
    out.wait()


def on_device(latents, cotangent, w_up, w_down, depth_w, time_table, timesteps, brick_counts, send_list, recv_list):
    bricks, voxels, channels = latents.shape
    rows = bricks * voxels
    scale = 1.0 / math.sqrt(rows * lax.axis_size("rep") * lax.axis_size("space"))
    anywhere = pl.BlockSpec(memory_space=pl.ANY)
    vmem = pl.BlockSpec(memory_space=pltpu.VMEM)
    smem = pl.BlockSpec(memory_space=pltpu.SMEM)
    dma = pltpu.SemaphoreType.DMA
    out, up, down, depth = pl.pallas_call(
        functools.partial(kernel, scale),
        out_shape=(
            jax.ShapeDtypeStruct((rows, channels), BF),
            jax.ShapeDtypeStruct((2, 256, 256), F32),
            jax.ShapeDtypeStruct((2, 256, 256), F32),
            jax.ShapeDtypeStruct((2, 7, 64), F32),
        ),
        in_specs=[anywhere] * 4 + [vmem, anywhere] + [smem] * 4,
        out_specs=(anywhere, vmem, vmem, vmem),
        scratch_shapes=[
            pltpu.VMEM((rows, 256), BF),
            pltpu.VMEM((rows, 256), BF),
            pltpu.VMEM((2, 256, 1024), BF),
            pltpu.VMEM((2, 1024, 256), BF),
            pltpu.VMEM((1000, 256), F32),
            pltpu.VMEM((2, rows, 256), BF),
            pltpu.VMEM((2, rows, 256), BF),
            pltpu.VMEM((2, rows, 1024), BF),
            pltpu.VMEM((rows, 1024), BF),
            pltpu.VMEM((rows, 1024), BF),
            pltpu.VMEM((rows, 256), BF),
            pltpu.VMEM((256, rows), BF),
            pltpu.VMEM((256, rows), BF),
            pltpu.VMEM((rows, 256), BF),
            pltpu.VMEM((21, 64, 256), F32),
            pltpu.VMEM((4, 4, 64, 256), F32),
            pltpu.VMEM((4, 2, 2, 64, 256), BF),
            pltpu.VMEM((4, 2, 64, 256), BF),
            pltpu.VMEM((4, 2, 64, 256), BF),
            pltpu.VMEM((2, 2, 4, 2, 128, 256), F32),
            pltpu.VMEM((2, 2, 4, 128, 256), BF),
            pltpu.VMEM((2, 2, 4, 128, 256), BF),
            pltpu.VMEM((2, 2, 4, 128, 256), BF),
            pltpu.VMEM((2, 2, 3, 128, 256), BF),
            pltpu.VMEM((2, 16, 16, 256), BF),
            pltpu.VMEM((2, 16, 16, 256), F32),
            pltpu.VMEM((2, 15, 16, 256), BF),
            pltpu.VMEM((2, 16, 16, 256), BF),
            pltpu.VMEM((2, 16, 16, 256), BF),
            pltpu.VMEM((16, 256), F32),
            pltpu.VMEM((16, 256), BF),
            pltpu.VMEM((16, 256), BF),
            pltpu.VMEM((3, 16, 256), BF),
            pltpu.VMEM((16, 256), BF),
            pltpu.VMEM((15, 16, 256), BF),
            pltpu.VMEM((16, 256), BF),
            dma((5,)),
            dma,
            dma((4, 2)),
            dma((4, 2)),
            dma((2, 2)),
            dma((2, 2)),
            dma((2, 2, 3)),
            dma((2, 2, 3)),
            dma((2,)),
            dma((2,)),
            dma((2,)),
            dma((2,)),
            dma((2,)),
            dma((2,)),
            dma((5,)),
            dma((5,)),
        ],
        compiler_params=pltpu.CompilerParams(
            collective_id=0, has_side_effects=True, vmem_limit_bytes=58 * 1024 * 1024
        ),
        name="blocks",
    )(
        latents.reshape(rows, channels),
        cotangent.reshape(rows, channels),
        w_up, w_down, depth_w, time_table, timesteps, brick_counts, send_list, recv_list,
    )
    return out.reshape(latents.shape), up, down, depth


def solution(mesh):
    spread = ("rep", "space")
    return jax.shard_map(
        on_device,
        mesh=mesh,
        in_specs=(
            P(spread, None, None),
            P(spread, None, None),
            P(), P(), P(), P(),
            P("rep"),
            P(spread),
            P(spread, None, None),
            P(spread, None),
        ),
        out_specs=(
            P(spread, None, None),
            P(None, None, "rep"),
            P(None, "rep", None),
            P(None, None, "rep"),
        ),
        check_vma=False,
    )
```

```python
import functools
import math

import jax
import jax.numpy as jnp
from jax import lax
from jax.experimental import pallas as pl
from jax.experimental.pallas import tpu as pltpu
from jax.sharding import PartitionSpec as P

MESH = pl.DeviceIdType.MESH
BF = jnp.bfloat16
F32 = jnp.float32
CUBIC = 0.044715
ROOT = math.sqrt(2.0 / math.pi)
LOG2E = math.log2(math.e)


def gelu_pair(u):
    square = u * u
    power = u * ((-2.0 * ROOT * LOG2E) + (-2.0 * ROOT * CUBIC * LOG2E) * square)
    e = jnp.exp2(jnp.minimum(power, 80.0))
    gate = 1.0 / (1.0 + e)
    hidden = u * gate
    slope = gate + hidden * (e * gate) * ((2.0 * ROOT) + (6.0 * ROOT * CUBIC) * square)
    return hidden, slope


def dot(a, b):
    return jnp.dot(a, b, preferred_element_type=F32)


def kernel(
    scale,
    lat_hbm, cot_hbm, wu_hbm, wd_hbm, dw_ref, tt_hbm, ts_ref, cnt_ref, snd_ref, rcv_ref,
    out_hbm, gup_ref, gdn_ref, dep_ref,
    latv, cotv, wu, wd, tt, field, act, hid, slo, dp, dact, turn_g, turn_a, grad, pool, ghost, base, wut, wdt,
    fsend, flow, fupp, k1, s1, r1, s2, r2, s3, u3, r3, r5, r6, dacc, ds1, dr1, dr2, ds3, dr3, ds2,
    in_sem, out_sem, fs_sem, fr_sem, c1s, c1r, c2s, c2r, c3s, c3r, c5s, c5r, c6s, c6r, e_s, e_r,
):
    me_x = lax.axis_index("rep")
    me_p = lax.axis_index("space")
    core = lax.rem(me_p, 2)
    me_q = me_p // 2
    twin = {"rep": me_x, "space": me_p + 1 - 2 * core}
    below = {"rep": me_x, "space": lax.rem(me_p + 31, 32)}
    above = {"rep": me_x, "space": lax.rem(me_p + 1, 32)}

    def along_x(d):
        return {"rep": lax.rem(me_x + d, 4), "space": me_p}

    def along_q(d):
        return {"rep": me_x, "space": lax.rem(me_q + d, 16) * 2 + core}

    loads = [
        pltpu.make_async_copy(a, b, in_sem.at[i])
        for i, (a, b) in enumerate(
            ((lat_hbm, latv), (wu_hbm, wu), (tt_hbm, tt), (wd_hbm, wd), (cot_hbm, cotv))
        )
    ]
    for copy in loads:
        copy.start()

    barrier = pltpu.get_barrier_semaphore()
    for peer in [twin, below, above] + [along_x(d) for d in (1, 2, 3)]:
        pl.semaphore_signal(barrier, inc=1, device_id=peer, device_id_type=MESH)

    @pl.loop(1, 16)
    def _(d):
        pl.semaphore_signal(barrier, inc=1, device_id=along_q(d), device_id_type=MESH)

    def rows_of(s):
        return pl.ds(pl.multiple_of(s * 512, 512), 512)

    def occupied(s):
        return jnp.minimum(jnp.maximum(cnt_ref[0] - s, 0), 1).astype(F32)

    def remote(src, dst, send, recv, peer):
        return pltpu.make_async_remote_copy(
            src_ref=src, dst_ref=dst, send_sem=send, recv_sem=recv, device_id=peer, device_id_type=MESH
        )

    def pool_faces(src):
        @pl.loop(0, 4)
        def _(s):
            for x in range(8):
                plane = src[pl.ds(pl.multiple_of(s * 512 + x * 64, 64), 64), :].astype(F32)
                if x == 0:
                    pool[1 + 4 * s] = plane
                if x == 7:
                    pool[2 + 4 * s] = plane
                pool[3 + 4 * s, x * 8:x * 8 + 8] = plane[:8]
                pool[4 + 4 * s, x * 8:x * 8 + 8] = plane[56:]

    def face_copies(turn):
        return (
            remote(fsend.at[turn, 1], flow.at[turn], fs_sem.at[turn, 1], fr_sem.at[turn, 1], above),
            remote(fsend.at[turn, 0], fupp.at[turn], fs_sem.at[turn, 0], fr_sem.at[turn, 0], below),
        )

    def send_faces(turn):
        for k in range(2):
            for e in range(2):
                fsend[turn, k, e] = pool[1 + snd_ref[0, k, e]].astype(BF)
        for copy in face_copies(turn):
            copy.start()

    def take_faces(turn, kept):
        for copy in face_copies(turn):
            copy.wait()
        lower = jnp.where(me_p > 0, 1.0, 0.0).astype(F32)
        upper = jnp.where(me_p < 31, 1.0, 0.0).astype(F32)
        for e in range(2):
            pool[17 + e] = flow[turn, e].astype(F32) * lower
            pool[19 + e] = fupp[turn, e].astype(F32) * upper

        @pl.loop(0, 4)
        def _(s):
            for side in range(4):
                ghost[kept, s, side] = pool[rcv_ref[s, side]]

    zed = lax.broadcasted_iota(jnp.int32, (8, 128), 0)

    def taps(src, s, cols):
        def plane(x):
            rows = pl.ds(pl.multiple_of(s * 512 + x * 64, 64), 64)
            return src[rows, cols].astype(F32).reshape(8, 8, 128)

        blank = jnp.zeros((1, 8, 128), F32)
        before = None
        here = plane(0)
        for x in range(8):
            after = plane(x + 1) if x < 7 else None
            y_low = jnp.concatenate([blank, here[:7]], axis=0)
            y_upp = jnp.concatenate([here[1:], blank], axis=0)
            yield x, (here, before, after, y_low, y_upp, pltpu.roll(here, 1, 1), pltpu.roll(here, 7, 1))
            before, here = here, after

    def tap_weights(b, cols, low, upp):
        w = [jnp.broadcast_to(dw_ref[i, b:b + 1, cols], (8, 128)) for i in range(7)]
        w[5] = jnp.where(zed == low, 0.0, w[5])
        w[6] = jnp.where(zed == upp, 0.0, w[6])
        return w

    def base_forward(b):
        for lane in range(2):
            cols = slice(lane * 128, lane * 128 + 128)
            w = tap_weights(b, cols, 0, 7)
            shift = jnp.broadcast_to(moment[:, cols], (8, 128))

            @pl.loop(0, 4)
            def _(s):
                for x, near in taps(field.at[b], s, cols):
                    total = shift[None]
                    for i in range(7):
                        if near[i] is not None:
                            total = total + w[i][None] * near[i]
                    rows = pl.ds(pl.multiple_of(s * 512 + x * 64, 64), 64)
                    base[rows, cols] = total.reshape(64, 128)

    def with_ghosts(kept, s, x, w):
        total = base[pl.ds(pl.multiple_of(s * 512 + x * 64, 64), 64), :]
        if x == 0:
            total = total + w[0] * ghost[kept, s, 0]
        if x == 7:
            total = total + w[1] * ghost[kept, s, 1]
        edge = slice(x * 8, x * 8 + 8)
        low = total[:8] + w[2] * ghost[kept, s, 2, edge]
        upp = total[56:] + w[3] * ghost[kept, s, 3, edge]
        return jnp.concatenate([low, total[8:56], upp], axis=0)

    def finish_forward(b):
        w = [dw_ref[i, b:b + 1, :] for i in (1, 2, 3, 4)]

        @pl.loop(0, 4)
        def _(s):
            for x in range(8):
                rows = pl.ds(pl.multiple_of(s * 512 + x * 64, 64), 64)
                act[b, rows, :] = with_ghosts(b, s, x, w).astype(BF)

    mirror = (0, 2, 1, 4, 3, 6, 5)

    def base_backward(b):
        for lane in range(2):
            cols = slice(lane * 128, lane * 128 + 128)
            w = tap_weights(b, cols, 7, 0)

            def slot(s, sums):
                sums = list(sums)
                for x, near in taps(dact, s, cols):
                    rows = pl.ds(pl.multiple_of(s * 512 + x * 64, 64), 64)
                    total = grad[rows, cols].astype(F32).reshape(8, 8, 128)
                    value = field[b, rows, cols].astype(F32).reshape(8, 8, 128)
                    here = near[0]
                    for i in range(7):
                        if near[mirror[i]] is not None:
                            total = total + w[i][None] * near[mirror[i]]
                            sums[i] = sums[i] + jnp.sum(value * near[mirror[i]], axis=0)
                    if x == 0:
                        sums[1] = sums[1] + jnp.sum(ghost[b, s, 0, :, cols].reshape(8, 8, 128) * here, axis=0)
                    if x == 7:
                        sums[2] = sums[2] + jnp.sum(ghost[b, s, 1, :, cols].reshape(8, 8, 128) * here, axis=0)
                    sums[3] = sums[3] + ghost[b, s, 2, x * 8:x * 8 + 8, cols] * here[0]
                    sums[4] = sums[4] + ghost[b, s, 3, x * 8:x * 8 + 8, cols] * here[7]
                    base[rows, cols] = total.reshape(64, 128)
                return tuple(sums)

            sums = list(lax.fori_loop(0, 4, slot, tuple(jnp.zeros((8, 128), F32) for _ in range(7))))
            sums[5] = jnp.where(zed == 7, 0.0, sums[5])
            sums[6] = jnp.where(zed == 0, 0.0, sums[6])
            for i in range(7):
                dacc[7 * b + i:7 * b + i + 1, cols] = jnp.sum(sums[i], axis=0, keepdims=True)

    def finish_backward(b):
        w = [dw_ref[i, b:b + 1, :] for i in (2, 1, 4, 3)]

        @pl.loop(0, 4)
        def _(s):
            occ = occupied(s)
            for x in range(8):
                rows = pl.ds(pl.multiple_of(s * 512 + x * 64, 64), 64)
                grad[rows, :] = (with_ghosts(2, s, x, w) * occ).astype(BF)

    def c1(b, kind):
        return remote(s1.at[b, kind], r1.at[b, kind], c1s.at[b, kind], c1r.at[b, kind], twin)

    def weight_grad(b, kind, left, right):
        tile = dot(left[...], right[...])
        for j in range(4):
            k1[b, kind, j] = tile[:, j * 256:j * 256 + 256].reshape(2, 128, 256)
            s1[b, kind, j] = k1[b, kind, j, 1 - core].astype(BF)
        c1(b, kind).start()

    def c2(b, kind, d):
        to = lax.rem(me_x + d, 4)
        return remote(s2.at[b, kind, to], r2.at[b, kind, d - 1], c2s.at[b, kind, d - 1], c2r.at[b, kind, d - 1], along_x(d))

    def step2(b, kind):
        c1(b, kind).wait()
        for d in (2, 1, 3):
            to = lax.rem(me_x + d, 4)
            s2[b, kind, to] = (k1[b, kind, to, core] + r1[b, kind, to].astype(F32)).astype(BF)
            c2(b, kind, d).start()

    def c3(b, d):
        to = lax.rem(me_q + d, 16)
        return remote(s3.at[b, to], r3.at[b, d - 1], c3s.at[b], c3r.at[b], along_q(d))

    def step3(b):
        for kind in range(2):
            for d in (1, 2, 3):
                c2(b, kind, d).wait()
            total = k1[b, kind, me_x, core] + r1[b, kind, me_x].astype(F32)
            for d in range(3):
                total = total + r2[b, kind, d].astype(F32)
            u3[b, kind * 8:kind * 8 + 8] = total.reshape(8, 16, 256)
            s3[b, kind * 8:kind * 8 + 8] = total.reshape(8, 16, 256).astype(BF)

        @pl.loop(1, 16)
        def _(d):
            c3(b, d).start()

    def wait_all(ref, send, recv):
        pltpu.make_async_copy(ref, ref, send).wait()
        pltpu.make_async_copy(ref, ref, recv).wait()

    def c5(b, d):
        return remote(r5.at[b, me_q], r5.at[b, me_q], c5s.at[b], c5r.at[b], along_q(d))

    def step5(b):
        wait_all(r3.at[b], c3s.at[b], c3r.at[b])
        total = u3[b, me_q]
        for d in range(15):
            total = total + r3[b, d].astype(F32)
        r5[b, me_q] = total.astype(BF)

        @pl.loop(1, 16)
        def _(d):
            c5(b, d).start()

    def c6(b):
        return remote(r5.at[b], r6.at[b], c6s.at[b], c6r.at[b], twin)

    def step6(b):
        wait_all(r3.at[b], c5s.at[b], c5r.at[b])
        c6(b).start()

    def finish(b):
        c6(b).wait()
        for side, ref in ((core, r5), (1 - core, r6)):
            at = pl.ds(pl.multiple_of(side * 128, 128), 128)
            gup_ref[b, at, :] = ref[b, 8:].reshape(128, 256).astype(F32) * scale
            gdn_ref[b, :, at] = (ref[b, :8].reshape(128, 256).astype(F32) * scale).T

    def e1():
        return remote(ds1, dr1, e_s.at[0], e_r.at[0], twin)

    def e2(d):
        return remote(ds2, dr2.at[d - 1], e_s.at[d], e_r.at[d], along_x(d))

    def e3(d):
        return remote(ds3, dr3.at[d - 1], e_s.at[4], e_r.at[4], along_q(d))

    def turn(dst, src):
        @pl.loop(0, 4)
        def _(s):
            dst[:, rows_of(s)] = src[rows_of(s), :].T

    loads[0].wait()

    @pl.loop(0, 4)
    def _(s):
        field[0, rows_of(s), :] = (latv[rows_of(s), :].astype(F32) * occupied(s)).astype(BF)

    pool[0] = jnp.zeros((64, 256), F32)
    pool_faces(field.at[0])
    pl.semaphore_wait(barrier, 21)
    send_faces(0)
    loads[2].wait()
    table_row = lax.broadcasted_iota(jnp.int32, (1000, 256), 0)
    moment = jnp.sum(jnp.where(table_row == ts_ref[0], tt[...], 0.0), axis=0, keepdims=True)
    base_forward(0)
    loads[1].wait()
    loads[3].wait()
    for b in range(2):
        wut[b] = wu[b].T
        wdt[b] = wd[b].T
    loads[4].wait()

    @pl.loop(0, 4)
    def _(s):
        rows = rows_of(s)
        value = (cotv[rows, :].astype(F32) * occupied(s)).astype(BF)
        grad[rows, :] = value
        turn_g[:, rows] = value.T

    take_faces(0, 0)
    finish_forward(0)
    for n in range(4):
        part = slice(n * 256, n * 256 + 256)
        hid[0, :, part], slo[:, part] = gelu_pair(dot(act[0], wu[0, :, part]).astype(BF))
    for s in range(4):
        rows = slice(s * 512, s * 512 + 512)
        total = field[0, rows, :].astype(F32) + dot(hid[0, rows, :], wd[0])
        field[1, rows, :] = (total * occupied(s)).astype(BF)
    pool_faces(field.at[1])
    send_faces(1)
    base_forward(1)
    for n in range(4):
        part = slice(n * 256, n * 256 + 256)
        dp[:, part] = dot(grad[...], wdt[1, :, part]).astype(BF)
    turn(turn_a.at[0], act.at[0])
    take_faces(1, 1)
    finish_forward(1)

    for n in range(4):
        part = slice(n * 256, n * 256 + 256)
        hidden, slope = gelu_pair(dot(act[1], wu[1, :, part]).astype(BF))
        hid[1, :, part] = hidden
        dp[:, part] = dp[:, part] * slope
    dact[...] = dot(dp[...], wut[1]).astype(BF)
    pool_faces(dact)
    send_faces(2)
    weight_grad(1, 0, turn_g, hid.at[1])
    turn(turn_a.at[1], act.at[1])
    weight_grad(1, 1, turn_a.at[1], dp)
    base_backward(1)
    step2(1, 0)
    step2(1, 1)
    take_faces(2, 2)
    finish_backward(1)

    turn(turn_g, grad)
    weight_grad(0, 0, turn_g, hid.at[0])
    for n in range(4):
        part = slice(n * 256, n * 256 + 256)
        dp[:, part] = dot(grad[...], wdt[0, :, part]).astype(BF) * slo[:, part]
    step2(0, 0)
    weight_grad(0, 1, turn_a.at[0], dp)
    dact[...] = dot(dp[...], wut[0]).astype(BF)
    pool_faces(dact)
    send_faces(3)
    step2(0, 1)
    step3(1)
    dacc[14:16] = jnp.zeros((2, 256), F32)
    base_backward(0)
    ds1[...] = dacc[...].astype(BF)
    e1().start()
    take_faces(3, 2)
    finish_backward(0)
    out = pltpu.make_async_copy(grad, out_hbm, out_sem)
    out.start()
    e1().wait()
    dsum = dacc[...] + dr1[...].astype(F32)
    ds2[...] = dsum.astype(BF)
    for d in (1, 2, 3):
        e2(d).start()
    step3(0)
    step5(1)
    for d in (1, 2, 3):
        e2(d).wait()
    for d in range(3):
        dsum = dsum + dr2[d].astype(F32)
    ds3[...] = dsum.astype(BF)

    @pl.loop(1, 16)
    def _(d):
        e3(d).start()

    step5(0)
    step6(1)
    wait_all(dr3, e_s.at[4], e_r.at[4])
    for d in range(15):
        dsum = dsum + dr3[d].astype(F32)
    dsum = dsum * scale
    share = jnp.zeros((16, 64), F32)
    for j in range(4):
        share = jnp.where(me_x == j, dsum[:, j * 64:j * 64 + 64], share)
    for i in range(7):
        dep_ref[i, 0:1] = share[i:i + 1]
        dep_ref[i, 1:2] = share[7 + i:8 + i]
    finish(1)
    step6(0)
    finish(0)
    out.wait()


def on_device(latents, cotangent, w_up, w_down, depth_w, time_table, timesteps, brick_counts, send_list, recv_list):
    bricks, voxels, channels = latents.shape
    rows = bricks * voxels
    scale = 1.0 / math.sqrt(rows * lax.axis_size("rep") * lax.axis_size("space"))
    anywhere = pl.BlockSpec(memory_space=pl.ANY)
    vmem = pl.BlockSpec(memory_space=pltpu.VMEM)
    smem = pl.BlockSpec(memory_space=pltpu.SMEM)
    dma = pltpu.SemaphoreType.DMA
    out, up, down, depth = pl.pallas_call(
        functools.partial(kernel, scale),
        out_shape=(
            jax.ShapeDtypeStruct((rows, channels), BF),
            jax.ShapeDtypeStruct((2, 256, 256), F32),
            jax.ShapeDtypeStruct((2, 256, 256), F32),
            jax.ShapeDtypeStruct((7, 2, 64), F32),
        ),
        in_specs=[anywhere] * 4 + [vmem, anywhere] + [smem] * 4,
        out_specs=(anywhere, vmem, vmem, vmem),
        scratch_shapes=[
            pltpu.VMEM((rows, 256), BF),
            pltpu.VMEM((rows, 256), BF),
            pltpu.VMEM((2, 256, 1024), BF),
            pltpu.VMEM((2, 1024, 256), BF),
            pltpu.VMEM((1000, 256), F32),
            pltpu.VMEM((2, rows, 256), BF),
            pltpu.VMEM((2, rows, 256), BF),
            pltpu.VMEM((2, rows, 1024), BF),
            pltpu.VMEM((rows, 1024), BF),
            pltpu.VMEM((rows, 1024), BF),
            pltpu.VMEM((rows, 256), BF),
            pltpu.VMEM((256, rows), BF),
            pltpu.VMEM((2, 256, rows), BF),
            pltpu.VMEM((rows, 256), BF),
            pltpu.VMEM((21, 64, 256), F32),
            pltpu.VMEM((3, 4, 4, 64, 256), F32),
            pltpu.VMEM((rows, 256), F32),
            pltpu.VMEM((2, 1024, 256), BF),
            pltpu.VMEM((2, 256, 1024), BF),
            pltpu.VMEM((4, 2, 2, 64, 256), BF),
            pltpu.VMEM((4, 2, 64, 256), BF),
            pltpu.VMEM((4, 2, 64, 256), BF),
            pltpu.VMEM((2, 2, 4, 2, 128, 256), F32),
            pltpu.VMEM((2, 2, 4, 128, 256), BF),
            pltpu.VMEM((2, 2, 4, 128, 256), BF),
            pltpu.VMEM((2, 2, 4, 128, 256), BF),
            pltpu.VMEM((2, 2, 3, 128, 256), BF),
            pltpu.VMEM((2, 16, 16, 256), BF),
            pltpu.VMEM((2, 16, 16, 256), F32),
            pltpu.VMEM((2, 15, 16, 256), BF),
            pltpu.VMEM((2, 16, 16, 256), BF),
            pltpu.VMEM((2, 16, 16, 256), BF),
            pltpu.VMEM((16, 256), F32),
            pltpu.VMEM((16, 256), BF),
            pltpu.VMEM((16, 256), BF),
            pltpu.VMEM((3, 16, 256), BF),
            pltpu.VMEM((16, 256), BF),
            pltpu.VMEM((15, 16, 256), BF),
            pltpu.VMEM((16, 256), BF),
            dma((5,)),
            dma,
            dma((4, 2)),
            dma((4, 2)),
            dma((2, 2)),
            dma((2, 2)),
            dma((2, 2, 3)),
            dma((2, 2, 3)),
            dma((2,)),
            dma((2,)),
            dma((2,)),
            dma((2,)),
            dma((2,)),
            dma((2,)),
            dma((5,)),
            dma((5,)),
        ],
        compiler_params=pltpu.CompilerParams(
            collective_id=0, has_side_effects=True, vmem_limit_bytes=58 * 1024 * 1024
        ),
        name="blocks",
    )(
        latents.reshape(rows, channels),
        cotangent.reshape(rows, channels),
        w_up, w_down, depth_w.transpose(1, 0, 2), time_table, timesteps, brick_counts, send_list, recv_list,
    )
    return out.reshape(latents.shape), up, down, depth.transpose(1, 0, 2)


def solution(mesh):
    spread = ("rep", "space")
    return jax.shard_map(
        on_device,
        mesh=mesh,
        in_specs=(
            P(spread, None, None),
            P(spread, None, None),
            P(), P(), P(), P(),
            P("rep"),
            P(spread),
            P(spread, None, None),
            P(spread, None),
        ),
        out_specs=(
            P(spread, None, None),
            P(None, None, "rep"),
            P(None, "rep", None),
            P(None, None, "rep"),
        ),
        check_vma=False,
    )
```

```python
import functools
import math

import jax
import jax.numpy as jnp
from jax import lax
from jax.experimental import pallas as pl
from jax.experimental.pallas import tpu as pltpu
from jax.sharding import PartitionSpec as P

MESH = pl.DeviceIdType.MESH
BF = jnp.bfloat16
F32 = jnp.float32
CUBIC = 0.044715
ROOT = math.sqrt(2.0 / math.pi)
LOG2E = math.log2(math.e)


def gelu_pair(u):
    square = u * u
    power = u * ((-2.0 * ROOT * LOG2E) + (-2.0 * ROOT * CUBIC * LOG2E) * square)
    e = jnp.exp2(jnp.minimum(power, 80.0))
    gate = 1.0 / (1.0 + e)
    hidden = u * gate
    slope = gate + hidden * (e * gate) * ((2.0 * ROOT) + (6.0 * ROOT * CUBIC) * square)
    return hidden, slope


def dot(a, b):
    return jnp.dot(a, b, preferred_element_type=F32)


def kernel(
    scale,
    lat_hbm, cot_hbm, wu_hbm, wd_hbm, dw_ref, tt_hbm, ts_ref, cnt_ref, snd_ref, rcv_ref,
    out_ref, gup_ref, gdn_ref, dep_ref,
    latv, cotv, wu, wd, tt, field, act, hid, slo, dp, dact, turn_g, turn_a, grad, pool, ghost, base, wut, wdt,
    fsend, flow, fupp, k1, s1, r1, s2, r2, r3, r5, dacc, ds1, dr1, ds2, dr2, ds3, dr3,
    in_sem, fs_sem, fr_sem, c1s, c1r, c2s, c2r, c3s, c3r, c5s, c5r, e_s, e_r,
):
    me_x = lax.axis_index("rep")
    me_p = lax.axis_index("space")
    core = lax.rem(me_p, 2)
    twin = {"rep": me_x, "space": me_p + 1 - 2 * core}
    below = {"rep": me_x, "space": lax.rem(me_p + 31, 32)}
    above = {"rep": me_x, "space": lax.rem(me_p + 1, 32)}

    me_z = me_p // 8
    me_y = lax.rem(me_p // 2, 4)
    me_xy = me_x * 4 + me_y

    def along_xy(d):
        to = lax.rem(me_xy + d, 16)
        return {"rep": to // 4, "space": me_z * 8 + lax.rem(to, 4) * 2 + core}

    def along_z(d):
        return {"rep": me_x, "space": lax.rem(me_p + 8 * d, 32)}

    def along_y(d, side):
        return {"rep": me_x, "space": me_z * 8 + lax.rem(me_y + d, 4) * 2 + side}

    loads = [
        pltpu.make_async_copy(a, b, in_sem.at[i])
        for i, (a, b) in enumerate(
            ((lat_hbm, latv), (wu_hbm, wu), (tt_hbm, tt), (wd_hbm, wd), (cot_hbm, cotv))
        )
    ]
    for copy in loads:
        copy.start()

    barrier = pltpu.get_barrier_semaphore()
    for peer in [twin, below, above] + [along_z(d) for d in (1, 2, 3)]:
        pl.semaphore_signal(barrier, inc=1, device_id=peer, device_id_type=MESH)

    for d in (1, 2, 3):
        pl.semaphore_signal(barrier, inc=1, device_id=along_y(d, 1 - core), device_id_type=MESH)

    @pl.loop(1, 16)
    def _(d):
        pl.semaphore_signal(barrier, inc=1, device_id=along_xy(d), device_id_type=MESH)

    def rows_of(s):
        return pl.ds(pl.multiple_of(s * 512, 512), 512)

    def occupied(s):
        return jnp.minimum(jnp.maximum(cnt_ref[0] - s, 0), 1).astype(F32)

    def remote(src, dst, send, recv, peer):
        return pltpu.make_async_remote_copy(
            src_ref=src, dst_ref=dst, send_sem=send, recv_sem=recv, device_id=peer, device_id_type=MESH
        )

    def pool_faces(src):
        @pl.loop(0, 4)
        def _(s):
            for x in range(8):
                plane = src[pl.ds(pl.multiple_of(s * 512 + x * 64, 64), 64), :].astype(F32)
                if x == 0:
                    pool[1 + 4 * s] = plane
                if x == 7:
                    pool[2 + 4 * s] = plane
                pool[3 + 4 * s, x * 8:x * 8 + 8] = plane[:8]
                pool[4 + 4 * s, x * 8:x * 8 + 8] = plane[56:]

    def face_copies(turn):
        return (
            remote(fsend.at[turn, 1], flow.at[turn], fs_sem.at[turn, 1], fr_sem.at[turn, 1], above),
            remote(fsend.at[turn, 0], fupp.at[turn], fs_sem.at[turn, 0], fr_sem.at[turn, 0], below),
        )

    def send_faces(turn):
        for k in range(2):
            for e in range(2):
                fsend[turn, k, e] = pool[1 + snd_ref[0, k, e]].astype(BF)
        for copy in face_copies(turn):
            copy.start()

    def take_faces(turn, kept):
        for copy in face_copies(turn):
            copy.wait()
        lower = jnp.where(me_p > 0, 1.0, 0.0).astype(F32)
        upper = jnp.where(me_p < 31, 1.0, 0.0).astype(F32)
        for e in range(2):
            pool[17 + e] = flow[turn, e].astype(F32) * lower
            pool[19 + e] = fupp[turn, e].astype(F32) * upper

        @pl.loop(0, 4)
        def _(s):
            for side in range(4):
                ghost[kept, s, side] = pool[rcv_ref[s, side]]

    zed = lax.broadcasted_iota(jnp.int32, (8, 128), 0)

    def taps(src, s, cols):
        def plane(x):
            rows = pl.ds(pl.multiple_of(s * 512 + x * 64, 64), 64)
            return src[rows, cols].astype(F32).reshape(8, 8, 128)

        blank = jnp.zeros((1, 8, 128), F32)
        before = None
        here = plane(0)
        for x in range(8):
            after = plane(x + 1) if x < 7 else None
            y_low = jnp.concatenate([blank, here[:7]], axis=0)
            y_upp = jnp.concatenate([here[1:], blank], axis=0)
            yield x, (here, before, after, y_low, y_upp, pltpu.roll(here, 1, 1), pltpu.roll(here, 7, 1))
            before, here = here, after

    def tap_weights(b, cols, low, upp):
        w = [jnp.broadcast_to(dw_ref[i, b:b + 1, cols], (8, 128)) for i in range(7)]
        w[5] = jnp.where(zed == low, 0.0, w[5])
        w[6] = jnp.where(zed == upp, 0.0, w[6])
        return w

    def base_forward(b):
        for lane in range(2):
            cols = slice(lane * 128, lane * 128 + 128)
            w = tap_weights(b, cols, 0, 7)
            shift = jnp.broadcast_to(moment[:, cols], (8, 128))

            @pl.loop(0, 4)
            def _(s):
                for x, near in taps(field.at[b], s, cols):
                    total = shift[None]
                    for i in range(7):
                        if near[i] is not None:
                            total = total + w[i][None] * near[i]
                    rows = pl.ds(pl.multiple_of(s * 512 + x * 64, 64), 64)
                    base[rows, cols] = total.reshape(64, 128)

    def with_ghosts(kept, s, x, w):
        total = base[pl.ds(pl.multiple_of(s * 512 + x * 64, 64), 64), :]
        if x == 0:
            total = total + w[0] * ghost[kept, s, 0]
        if x == 7:
            total = total + w[1] * ghost[kept, s, 1]
        edge = slice(x * 8, x * 8 + 8)
        low = total[:8] + w[2] * ghost[kept, s, 2, edge]
        upp = total[56:] + w[3] * ghost[kept, s, 3, edge]
        return jnp.concatenate([low, total[8:56], upp], axis=0)

    def finish_forward(b):
        w = [dw_ref[i, b:b + 1, :] for i in (1, 2, 3, 4)]

        @pl.loop(0, 4)
        def _(s):
            for x in range(8):
                rows = pl.ds(pl.multiple_of(s * 512 + x * 64, 64), 64)
                act[b, rows, :] = with_ghosts(b, s, x, w).astype(BF)

    mirror = (0, 2, 1, 4, 3, 6, 5)

    def base_backward(b):
        for lane in range(2):
            cols = slice(lane * 128, lane * 128 + 128)
            w = tap_weights(b, cols, 7, 0)

            def slot(s, sums):
                sums = list(sums)
                for x, near in taps(dact, s, cols):
                    rows = pl.ds(pl.multiple_of(s * 512 + x * 64, 64), 64)
                    total = grad[rows, cols].astype(F32).reshape(8, 8, 128)
                    value = field[b, rows, cols].astype(F32).reshape(8, 8, 128)
                    here = near[0]
                    for i in range(7):
                        if near[mirror[i]] is not None:
                            total = total + w[i][None] * near[mirror[i]]
                            sums[i] = sums[i] + jnp.sum(value * near[mirror[i]], axis=0)
                    if x == 0:
                        sums[1] = sums[1] + jnp.sum(ghost[b, s, 0, :, cols].reshape(8, 8, 128) * here, axis=0)
                    if x == 7:
                        sums[2] = sums[2] + jnp.sum(ghost[b, s, 1, :, cols].reshape(8, 8, 128) * here, axis=0)
                    sums[3] = sums[3] + ghost[b, s, 2, x * 8:x * 8 + 8, cols] * here[0]
                    sums[4] = sums[4] + ghost[b, s, 3, x * 8:x * 8 + 8, cols] * here[7]
                    base[rows, cols] = total.reshape(64, 128)
                return tuple(sums)

            sums = list(lax.fori_loop(0, 4, slot, tuple(jnp.zeros((8, 128), F32) for _ in range(7))))
            sums[5] = jnp.where(zed == 7, 0.0, sums[5])
            sums[6] = jnp.where(zed == 0, 0.0, sums[6])
            for i in range(7):
                dacc[7 * b + i:7 * b + i + 1, cols] = jnp.sum(sums[i], axis=0, keepdims=True)

    def finish_backward(b):
        w = [dw_ref[i, b:b + 1, :] for i in (2, 1, 4, 3)]

        @pl.loop(0, 4)
        def _(s):
            occ = occupied(s)
            for x in range(8):
                rows = pl.ds(pl.multiple_of(s * 512 + x * 64, 64), 64)
                grad[rows, :] = (with_ghosts(2, s, x, w) * occ).astype(BF)

    def c1(b, kind):
        return remote(s1.at[b, kind], r1.at[b, kind], c1s.at[b, kind], c1r.at[b, kind], twin)

    def weight_grad(b, kind, left, right):
        tile = dot(left[...], right[...])
        for j in range(4):
            k1[b, kind, j] = tile[:, j * 256:j * 256 + 256].reshape(2, 128, 256)
            s1[b, kind, j] = k1[b, kind, j, 1 - core].astype(BF)
        c1(b, kind).start()

    def wait_all(ref, send, recv):
        pltpu.make_async_copy(ref, ref, send).wait()
        pltpu.make_async_copy(ref, ref, recv).wait()

    def c2(b, kind, d):
        to = lax.rem(me_xy + d, 16)
        return remote(s2.at[b, kind, to], r2.at[b, kind, d - 1], c2s.at[b, kind], c2r.at[b, kind], along_xy(d))

    def step2(b, kind):
        c1(b, kind).wait()
        for j in range(4):
            total = k1[b, kind, j, core] + r1[b, kind, j].astype(F32)
            s2[b, kind, 4 * j:4 * j + 4] = total.reshape(4, 32, 256).astype(BF)

        @pl.loop(1, 16)
        def _(d):
            c2(b, kind, d).start()

    def c3(b, d):
        return remote(r3.at[b, me_z], r3.at[b, me_z], c3s.at[b, d - 1], c3r.at[b, d - 1], along_z(d))

    def step3(b):
        for kind in range(2):
            wait_all(r2.at[b, kind], c2s.at[b, kind], c2r.at[b, kind])
            rows = pl.ds(pl.multiple_of(me_y * 32, 32), 32)
            total = k1[b, kind, me_x, core, rows] + r1[b, kind, me_x, rows].astype(F32)
            for d in range(15):
                total = total + r2[b, kind, d].astype(F32)
            r3[b, me_z, kind] = total.astype(BF)
        for d in (2, 1, 3):
            c3(b, d).start()

    def c5(b, i):
        peers = [twin] + [along_y(d, side) for d in (1, 2, 3) for side in (core, 1 - core)]
        return remote(r5.at[b, core, me_y], r5.at[b, core, me_y], c5s.at[b, i], c5r.at[b, i], peers[i])

    def step5(b):
        for d in (1, 2, 3):
            c3(b, d).wait()
        for kind in range(2):
            total = r3[b, 0, kind].astype(F32)
            for z in range(1, 4):
                total = total + r3[b, z, kind].astype(F32)
            r5[b, core, me_y, kind] = total.astype(BF)
        for i in (3, 4, 1, 2, 5, 6, 0):
            c5(b, i).start()

    def finish(b):
        for i in range(7):
            c5(b, i).wait()
        for side in range(2):
            at = slice(side * 128, side * 128 + 128)
            gup_ref[b, at, :] = r5[b, side, :, 1].reshape(128, 256).astype(F32) * scale
            gdn_ref[b, :, at] = (r5[b, side, :, 0].reshape(128, 256).astype(F32) * scale).T

    def e1():
        return remote(ds1, dr1, e_s.at[0], e_r.at[0], twin)

    def e2(d):
        return remote(ds2, dr2.at[d - 1], e_s.at[1], e_r.at[1], along_xy(d))

    def e3(d):
        return remote(ds3, dr3.at[d - 1], e_s.at[1 + d], e_r.at[1 + d], along_z(d))

    def turn(dst, src):
        @pl.loop(0, 4)
        def _(s):
            dst[:, rows_of(s)] = src[rows_of(s), :].T

    loads[0].wait()

    @pl.loop(0, 4)
    def _(s):
        field[0, rows_of(s), :] = (latv[rows_of(s), :].astype(F32) * occupied(s)).astype(BF)

    pool[0] = jnp.zeros((64, 256), F32)
    pool_faces(field.at[0])
    pl.semaphore_wait(barrier, 24)
    send_faces(0)
    loads[2].wait()
    table_row = lax.broadcasted_iota(jnp.int32, (1000, 256), 0)
    moment = jnp.sum(jnp.where(table_row == ts_ref[0], tt[...], 0.0), axis=0, keepdims=True)
    base_forward(0)
    loads[1].wait()
    loads[3].wait()
    for b in range(2):
        wut[b] = wu[b].T
        wdt[b] = wd[b].T
    loads[4].wait()

    @pl.loop(0, 4)
    def _(s):
        rows = rows_of(s)
        value = (cotv[rows, :].astype(F32) * occupied(s)).astype(BF)
        grad[rows, :] = value
        turn_g[:, rows] = value.T

    take_faces(0, 0)
    finish_forward(0)
    for n in range(4):
        part = slice(n * 256, n * 256 + 256)
        hid[0, :, part], slo[:, part] = gelu_pair(dot(act[0], wu[0, :, part]).astype(BF))
    for s in range(4):
        rows = slice(s * 512, s * 512 + 512)
        total = field[0, rows, :].astype(F32) + dot(hid[0, rows, :], wd[0])
        field[1, rows, :] = (total * occupied(s)).astype(BF)
    pool_faces(field.at[1])
    send_faces(1)
    base_forward(1)
    for n in range(4):
        part = slice(n * 256, n * 256 + 256)
        dp[:, part] = dot(grad[...], wdt[1, :, part]).astype(BF)
    turn(turn_a.at[0], act.at[0])
    take_faces(1, 1)
    finish_forward(1)

    for n in range(4):
        part = slice(n * 256, n * 256 + 256)
        hidden, slope = gelu_pair(dot(act[1], wu[1, :, part]).astype(BF))
        hid[1, :, part] = hidden
        dp[:, part] = dp[:, part] * slope
    dact[...] = dot(dp[...], wut[1]).astype(BF)
    pool_faces(dact)
    send_faces(2)
    weight_grad(1, 0, turn_g, hid.at[1])
    turn(turn_a.at[1], act.at[1])
    weight_grad(1, 1, turn_a.at[1], dp)
    base_backward(1)
    step2(1, 0)
    step2(1, 1)
    take_faces(2, 2)
    finish_backward(1)

    turn(turn_g, grad)
    weight_grad(0, 0, turn_g, hid.at[0])
    for n in range(4):
        part = slice(n * 256, n * 256 + 256)
        dp[:, part] = dot(grad[...], wdt[0, :, part]).astype(BF) * slo[:, part]
    step2(0, 0)
    weight_grad(0, 1, turn_a.at[0], dp)
    dact[...] = dot(dp[...], wut[0]).astype(BF)
    step2(0, 1)
    pool_faces(dact)
    send_faces(3)
    step3(1)
    dacc[14:16] = jnp.zeros((2, 256), F32)
    base_backward(0)
    ds1[...] = dacc[...].astype(BF)
    e1().start()
    step5(1)
    take_faces(3, 2)
    finish_backward(0)
    out_ref[...] = grad[...]
    e1().wait()
    dsum = dacc[...] + dr1[...].astype(F32)
    ds2[...] = dsum.astype(BF)

    @pl.loop(1, 16)
    def _(d):
        e2(d).start()

    step3(0)
    finish(1)
    wait_all(dr2, e_s.at[1], e_r.at[1])
    for d in range(15):
        dsum = dsum + dr2[d].astype(F32)
    ds3[...] = dsum.astype(BF)
    for d in (1, 2, 3):
        e3(d).start()
    step5(0)
    for d in (1, 2, 3):
        e3(d).wait()
    for d in range(3):
        dsum = dsum + dr3[d].astype(F32)
    dsum = dsum * scale
    share = jnp.zeros((16, 64), F32)
    for j in range(4):
        share = jnp.where(me_x == j, dsum[:, j * 64:j * 64 + 64], share)
    for i in range(7):
        dep_ref[i, 0:1] = share[i:i + 1]
        dep_ref[i, 1:2] = share[7 + i:8 + i]
    finish(0)


def on_device(latents, cotangent, w_up, w_down, depth_w, time_table, timesteps, brick_counts, send_list, recv_list):
    bricks, voxels, channels = latents.shape
    rows = bricks * voxels
    scale = 1.0 / math.sqrt(rows * lax.axis_size("rep") * lax.axis_size("space"))
    anywhere = pl.BlockSpec(memory_space=pl.ANY)
    vmem = pl.BlockSpec(memory_space=pltpu.VMEM)
    smem = pl.BlockSpec(memory_space=pltpu.SMEM)
    dma = pltpu.SemaphoreType.DMA
    out, up, down, depth = pl.pallas_call(
        functools.partial(kernel, scale),
        out_shape=(
            pltpu.VMEM((rows, channels), BF),
            pltpu.VMEM((2, 256, 256), F32),
            pltpu.VMEM((2, 256, 256), F32),
            pltpu.VMEM((7, 2, 64), F32),
        ),
        in_specs=[anywhere] * 4 + [vmem, anywhere] + [smem] * 4,
        out_specs=(vmem, vmem, vmem, vmem),
        scratch_shapes=[
            pltpu.VMEM((rows, 256), BF),
            pltpu.VMEM((rows, 256), BF),
            pltpu.VMEM((2, 256, 1024), BF),
            pltpu.VMEM((2, 1024, 256), BF),
            pltpu.VMEM((1000, 256), F32),
            pltpu.VMEM((2, rows, 256), BF),
            pltpu.VMEM((2, rows, 256), BF),
            pltpu.VMEM((2, rows, 1024), BF),
            pltpu.VMEM((rows, 1024), BF),
            pltpu.VMEM((rows, 1024), BF),
            pltpu.VMEM((rows, 256), BF),
            pltpu.VMEM((256, rows), BF),
            pltpu.VMEM((2, 256, rows), BF),
            pltpu.VMEM((rows, 256), BF),
            pltpu.VMEM((21, 64, 256), F32),
            pltpu.VMEM((3, 4, 4, 64, 256), F32),
            pltpu.VMEM((rows, 256), F32),
            pltpu.VMEM((2, 1024, 256), BF),
            pltpu.VMEM((2, 256, 1024), BF),
            pltpu.VMEM((4, 2, 2, 64, 256), BF),
            pltpu.VMEM((4, 2, 64, 256), BF),
            pltpu.VMEM((4, 2, 64, 256), BF),
            pltpu.VMEM((2, 2, 4, 2, 128, 256), F32),
            pltpu.VMEM((2, 2, 4, 128, 256), BF),
            pltpu.VMEM((2, 2, 4, 128, 256), BF),
            pltpu.VMEM((2, 2, 16, 32, 256), BF),
            pltpu.VMEM((2, 2, 15, 32, 256), BF),
            pltpu.VMEM((2, 4, 2, 32, 256), BF),
            pltpu.VMEM((2, 2, 4, 2, 32, 256), BF),
            pltpu.VMEM((16, 256), F32),
            pltpu.VMEM((16, 256), BF),
            pltpu.VMEM((16, 256), BF),
            pltpu.VMEM((16, 256), BF),
            pltpu.VMEM((15, 16, 256), BF),
            pltpu.VMEM((16, 256), BF),
            pltpu.VMEM((3, 16, 256), BF),
            dma((5,)),
            dma((4, 2)),
            dma((4, 2)),
            dma((2, 2)),
            dma((2, 2)),
            dma((2, 2)),
            dma((2, 2)),
            dma((2, 3)),
            dma((2, 3)),
            dma((2, 7)),
            dma((2, 7)),
            dma((5,)),
            dma((5,)),
        ],
        compiler_params=pltpu.CompilerParams(
            collective_id=0, has_side_effects=True, vmem_limit_bytes=58 * 1024 * 1024
        ),
        name="blocks",
    )(
        latents.reshape(rows, channels),
        cotangent.reshape(rows, channels),
        w_up, w_down, depth_w.transpose(1, 0, 2), time_table, timesteps, brick_counts, send_list, recv_list,
    )
    return out.reshape(latents.shape), up, down, depth.transpose(1, 0, 2)


def solution(mesh):
    spread = ("rep", "space")
    return jax.shard_map(
        on_device,
        mesh=mesh,
        in_specs=(
            P(spread, None, None),
            P(spread, None, None),
            P(), P(), P(), P(),
            P("rep"),
            P(spread),
            P(spread, None, None),
            P(spread, None),
        ),
        out_specs=(
            P(spread, None, None),
            P(None, None, "rep"),
            P(None, "rep", None),
            P(None, None, "rep"),
        ),
        check_vma=False,
    )
```

```python
import functools
import math

import jax
import jax.numpy as jnp
from jax import lax
from jax.experimental import pallas as pl
from jax.experimental.pallas import tpu as pltpu
from jax.sharding import PartitionSpec as P

MESH = pl.DeviceIdType.MESH
BF = jnp.bfloat16
F32 = jnp.float32
CUBIC = 0.044715
ROOT = math.sqrt(2.0 / math.pi)
LOG2E = math.log2(math.e)


def gelu_pair(u):
    square = u * u
    power = u * ((-2.0 * ROOT * LOG2E) + (-2.0 * ROOT * CUBIC * LOG2E) * square)
    e = jnp.exp2(jnp.minimum(power, 80.0))
    gate = 1.0 / (1.0 + e)
    hidden = u * gate
    slope = gate + hidden * (e * gate) * ((2.0 * ROOT) + (6.0 * ROOT * CUBIC) * square)
    return hidden, slope


def dot(a, b):
    return jnp.dot(a, b, preferred_element_type=F32)


def kernel(
    scale,
    lat_hbm, cot_hbm, wu_hbm, wd_hbm, dw_ref, tt_hbm, ts_ref, cnt_ref, snd_ref, rcv_ref,
    out_ref, gup_ref, gdn_ref, dep_ref,
    latv, cotv, wu, wd, tt, field, act, hid, slo, dp, dact, turn_g, turn_a, grad, pool, ghost, base, wut, wdt,
    fsend, flow, fupp, k1, s1, r1, s2, r2, r3, r5, dacc, dsums, ds, dr1, dr2,
    in_sem, fs_sem, fr_sem, c1s, c1r, c2s, c2r, c3s, c3r, c5s, c5r, e_s, e_r,
):
    me_x = lax.axis_index("rep")
    me_p = lax.axis_index("space")
    core = lax.rem(me_p, 2)
    twin = {"rep": me_x, "space": me_p + 1 - 2 * core}
    below = {"rep": me_x, "space": lax.rem(me_p + 31, 32)}
    above = {"rep": me_x, "space": lax.rem(me_p + 1, 32)}

    me_z = me_p // 8
    me_y = lax.rem(me_p // 2, 4)
    me_xy = me_x * 4 + me_y

    def along_xy(d):
        to = lax.rem(me_xy + d, 16)
        return {"rep": to // 4, "space": me_z * 8 + lax.rem(to, 4) * 2 + core}

    def along_z(d):
        return {"rep": me_x, "space": lax.rem(me_p + 8 * d, 32)}

    def along_y(d, side):
        return {"rep": me_x, "space": me_z * 8 + lax.rem(me_y + d, 4) * 2 + side}

    loads = [
        pltpu.make_async_copy(a, b, in_sem.at[i])
        for i, (a, b) in enumerate(
            ((lat_hbm, latv), (wu_hbm, wu), (tt_hbm, tt), (wd_hbm, wd), (cot_hbm, cotv))
        )
    ]
    for copy in loads:
        copy.start()

    barrier = pltpu.get_barrier_semaphore()
    for peer in [twin, below, above] + [along_z(d) for d in (1, 2, 3)]:
        pl.semaphore_signal(barrier, inc=1, device_id=peer, device_id_type=MESH)

    for d in (1, 2, 3):
        pl.semaphore_signal(barrier, inc=1, device_id=along_y(d, 1 - core), device_id_type=MESH)

    @pl.loop(1, 16)
    def _(d):
        pl.semaphore_signal(barrier, inc=1, device_id=along_xy(d), device_id_type=MESH)

    def rows_of(s):
        return pl.ds(pl.multiple_of(s * 512, 512), 512)

    def occupied(s):
        return jnp.minimum(jnp.maximum(cnt_ref[0] - s, 0), 1).astype(F32)

    def remote(src, dst, send, recv, peer):
        return pltpu.make_async_remote_copy(
            src_ref=src, dst_ref=dst, send_sem=send, recv_sem=recv, device_id=peer, device_id_type=MESH
        )

    def pool_faces(src):
        @pl.loop(0, 4)
        def _(s):
            for x in range(8):
                plane = src[pl.ds(pl.multiple_of(s * 512 + x * 64, 64), 64), :].astype(F32)
                if x == 0:
                    pool[1 + 4 * s] = plane
                if x == 7:
                    pool[2 + 4 * s] = plane
                pool[3 + 4 * s, x * 8:x * 8 + 8] = plane[:8]
                pool[4 + 4 * s, x * 8:x * 8 + 8] = plane[56:]

    def face_copies(turn):
        return (
            remote(fsend.at[turn, 1], flow.at[turn], fs_sem.at[turn, 1], fr_sem.at[turn, 1], above),
            remote(fsend.at[turn, 0], fupp.at[turn], fs_sem.at[turn, 0], fr_sem.at[turn, 0], below),
        )

    def send_faces(turn):
        for k in range(2):
            for e in range(2):
                fsend[turn, k, e] = pool[1 + snd_ref[0, k, e]].astype(BF)
        for copy in face_copies(turn):
            copy.start()

    def take_faces(turn, kept):
        for copy in face_copies(turn):
            copy.wait()
        lower = jnp.where(me_p > 0, 1.0, 0.0).astype(F32)
        upper = jnp.where(me_p < 31, 1.0, 0.0).astype(F32)
        for e in range(2):
            pool[17 + e] = flow[turn, e].astype(F32) * lower
            pool[19 + e] = fupp[turn, e].astype(F32) * upper

        @pl.loop(0, 4)
        def _(s):
            for side in range(4):
                ghost[kept, s, side] = pool[rcv_ref[s, side]]

    zed = lax.broadcasted_iota(jnp.int32, (8, 128), 0)

    def taps(src, s, cols):
        def plane(x):
            rows = pl.ds(pl.multiple_of(s * 512 + x * 64, 64), 64)
            return src[rows, cols].astype(F32).reshape(8, 8, 128)

        blank = jnp.zeros((1, 8, 128), F32)
        before = None
        here = plane(0)
        for x in range(8):
            after = plane(x + 1) if x < 7 else None
            y_low = jnp.concatenate([blank, here[:7]], axis=0)
            y_upp = jnp.concatenate([here[1:], blank], axis=0)
            yield x, (here, before, after, y_low, y_upp, pltpu.roll(here, 1, 1), pltpu.roll(here, 7, 1))
            before, here = here, after

    def tap_weights(b, cols, low, upp):
        w = [jnp.broadcast_to(dw_ref[i, b:b + 1, cols], (8, 128)) for i in range(7)]
        w[5] = jnp.where(zed == low, 0.0, w[5])
        w[6] = jnp.where(zed == upp, 0.0, w[6])
        return w

    def base_forward(b):
        for lane in range(2):
            cols = slice(lane * 128, lane * 128 + 128)
            w = tap_weights(b, cols, 0, 7)
            shift = jnp.broadcast_to(moment[:, cols], (8, 128))

            @pl.loop(0, 4)
            def _(s):
                for x, near in taps(field.at[b], s, cols):
                    total = shift[None]
                    for i in range(7):
                        if near[i] is not None:
                            total = total + w[i][None] * near[i]
                    rows = pl.ds(pl.multiple_of(s * 512 + x * 64, 64), 64)
                    base[rows, cols] = total.reshape(64, 128)

    def with_ghosts(kept, s, x, w):
        total = base[pl.ds(pl.multiple_of(s * 512 + x * 64, 64), 64), :]
        if x == 0:
            total = total + w[0] * ghost[kept, s, 0]
        if x == 7:
            total = total + w[1] * ghost[kept, s, 1]
        edge = slice(x * 8, x * 8 + 8)
        low = total[:8] + w[2] * ghost[kept, s, 2, edge]
        upp = total[56:] + w[3] * ghost[kept, s, 3, edge]
        return jnp.concatenate([low, total[8:56], upp], axis=0)

    def finish_forward(b):
        w = [dw_ref[i, b:b + 1, :] for i in (1, 2, 3, 4)]

        @pl.loop(0, 4)
        def _(s):
            for x in range(8):
                rows = pl.ds(pl.multiple_of(s * 512 + x * 64, 64), 64)
                act[b, rows, :] = with_ghosts(b, s, x, w).astype(BF)

    mirror = (0, 2, 1, 4, 3, 6, 5)

    def base_backward(b, products):
        dsums[...] = jnp.zeros((7, 8, 256), F32)

        @pl.loop(0, 2)
        def _(h):
            part = pl.ds(pl.multiple_of(h * 512, 512), 512)
            for kind, left, right in products:
                tile = dot(left[...], right[:, part])
                for j in range(2):
                    k1[b, kind, 2 * h + j] = tile[:, j * 256:j * 256 + 256].reshape(2, 128, 256)
                    s1[b, kind, 2 * h + j] = k1[b, kind, 2 * h + j, 1 - core].astype(BF)
            for lane in range(2):
                cols = slice(lane * 128, lane * 128 + 128)
                w = tap_weights(b, cols, 7, 0)
                sums = [dsums[i, :, cols] for i in range(7)]
                for t in range(2):
                    s = 2 * h + t
                    for x, near in taps(dact, s, cols):
                        rows = pl.ds(pl.multiple_of(s * 512 + x * 64, 64), 64)
                        total = grad[rows, cols].astype(F32).reshape(8, 8, 128)
                        value = field[b, rows, cols].astype(F32).reshape(8, 8, 128)
                        here = near[0]
                        for i in range(7):
                            if near[mirror[i]] is not None:
                                total = total + w[i][None] * near[mirror[i]]
                                sums[i] = sums[i] + jnp.sum(value * near[mirror[i]], axis=0)
                        if x == 0:
                            sums[1] = sums[1] + jnp.sum(ghost[b, s, 0, :, cols].reshape(8, 8, 128) * here, axis=0)
                        if x == 7:
                            sums[2] = sums[2] + jnp.sum(ghost[b, s, 1, :, cols].reshape(8, 8, 128) * here, axis=0)
                        sums[3] = sums[3] + ghost[b, s, 2, x * 8:x * 8 + 8, cols] * here[0]
                        sums[4] = sums[4] + ghost[b, s, 3, x * 8:x * 8 + 8, cols] * here[7]
                        base[rows, cols] = total.reshape(64, 128)
                for i in range(7):
                    dsums[i, :, cols] = sums[i]

        for kind, left, right in products:
            c1(b, kind).start()
        inside = lax.broadcasted_iota(jnp.int32, (8, 256), 0)
        for i in range(7):
            total = dsums[i]
            if i == 5:
                total = jnp.where(inside == 7, 0.0, total)
            if i == 6:
                total = jnp.where(inside == 0, 0.0, total)
            dacc[7 * b + i:7 * b + i + 1, :] = jnp.sum(total, axis=0, keepdims=True)

    def finish_backward(b, dst):
        w = [dw_ref[i, b:b + 1, :] for i in (2, 1, 4, 3)]

        @pl.loop(0, 4)
        def _(s):
            occ = occupied(s)
            for x in range(8):
                rows = pl.ds(pl.multiple_of(s * 512 + x * 64, 64), 64)
                dst[rows, :] = (with_ghosts(2, s, x, w) * occ).astype(BF)

    def c1(b, kind):
        return remote(s1.at[b, kind], r1.at[b, kind], c1s.at[b, kind], c1r.at[b, kind], twin)

    def weight_grad(b, kind, left, right):
        tile = dot(left[...], right[...])
        for j in range(4):
            k1[b, kind, j] = tile[:, j * 256:j * 256 + 256].reshape(2, 128, 256)
            s1[b, kind, j] = k1[b, kind, j, 1 - core].astype(BF)
        c1(b, kind).start()

    def wait_all(ref, send, recv):
        pltpu.make_async_copy(ref, ref, send).wait()
        pltpu.make_async_copy(ref, ref, recv).wait()

    def c2(b, kind, d):
        to = lax.rem(me_xy + d, 16)
        return remote(s2.at[b, kind, to], r2.at[b, kind, d - 1], c2s.at[b, kind], c2r.at[b, kind], along_xy(d))

    def step2(b, kind):
        c1(b, kind).wait()
        for j in range(4):
            total = k1[b, kind, j, core] + r1[b, kind, j].astype(F32)
            s2[b, kind, 4 * j:4 * j + 4] = total.reshape(4, 32, 256).astype(BF)

        @pl.loop(1, 16)
        def _(d):
            c2(b, kind, d).start()

    def c3(b, d):
        return remote(r3.at[b, me_z], r3.at[b, me_z], c3s.at[b, d - 1], c3r.at[b, d - 1], along_z(d))

    def step3(b):
        for kind in range(2):
            wait_all(r2.at[b, kind], c2s.at[b, kind], c2r.at[b, kind])
            rows = pl.ds(pl.multiple_of(me_y * 32, 32), 32)
            total = k1[b, kind, me_x, core, rows] + r1[b, kind, me_x, rows].astype(F32)
            for d in range(15):
                total = total + r2[b, kind, d].astype(F32)
            r3[b, me_z, kind] = total.astype(BF)
        for d in (2, 1, 3):
            c3(b, d).start()

    def c5(b, i):
        peers = [twin] + [along_y(d, side) for d in (1, 2, 3) for side in (core, 1 - core)]
        return remote(r5.at[b, core, me_y], r5.at[b, core, me_y], c5s.at[b, i], c5r.at[b, i], peers[i])

    def step5(b):
        for d in (1, 2, 3):
            c3(b, d).wait()
        for kind in range(2):
            total = r3[b, 0, kind].astype(F32)
            for z in range(1, 4):
                total = total + r3[b, z, kind].astype(F32)
            r5[b, core, me_y, kind] = total.astype(BF)
        for i in (3, 4, 1, 2, 5, 6, 0):
            c5(b, i).start()

    def finish(b):
        for i in range(7):
            c5(b, i).wait()
        for side in range(2):
            at = slice(side * 128, side * 128 + 128)
            gup_ref[b, at, :] = r5[b, side, :, 1].reshape(128, 256).astype(F32) * scale
            gdn_ref[b, :, at] = (r5[b, side, :, 0].reshape(128, 256).astype(F32) * scale).T

    def e1():
        return remote(ds.at[0], dr1, e_s.at[0], e_r.at[0], twin)

    def e2(d):
        return remote(ds.at[1], dr2.at[0, d - 1], e_s.at[d], e_r.at[d], along_xy(4 * d))

    def e3(d):
        return remote(ds.at[2], dr2.at[1, d - 1], e_s.at[3 + d], e_r.at[3 + d], along_z(d))

    def e4(d):
        return remote(ds.at[3], dr2.at[2, d - 1], e_s.at[6 + d], e_r.at[6 + d], along_y(d, core))

    def taps_start(stage, copy):
        ds[stage] = dacc[...].astype(BF)
        for d in (2, 1, 3):
            copy(d).start()

    def taps_take(stage, copy):
        for d in (1, 2, 3):
            copy(d).wait()
        dacc[...] = dacc[...] + dr2[stage - 1, 0].astype(F32) + dr2[stage - 1, 1].astype(F32) + dr2[stage - 1, 2].astype(F32)

    loads[0].wait()

    @pl.loop(0, 4)
    def _(s):
        field[0, rows_of(s), :] = (latv[rows_of(s), :].astype(F32) * occupied(s)).astype(BF)

    pool[0] = jnp.zeros((64, 256), F32)
    pool_faces(field.at[0])
    pl.semaphore_wait(barrier, 24)
    send_faces(0)
    loads[2].wait()
    table_row = lax.broadcasted_iota(jnp.int32, (1000, 256), 0)
    moment = jnp.sum(jnp.where(table_row == ts_ref[0], tt[...], 0.0), axis=0, keepdims=True)
    base_forward(0)
    loads[1].wait()
    loads[3].wait()
    for b in range(2):
        wut[b] = wu[b].T
        wdt[b] = wd[b].T
    loads[4].wait()

    @pl.loop(0, 4)
    def _(s):
        rows = rows_of(s)
        value = (cotv[rows, :].astype(F32) * occupied(s)).astype(BF)
        grad[rows, :] = value
        turn_g[:, rows] = value.T

    take_faces(0, 0)
    finish_forward(0)
    for n in range(4):
        part = slice(n * 256, n * 256 + 256)
        hid[0, :, part], slo[:, part] = gelu_pair(dot(act[0], wu[0, :, part]).astype(BF))
    for s in range(4):
        rows = slice(s * 512, s * 512 + 512)
        total = field[0, rows, :].astype(F32) + dot(hid[0, rows, :], wd[0])
        field[1, rows, :] = (total * occupied(s)).astype(BF)
    pool_faces(field.at[1])
    send_faces(1)
    base_forward(1)
    for n in range(4):
        part = slice(n * 256, n * 256 + 256)
        dp[:, part] = dot(grad[...], wdt[1, :, part]).astype(BF)
    turn_a[0] = act[0].T
    take_faces(1, 1)
    finish_forward(1)

    turn_a[1] = act[1].T
    for n in range(4):
        part = slice(n * 256, n * 256 + 256)
        hidden, slope = gelu_pair(dot(act[1], wu[1, :, part]).astype(BF))
        hid[1, :, part] = hidden
        dp[:, part] = dp[:, part] * slope
    dact[...] = dot(dp[...], wut[1]).astype(BF)
    pool_faces(dact)
    send_faces(2)
    base_backward(1, ((0, turn_g, hid.at[1]), (1, turn_a.at[1], dp)))
    take_faces(2, 2)
    finish_backward(1, grad)
    step2(1, 0)
    step2(1, 1)

    turn_g[...] = grad[...].T
    weight_grad(0, 0, turn_g, hid.at[0])
    for n in range(4):
        part = slice(n * 256, n * 256 + 256)
        dp[:, part] = dot(grad[...], wdt[0, :, part]).astype(BF) * slo[:, part]
    step2(0, 0)
    weight_grad(0, 1, turn_a.at[0], dp)
    dact[...] = dot(dp[...], wut[0]).astype(BF)
    step2(0, 1)
    pool_faces(dact)
    send_faces(3)
    step3(1)
    dacc[14:16] = jnp.zeros((2, 256), F32)
    base_backward(0, ())
    ds[0] = dacc[...].astype(BF)
    e1().start()
    step5(1)
    e1().wait()
    dacc[...] = dacc[...] + dr1[...].astype(F32)
    taps_start(1, e2)
    take_faces(3, 2)
    finish_backward(0, out_ref)
    step3(0)
    taps_take(1, e2)
    taps_start(2, e3)
    finish(1)
    step5(0)
    taps_take(2, e3)
    taps_start(3, e4)
    taps_take(3, e4)
    dsum = dacc[...] * scale
    share = jnp.zeros((16, 64), F32)
    for j in range(4):
        share = jnp.where(me_x == j, dsum[:, j * 64:j * 64 + 64], share)
    for i in range(7):
        dep_ref[i, 0:1] = share[i:i + 1]
        dep_ref[i, 1:2] = share[7 + i:8 + i]
    finish(0)


def store(*refs):
    sems = refs[8]
    copies = [pltpu.make_async_copy(refs[i], refs[4 + i], sems.at[i]) for i in range(4)]
    for copy in copies:
        copy.start()
    for copy in copies:
        copy.wait()


def on_device(latents, cotangent, w_up, w_down, depth_w, time_table, timesteps, brick_counts, send_list, recv_list):
    bricks, voxels, channels = latents.shape
    rows = bricks * voxels
    scale = 1.0 / math.sqrt(rows * lax.axis_size("rep") * lax.axis_size("space"))
    anywhere = pl.BlockSpec(memory_space=pl.ANY)
    vmem = pl.BlockSpec(memory_space=pltpu.VMEM)
    smem = pl.BlockSpec(memory_space=pltpu.SMEM)
    dma = pltpu.SemaphoreType.DMA
    results = pl.pallas_call(
        functools.partial(kernel, scale),
        out_shape=(
            pltpu.VMEM((rows, channels), BF),
            pltpu.VMEM((2, 256, 256), F32),
            pltpu.VMEM((2, 256, 256), F32),
            pltpu.VMEM((7, 2, 64), F32),
        ),
        in_specs=[anywhere] * 4 + [vmem, anywhere] + [smem] * 4,
        out_specs=(vmem, vmem, vmem, vmem),
        scratch_shapes=[
            pltpu.VMEM((rows, 256), BF),
            pltpu.VMEM((rows, 256), BF),
            pltpu.VMEM((2, 256, 1024), BF),
            pltpu.VMEM((2, 1024, 256), BF),
            pltpu.VMEM((1000, 256), F32),
            pltpu.VMEM((2, rows, 256), BF),
            pltpu.VMEM((2, rows, 256), BF),
            pltpu.VMEM((2, rows, 1024), BF),
            pltpu.VMEM((rows, 1024), BF),
            pltpu.VMEM((rows, 1024), BF),
            pltpu.VMEM((rows, 256), BF),
            pltpu.VMEM((256, rows), BF),
            pltpu.VMEM((2, 256, rows), BF),
            pltpu.VMEM((rows, 256), BF),
            pltpu.VMEM((21, 64, 256), F32),
            pltpu.VMEM((3, 4, 4, 64, 256), F32),
            pltpu.VMEM((rows, 256), F32),
            pltpu.VMEM((2, 1024, 256), BF),
            pltpu.VMEM((2, 256, 1024), BF),
            pltpu.VMEM((4, 2, 2, 64, 256), BF),
            pltpu.VMEM((4, 2, 64, 256), BF),
            pltpu.VMEM((4, 2, 64, 256), BF),
            pltpu.VMEM((2, 2, 4, 2, 128, 256), F32),
            pltpu.VMEM((2, 2, 4, 128, 256), BF),
            pltpu.VMEM((2, 2, 4, 128, 256), BF),
            pltpu.VMEM((2, 2, 16, 32, 256), BF),
            pltpu.VMEM((2, 2, 15, 32, 256), BF),
            pltpu.VMEM((2, 4, 2, 32, 256), BF),
            pltpu.VMEM((2, 2, 4, 2, 32, 256), BF),
            pltpu.VMEM((16, 256), F32),
            pltpu.VMEM((7, 8, 256), F32),
            pltpu.VMEM((4, 16, 256), BF),
            pltpu.VMEM((16, 256), BF),
            pltpu.VMEM((3, 3, 16, 256), BF),
            dma((5,)),
            dma((4, 2)),
            dma((4, 2)),
            dma((2, 2)),
            dma((2, 2)),
            dma((2, 2)),
            dma((2, 2)),
            dma((2, 3)),
            dma((2, 3)),
            dma((2, 7)),
            dma((2, 7)),
            dma((10,)),
            dma((10,)),
        ],
        compiler_params=pltpu.CompilerParams(
            collective_id=0, has_side_effects=True, vmem_limit_bytes=58 * 1024 * 1024
        ),
        name="blocks",
    )(
        latents.reshape(rows, channels),
        cotangent.reshape(rows, channels),
        w_up, w_down, depth_w.transpose(1, 0, 2), time_table, timesteps, brick_counts, send_list, recv_list,
    )
    out, up, down, depth = pl.pallas_call(
        store,
        out_shape=[jax.ShapeDtypeStruct(a.shape, a.dtype) for a in results],
        in_specs=[vmem] * 4,
        out_specs=[anywhere] * 4,
        scratch_shapes=[dma((4,))],
        name="store",
    )(*[pltpu.with_memory_space_constraint(a, pltpu.VMEM) for a in results])
    return out.reshape(latents.shape), up, down, depth.transpose(1, 0, 2)


def solution(mesh):
    spread = ("rep", "space")
    return jax.shard_map(
        on_device,
        mesh=mesh,
        in_specs=(
            P(spread, None, None),
            P(spread, None, None),
            P(), P(), P(), P(),
            P("rep"),
            P(spread),
            P(spread, None, None),
            P(spread, None),
        ),
        out_specs=(
            P(spread, None, None),
            P(None, None, "rep"),
            P(None, "rep", None),
            P(None, None, "rep"),
        ),
        check_vma=False,
    )
```

```python
import functools
import math

import jax
import jax.numpy as jnp
from jax import lax
from jax.experimental import pallas as pl
from jax.experimental.pallas import tpu as pltpu
from jax.sharding import PartitionSpec as P

MESH = pl.DeviceIdType.MESH
BF = jnp.bfloat16
F32 = jnp.float32
CUBIC = 0.044715
ROOT = math.sqrt(2.0 / math.pi)
LOG2E = math.log2(math.e)


def gelu_pair(u):
    square = u * u
    power = u * ((-2.0 * ROOT * LOG2E) + (-2.0 * ROOT * CUBIC * LOG2E) * square)
    e = jnp.exp2(jnp.minimum(power, 80.0))
    gate = 1.0 / (1.0 + e)
    hidden = u * gate
    slope = gate + hidden * (e * gate) * ((2.0 * ROOT) + (6.0 * ROOT * CUBIC) * square)
    return hidden, slope


def dot(a, b):
    return jnp.dot(a, b, preferred_element_type=F32)


def kernel(
    scale,
    lat_hbm, cot_hbm, wu_hbm, wd_hbm, dw_ref, tt_hbm, ts_ref, cnt_ref, snd_ref, rcv_ref,
    out_ref, gup_ref, gdn_ref, dep_ref,
    latv, cotv, wu, wd, tt, field, act, hid, slo, dp, dact, turn_g, turn_a, grad, pool, ghost, base, wut, wdt,
    fsend, flow, fupp, k1, s1, r1, s2, r2, r3, r5, dacc, dsums, ds, dr1, dr2,
    in_sem, fs_sem, fr_sem, c1s, c1r, c2s, c2r, c3s, c3r, c5s, c5r, e_s, e_r,
):
    me_x = lax.axis_index("rep")
    me_p = lax.axis_index("space")
    core = lax.rem(me_p, 2)
    twin = {"rep": me_x, "space": me_p + 1 - 2 * core}
    below = {"rep": me_x, "space": lax.rem(me_p + 31, 32)}
    above = {"rep": me_x, "space": lax.rem(me_p + 1, 32)}

    me_z = me_p // 8
    me_y = lax.rem(me_p // 2, 4)
    me_xy = me_x * 4 + me_y

    def along_xy(d):
        to = lax.rem(me_xy + d, 16)
        return {"rep": to // 4, "space": me_z * 8 + lax.rem(to, 4) * 2 + core}

    def along_z(d):
        return {"rep": me_x, "space": lax.rem(me_p + 8 * d, 32)}

    def along_y(d, side):
        return {"rep": me_x, "space": me_z * 8 + lax.rem(me_y + d, 4) * 2 + side}

    loads = [
        pltpu.make_async_copy(a, b, in_sem.at[i])
        for i, (a, b) in enumerate(
            ((lat_hbm, latv), (wu_hbm, wu), (tt_hbm, tt), (wd_hbm, wd), (cot_hbm, cotv))
        )
    ]
    loads[0].start()
    barrier = pltpu.get_barrier_semaphore()

    @pl.loop(1, 16)
    def _(d):
        pl.semaphore_signal(barrier, inc=1, device_id=along_xy(d), device_id_type=MESH)

    for peer in [along_z(d) for d in (2, 1, 3)] + [along_y(d, 1 - core) for d in (2, 1, 3)] + [above, below, twin]:
        pl.semaphore_signal(barrier, inc=1, device_id=peer, device_id_type=MESH)
    for copy in loads[1:]:
        copy.start()

    def rows_of(s):
        return pl.ds(pl.multiple_of(s * 512, 512), 512)

    def occupied(s):
        return jnp.minimum(jnp.maximum(cnt_ref[0] - s, 0), 1).astype(F32)

    def remote(src, dst, send, recv, peer):
        return pltpu.make_async_remote_copy(
            src_ref=src, dst_ref=dst, send_sem=send, recv_sem=recv, device_id=peer, device_id_type=MESH
        )

    def pool_faces(src):
        @pl.loop(0, 4)
        def _(s):
            for x in range(8):
                plane = src[pl.ds(pl.multiple_of(s * 512 + x * 64, 64), 64), :].astype(F32)
                if x == 0:
                    pool[1 + 4 * s] = plane
                if x == 7:
                    pool[2 + 4 * s] = plane
                pool[3 + 4 * s, x * 8:x * 8 + 8] = plane[:8]
                pool[4 + 4 * s, x * 8:x * 8 + 8] = plane[56:]

    def pool_slot(s, value):
        planes = value.astype(F32).reshape(8, 64, 256)
        pool[1 + 4 * s] = planes[0]
        pool[2 + 4 * s] = planes[7]
        pool[3 + 4 * s] = planes[:, :8].reshape(64, 256)
        pool[4 + 4 * s] = planes[:, 56:].reshape(64, 256)

    def face_copies(turn):
        return (
            remote(fsend.at[turn, 1], flow.at[turn], fs_sem.at[turn, 1], fr_sem.at[turn, 1], above),
            remote(fsend.at[turn, 0], fupp.at[turn], fs_sem.at[turn, 0], fr_sem.at[turn, 0], below),
        )

    def send_faces(turn):
        for k in range(2):
            for e in range(2):
                fsend[turn, k, e] = pool[1 + snd_ref[0, k, e]].astype(BF)
        for copy in face_copies(turn):
            copy.start()

    def take_faces(turn, kept):
        for copy in face_copies(turn):
            copy.wait()
        lower = jnp.where(me_p > 0, 1.0, 0.0).astype(F32)
        upper = jnp.where(me_p < 31, 1.0, 0.0).astype(F32)
        for e in range(2):
            pool[17 + e] = flow[turn, e].astype(F32) * lower
            pool[19 + e] = fupp[turn, e].astype(F32) * upper

        @pl.loop(0, 4)
        def _(s):
            for side in range(4):
                ghost[kept, s, side] = pool[rcv_ref[s, side]]

    zed = lax.broadcasted_iota(jnp.int32, (8, 128), 0)

    def taps(src, s, cols):
        def plane(x):
            rows = pl.ds(pl.multiple_of(s * 512 + x * 64, 64), 64)
            return src[rows, cols].astype(F32).reshape(8, 8, 128)

        blank = jnp.zeros((1, 8, 128), F32)
        before = None
        here = plane(0)
        for x in range(8):
            after = plane(x + 1) if x < 7 else None
            y_low = jnp.concatenate([blank, here[:7]], axis=0)
            y_upp = jnp.concatenate([here[1:], blank], axis=0)
            yield x, (here, before, after, y_low, y_upp, pltpu.roll(here, 1, 1), pltpu.roll(here, 7, 1))
            before, here = here, after

    def tap_weights(b, cols, low, upp):
        w = [jnp.broadcast_to(dw_ref[i, b:b + 1, cols], (8, 128)) for i in range(7)]
        w[5] = jnp.where(zed == low, 0.0, w[5])
        w[6] = jnp.where(zed == upp, 0.0, w[6])
        return w

    def base_forward(b):
        for lane in range(2):
            cols = slice(lane * 128, lane * 128 + 128)
            w = tap_weights(b, cols, 0, 7)
            shift = jnp.broadcast_to(moment[:, cols], (8, 128))

            @pl.loop(0, 4)
            def _(s):
                for x, near in taps(field.at[b], s, cols):
                    total = shift[None]
                    for i in range(7):
                        if near[i] is not None:
                            total = total + w[i][None] * near[i]
                    rows = pl.ds(pl.multiple_of(s * 512 + x * 64, 64), 64)
                    base[rows, cols] = total.reshape(64, 128)

    def with_ghosts(kept, s, x, w):
        total = base[pl.ds(pl.multiple_of(s * 512 + x * 64, 64), 64), :]
        if x == 0:
            total = total + w[0] * ghost[kept, s, 0]
        if x == 7:
            total = total + w[1] * ghost[kept, s, 1]
        edge = slice(x * 8, x * 8 + 8)
        low = total[:8] + w[2] * ghost[kept, s, 2, edge]
        upp = total[56:] + w[3] * ghost[kept, s, 3, edge]
        return jnp.concatenate([low, total[8:56], upp], axis=0)

    def finish_forward(b):
        w = [dw_ref[i, b:b + 1, :] for i in (1, 2, 3, 4)]

        @pl.loop(0, 4)
        def _(s):
            for x in range(8):
                rows = pl.ds(pl.multiple_of(s * 512 + x * 64, 64), 64)
                act[b, rows, :] = with_ghosts(b, s, x, w).astype(BF)

    mirror = (0, 2, 1, 4, 3, 6, 5)

    def base_backward(b, products):
        dsums[...] = jnp.zeros((7, 8, 256), F32)

        @pl.loop(0, 2)
        def _(h):
            part = pl.ds(pl.multiple_of(h * 512, 512), 512)
            for kind, left, right in products:
                tile = dot(left[...], right[:, part])
                for j in range(2):
                    k1[b, kind, 2 * h + j] = tile[:, j * 256:j * 256 + 256].reshape(2, 128, 256)
                    s1[b, kind, 2 * h + j] = k1[b, kind, 2 * h + j, 1 - core].astype(BF)
            for lane in range(2):
                cols = slice(lane * 128, lane * 128 + 128)
                w = tap_weights(b, cols, 7, 0)
                sums = [dsums[i, :, cols] for i in range(7)]
                for t in range(2):
                    s = 2 * h + t
                    for x, near in taps(dact, s, cols):
                        rows = pl.ds(pl.multiple_of(s * 512 + x * 64, 64), 64)
                        total = grad[rows, cols].astype(F32).reshape(8, 8, 128)
                        value = field[b, rows, cols].astype(F32).reshape(8, 8, 128)
                        here = near[0]
                        for i in range(7):
                            if near[mirror[i]] is not None:
                                total = total + w[i][None] * near[mirror[i]]
                                sums[i] = sums[i] + jnp.sum(value * near[mirror[i]], axis=0)
                        if x == 0:
                            sums[1] = sums[1] + jnp.sum(ghost[b, s, 0, :, cols].reshape(8, 8, 128) * here, axis=0)
                        if x == 7:
                            sums[2] = sums[2] + jnp.sum(ghost[b, s, 1, :, cols].reshape(8, 8, 128) * here, axis=0)
                        sums[3] = sums[3] + ghost[b, s, 2, x * 8:x * 8 + 8, cols] * here[0]
                        sums[4] = sums[4] + ghost[b, s, 3, x * 8:x * 8 + 8, cols] * here[7]
                        base[rows, cols] = total.reshape(64, 128)
                for i in range(7):
                    dsums[i, :, cols] = sums[i]

        for kind, left, right in products:
            c1(b, kind).start()
        inside = lax.broadcasted_iota(jnp.int32, (8, 256), 0)
        for i in range(7):
            total = dsums[i]
            if i == 5:
                total = jnp.where(inside == 7, 0.0, total)
            if i == 6:
                total = jnp.where(inside == 0, 0.0, total)
            dacc[7 * b + i:7 * b + i + 1, :] = jnp.sum(total, axis=0, keepdims=True)

    def finish_backward(b, dst):
        w = [dw_ref[i, b:b + 1, :] for i in (2, 1, 4, 3)]

        @pl.loop(0, 4)
        def _(s):
            occ = occupied(s)
            for x in range(8):
                rows = pl.ds(pl.multiple_of(s * 512 + x * 64, 64), 64)
                dst[rows, :] = (with_ghosts(2, s, x, w) * occ).astype(BF)

    def c1(b, kind):
        return remote(s1.at[b, kind], r1.at[b, kind], c1s.at[b, kind], c1r.at[b, kind], twin)

    def weight_grad(b, kind, left, right):
        tile = dot(left[...], right[...])
        for j in range(4):
            k1[b, kind, j] = tile[:, j * 256:j * 256 + 256].reshape(2, 128, 256)
            s1[b, kind, j] = k1[b, kind, j, 1 - core].astype(BF)
        c1(b, kind).start()

    def wait_all(ref, send, recv):
        pltpu.make_async_copy(ref, ref, send).wait()
        pltpu.make_async_copy(ref, ref, recv).wait()

    def c2(b, kind, d):
        to = lax.rem(me_xy + d, 16)
        return remote(s2.at[b, kind, to], r2.at[b, kind, d - 1], c2s.at[b, kind], c2r.at[b, kind], along_xy(d))

    def step2(b, kind):
        c1(b, kind).wait()
        for j in range(4):
            total = k1[b, kind, j, core] + r1[b, kind, j].astype(F32)
            s2[b, kind, 4 * j:4 * j + 4] = total.reshape(4, 32, 256).astype(BF)

        @pl.loop(1, 16)
        def _(d):
            c2(b, kind, d).start()

    def c3(b, kind, d):
        return remote(
            r3.at[b, kind, me_z], r3.at[b, kind, me_z], c3s.at[b, kind, d - 1], c3r.at[b, kind, d - 1], along_z(d)
        )

    def step3(b, kind):
        wait_all(r2.at[b, kind], c2s.at[b, kind], c2r.at[b, kind])
        rows = pl.ds(pl.multiple_of(me_y * 32, 32), 32)
        total = k1[b, kind, me_x, core, rows] + r1[b, kind, me_x, rows].astype(F32)
        for d in range(15):
            total = total + r2[b, kind, d].astype(F32)
        r3[b, kind, me_z] = total.astype(BF)
        for d in (2, 1, 3):
            c3(b, kind, d).start()

    def c5(b, kind, i):
        peers = [twin] + [along_y(d, side) for d in (1, 2, 3) for side in (core, 1 - core)]
        return remote(
            r5.at[b, kind, core, me_y], r5.at[b, kind, core, me_y], c5s.at[b, kind, i], c5r.at[b, kind, i], peers[i]
        )

    def step5(b, kind):
        for d in (1, 2, 3):
            c3(b, kind, d).wait()
        total = r3[b, kind, 0].astype(F32)
        for z in range(1, 4):
            total = total + r3[b, kind, z].astype(F32)
        r5[b, kind, core, me_y] = total.astype(BF)
        for i in (3, 4, 1, 2, 5, 6, 0):
            c5(b, kind, i).start()

    def finish(b, kind):
        for i in range(7):
            c5(b, kind, i).wait()
        for side in range(2):
            at = slice(side * 128, side * 128 + 128)
            total = r5[b, kind, side].reshape(128, 256).astype(F32) * scale
            if kind:
                gup_ref[b, at, :] = total
            else:
                gdn_ref[b, :, at] = total.T

    def e1():
        return remote(ds.at[0], dr1, e_s.at[0], e_r.at[0], twin)

    def e2(d):
        return remote(ds.at[1], dr2.at[0, d - 1], e_s.at[d], e_r.at[d], along_xy(4 * d))

    def e3(d):
        return remote(ds.at[2], dr2.at[1, d - 1], e_s.at[3 + d], e_r.at[3 + d], along_z(d))

    def e4(d):
        return remote(ds.at[3], dr2.at[2, d - 1], e_s.at[6 + d], e_r.at[6 + d], along_y(d, core))

    def taps_start(stage, copy):
        ds[stage] = dacc[...].astype(BF)
        for d in (2, 1, 3):
            copy(d).start()

    def taps_take(stage, copy):
        for d in (1, 2, 3):
            copy(d).wait()
        dacc[...] = dacc[...] + dr2[stage - 1, 0].astype(F32) + dr2[stage - 1, 1].astype(F32) + dr2[stage - 1, 2].astype(F32)

    loads[0].wait()

    @pl.loop(0, 4)
    def _(s):
        field[0, rows_of(s), :] = (latv[rows_of(s), :].astype(F32) * occupied(s)).astype(BF)

    pool[0] = jnp.zeros((64, 256), F32)
    pool_faces(field.at[0])
    pl.semaphore_wait(barrier, 24)
    send_faces(0)
    loads[2].wait()
    table_row = lax.broadcasted_iota(jnp.int32, (1000, 256), 0)
    moment = jnp.sum(jnp.where(table_row == ts_ref[0], tt[...], 0.0), axis=0, keepdims=True)
    base_forward(0)
    loads[1].wait()
    loads[3].wait()
    for b in range(2):
        wut[b] = wu[b].T
        wdt[b] = wd[b].T
    loads[4].wait()

    @pl.loop(0, 4)
    def _(s):
        rows = rows_of(s)
        value = (cotv[rows, :].astype(F32) * occupied(s)).astype(BF)
        grad[rows, :] = value
        turn_g[:, rows] = value.T

    take_faces(0, 0)
    finish_forward(0)
    for n in range(4):
        part = slice(n * 256, n * 256 + 256)
        hid[0, :, part], slo[:, part] = gelu_pair(dot(act[0], wu[0, :, part]).astype(BF))
    for s in range(4):
        rows = slice(s * 512, s * 512 + 512)
        total = field[0, rows, :].astype(F32) + dot(hid[0, rows, :], wd[0])
        total = (total * occupied(s)).astype(BF)
        field[1, rows, :] = total
        pool_slot(s, total)
    send_faces(1)
    base_forward(1)
    for n in range(4):
        part = slice(n * 256, n * 256 + 256)
        dp[:, part] = dot(grad[...], wdt[1, :, part]).astype(BF)
    turn_a[0] = act[0].T
    take_faces(1, 1)
    finish_forward(1)

    turn_a[1] = act[1].T
    for n in range(4):
        part = slice(n * 256, n * 256 + 256)
        hidden, slope = gelu_pair(dot(act[1], wu[1, :, part]).astype(BF))
        hid[1, :, part] = hidden
        dp[:, part] = dp[:, part] * slope
    for s in range(4):
        rows = slice(s * 512, s * 512 + 512)
        total = dot(dp[rows, :], wut[1]).astype(BF)
        dact[rows, :] = total
        pool_slot(s, total)
    send_faces(2)
    weight_grad(1, 0, turn_g, hid.at[1])
    base_backward(1, ((1, turn_a.at[1], dp),))
    step2(1, 0)
    take_faces(2, 2)
    finish_backward(1, grad)
    step2(1, 1)

    turn_g[...] = grad[...].T
    weight_grad(0, 0, turn_g, hid.at[0])
    for n in range(4):
        part = slice(n * 256, n * 256 + 256)
        dp[:, part] = dot(grad[...], wdt[0, :, part]).astype(BF) * slo[:, part]
    step2(0, 0)
    weight_grad(0, 1, turn_a.at[0], dp)
    for s in range(4):
        rows = slice(s * 512, s * 512 + 512)
        total = dot(dp[rows, :], wut[0]).astype(BF)
        dact[rows, :] = total
        pool_slot(s, total)
    step2(0, 1)
    send_faces(3)
    step3(1, 0)
    step3(1, 1)
    dacc[14:16] = jnp.zeros((2, 256), F32)
    base_backward(0, ())
    ds[0] = dacc[...].astype(BF)
    e1().start()
    step3(0, 0)
    e1().wait()
    dacc[...] = dacc[...] + dr1[...].astype(F32)
    taps_start(1, e2)
    take_faces(3, 2)
    finish_backward(0, out_ref)
    step3(0, 1)
    step5(1, 0)
    step5(1, 1)
    step5(0, 0)
    taps_take(1, e2)
    taps_start(2, e3)
    step5(0, 1)
    taps_take(2, e3)
    taps_start(3, e4)
    finish(1, 0)
    finish(1, 1)
    finish(0, 0)
    taps_take(3, e4)
    dsum = dacc[...] * scale
    share = jnp.zeros((16, 64), F32)
    for j in range(4):
        share = jnp.where(me_x == j, dsum[:, j * 64:j * 64 + 64], share)
    for i in range(7):
        dep_ref[i, 0:1] = share[i:i + 1]
        dep_ref[i, 1:2] = share[7 + i:8 + i]
    finish(0, 1)


def store(*refs):
    sems = refs[8]
    copies = [pltpu.make_async_copy(refs[i], refs[4 + i], sems.at[i]) for i in range(4)]
    for copy in copies:
        copy.start()
    for copy in copies:
        copy.wait()


def on_device(latents, cotangent, w_up, w_down, depth_w, time_table, timesteps, brick_counts, send_list, recv_list):
    bricks, voxels, channels = latents.shape
    rows = bricks * voxels
    scale = 1.0 / math.sqrt(rows * lax.axis_size("rep") * lax.axis_size("space"))
    anywhere = pl.BlockSpec(memory_space=pl.ANY)
    vmem = pl.BlockSpec(memory_space=pltpu.VMEM)
    smem = pl.BlockSpec(memory_space=pltpu.SMEM)
    dma = pltpu.SemaphoreType.DMA
    results = pl.pallas_call(
        functools.partial(kernel, scale),
        out_shape=(
            pltpu.VMEM((rows, channels), BF),
            pltpu.VMEM((2, 256, 256), F32),
            pltpu.VMEM((2, 256, 256), F32),
            pltpu.VMEM((7, 2, 64), F32),
        ),
        in_specs=[anywhere] * 4 + [vmem, anywhere] + [smem] * 4,
        out_specs=(vmem, vmem, vmem, vmem),
        scratch_shapes=[
            pltpu.VMEM((rows, 256), BF),
            pltpu.VMEM((rows, 256), BF),
            pltpu.VMEM((2, 256, 1024), BF),
            pltpu.VMEM((2, 1024, 256), BF),
            pltpu.VMEM((1000, 256), F32),
            pltpu.VMEM((2, rows, 256), BF),
            pltpu.VMEM((2, rows, 256), BF),
            pltpu.VMEM((2, rows, 1024), BF),
            pltpu.VMEM((rows, 1024), BF),
            pltpu.VMEM((rows, 1024), BF),
            pltpu.VMEM((rows, 256), BF),
            pltpu.VMEM((256, rows), BF),
            pltpu.VMEM((2, 256, rows), BF),
            pltpu.VMEM((rows, 256), BF),
            pltpu.VMEM((21, 64, 256), F32),
            pltpu.VMEM((3, 4, 4, 64, 256), F32),
            pltpu.VMEM((rows, 256), F32),
            pltpu.VMEM((2, 1024, 256), BF),
            pltpu.VMEM((2, 256, 1024), BF),
            pltpu.VMEM((4, 2, 2, 64, 256), BF),
            pltpu.VMEM((4, 2, 64, 256), BF),
            pltpu.VMEM((4, 2, 64, 256), BF),
            pltpu.VMEM((2, 2, 4, 2, 128, 256), F32),
            pltpu.VMEM((2, 2, 4, 128, 256), BF),
            pltpu.VMEM((2, 2, 4, 128, 256), BF),
            pltpu.VMEM((2, 2, 16, 32, 256), BF),
            pltpu.VMEM((2, 2, 15, 32, 256), BF),
            pltpu.VMEM((2, 2, 4, 32, 256), BF),
            pltpu.VMEM((2, 2, 2, 4, 32, 256), BF),
            pltpu.VMEM((16, 256), F32),
            pltpu.VMEM((7, 8, 256), F32),
            pltpu.VMEM((4, 16, 256), BF),
            pltpu.VMEM((16, 256), BF),
            pltpu.VMEM((3, 3, 16, 256), BF),
            dma((5,)),
            dma((4, 2)),
            dma((4, 2)),
            dma((2, 2)),
            dma((2, 2)),
            dma((2, 2)),
            dma((2, 2)),
            dma((2, 2, 3)),
            dma((2, 2, 3)),
            dma((2, 2, 7)),
            dma((2, 2, 7)),
            dma((10,)),
            dma((10,)),
        ],
        compiler_params=pltpu.CompilerParams(
            collective_id=0, has_side_effects=True, vmem_limit_bytes=58 * 1024 * 1024
        ),
        name="blocks",
    )(
        latents.reshape(rows, channels),
        cotangent.reshape(rows, channels),
        w_up, w_down, depth_w.transpose(1, 0, 2), time_table, timesteps, brick_counts, send_list, recv_list,
    )
    out, up, down, depth = pl.pallas_call(
        store,
        out_shape=[jax.ShapeDtypeStruct(a.shape, a.dtype) for a in results],
        in_specs=[vmem] * 4,
        out_specs=[anywhere] * 4,
        scratch_shapes=[dma((4,))],
        name="store",
    )(*[pltpu.with_memory_space_constraint(a, pltpu.VMEM) for a in results])
    return out.reshape(latents.shape), up, down, depth.transpose(1, 0, 2)


def solution(mesh):
    spread = ("rep", "space")
    return jax.shard_map(
        on_device,
        mesh=mesh,
        in_specs=(
            P(spread, None, None),
            P(spread, None, None),
            P(), P(), P(), P(),
            P("rep"),
            P(spread),
            P(spread, None, None),
            P(spread, None),
        ),
        out_specs=(
            P(spread, None, None),
            P(None, None, "rep"),
            P(None, "rep", None),
            P(None, None, "rep"),
        ),
        check_vma=False,
    )
```

```python
import functools
import math

import jax
import jax.numpy as jnp
from jax import lax
from jax.experimental import pallas as pl
from jax.experimental.pallas import tpu as pltpu
from jax.sharding import PartitionSpec as P

MESH = pl.DeviceIdType.MESH
BF = jnp.bfloat16
F32 = jnp.float32
CUBIC = 0.044715
ROOT = math.sqrt(2.0 / math.pi)
LOG2E = math.log2(math.e)


def gelu_pair(u):
    square = u * u
    power = u * ((-2.0 * ROOT * LOG2E) + (-2.0 * ROOT * CUBIC * LOG2E) * square)
    e = jnp.exp2(jnp.minimum(power, 80.0))
    gate = 1.0 / (1.0 + e)
    hidden = u * gate
    slope = gate + hidden * (e * gate) * ((2.0 * ROOT) + (6.0 * ROOT * CUBIC) * square)
    return hidden, slope


def dot(a, b):
    return jnp.dot(a, b, preferred_element_type=F32)


def kernel(
    scale,
    lat_hbm, cot_hbm, wu_hbm, wd_hbm, dw_ref, tt_hbm, ts_ref, cnt_ref, snd_ref, rcv_ref,
    out_ref, gup_ref, gdn_ref, dep_ref,
    latv, cotv, wu, wd, tt, field, act, hid, slo, dp, dact, turn_g, turn_a, grad, pool, ghost, base, wut, wdt,
    fsend, flow, fupp, k1, s1, r1, s2, r2, r3, r5, dacc, dsums, ds, dr1, dr2,
    in_sem, fs_sem, fr_sem, c1s, c1r, c2s, c2r, c3s, c3r, c5s, c5r, e_s, e_r,
):
    me_x = lax.axis_index("rep")
    me_p = lax.axis_index("space")
    core = lax.rem(me_p, 2)
    twin = {"rep": me_x, "space": me_p + 1 - 2 * core}
    below = {"rep": me_x, "space": lax.rem(me_p + 31, 32)}
    above = {"rep": me_x, "space": lax.rem(me_p + 1, 32)}

    me_z = me_p // 8
    me_y = lax.rem(me_p // 2, 4)
    me_xy = me_x * 4 + me_y

    def along_xy(d):
        to = lax.rem(me_xy + d, 16)
        return {"rep": to // 4, "space": me_z * 8 + lax.rem(to, 4) * 2 + core}

    def along_z(d):
        return {"rep": me_x, "space": lax.rem(me_p + 8 * d, 32)}

    def along_y(d, side):
        return {"rep": me_x, "space": me_z * 8 + lax.rem(me_y + d, 4) * 2 + side}

    loads = [
        pltpu.make_async_copy(a, b, in_sem.at[i])
        for i, (a, b) in enumerate(
            ((lat_hbm, latv), (wu_hbm, wu), (tt_hbm, tt), (wd_hbm, wd), (cot_hbm, cotv))
        )
    ]
    loads[0].start()
    barrier = pltpu.get_barrier_semaphore()

    @pl.loop(1, 16)
    def _(d):
        pl.semaphore_signal(barrier, inc=1, device_id=along_xy(d), device_id_type=MESH)

    for peer in [along_z(d) for d in (2, 1, 3)] + [along_y(d, 1 - core) for d in (2, 1, 3)] + [above, below, twin]:
        pl.semaphore_signal(barrier, inc=1, device_id=peer, device_id_type=MESH)
    for copy in loads[1:]:
        copy.start()

    def occupied(s):
        return jnp.minimum(jnp.maximum(cnt_ref[0] - s, 0), 1).astype(F32)

    def spot(s, x):
        if x in (0, 7):
            return pl.ds(pl.multiple_of(s * 224 + (64 if x else 0), 16), 64), None
        return (
            pl.ds(pl.multiple_of(s * 224 + 112 + 16 * x, 16), 16),
            pl.ds(pl.multiple_of(s * 288 + 848 + 48 * x, 16), 48),
        )

    def load_plane(ref, s, x, cols):
        edge, inner = spot(s, x)
        value = ref[edge, cols].astype(F32)
        width = value.shape[1]
        if inner is None:
            return value.reshape(8, 8, width)
        value = value.reshape(2, 8, width)
        inside = ref[inner, cols].astype(F32).reshape(6, 8, width)
        return jnp.concatenate([value[:1], inside, value[1:]], axis=0)

    def store_plane(ref, s, x, value):
        edge, inner = spot(s, x)
        value = value.reshape(8, 8, 256)
        if inner is None:
            ref[edge, :] = value.reshape(64, 256).astype(BF)
            return
        ref[edge, :] = jnp.concatenate([value[:1], value[7:]], axis=0).reshape(16, 256).astype(BF)
        ref[inner, :] = value[1:7].reshape(48, 256).astype(BF)

    def natural(s, x):
        return pl.ds(pl.multiple_of(s * 512 + x * 64, 64), 64)

    def remote(src, dst, send, recv, peer):
        return pltpu.make_async_remote_copy(
            src_ref=src, dst_ref=dst, send_sem=send, recv_sem=recv, device_id=peer, device_id_type=MESH
        )

    def pool_slot(s, edge):
        v = edge.astype(F32)
        middle = [128 + 16 * x for x in range(6)]
        pool[1 + 4 * s] = v[0:64]
        pool[2 + 4 * s] = v[64:128]
        pool[3 + 4 * s] = jnp.concatenate([v[0:8]] + [v[r:r + 8] for r in middle] + [v[64:72]], axis=0)
        pool[4 + 4 * s] = jnp.concatenate([v[56:64]] + [v[r + 8:r + 16] for r in middle] + [v[120:128]], axis=0)

    def face_copies(turn):
        return (
            remote(fsend.at[turn, 1], flow.at[turn], fs_sem.at[turn, 1], fr_sem.at[turn, 1], above),
            remote(fsend.at[turn, 0], fupp.at[turn], fs_sem.at[turn, 0], fr_sem.at[turn, 0], below),
        )

    def send_faces(turn):
        for k in range(2):
            for e in range(2):
                fsend[turn, k, e] = pool[1 + snd_ref[0, k, e]].astype(BF)
        for copy in face_copies(turn):
            copy.start()

    def take_faces(turn, kept):
        for copy in face_copies(turn):
            copy.wait()
        lower = jnp.where(me_p > 0, 1.0, 0.0).astype(F32)
        upper = jnp.where(me_p < 31, 1.0, 0.0).astype(F32)
        for e in range(2):
            pool[17 + e] = flow[turn, e].astype(F32) * lower
            pool[19 + e] = fupp[turn, e].astype(F32) * upper

        @pl.loop(0, 4)
        def _(s):
            for side in range(4):
                ghost[kept, s, side] = pool[rcv_ref[s, side]]

    zed = lax.broadcasted_iota(jnp.int32, (8, 128), 0)

    def taps(src, s, cols):
        def plane(x):
            return load_plane(src, s, x, cols)

        blank = jnp.zeros((1, 8, 128), F32)
        before = None
        here = plane(0)
        for x in range(8):
            after = plane(x + 1) if x < 7 else None
            y_low = jnp.concatenate([blank, here[:7]], axis=0)
            y_upp = jnp.concatenate([here[1:], blank], axis=0)
            yield x, (here, before, after, y_low, y_upp, pltpu.roll(here, 1, 1), pltpu.roll(here, 7, 1))
            before, here = here, after

    def tap_weights(b, cols, low, upp):
        w = [jnp.broadcast_to(dw_ref[i, b:b + 1, cols], (8, 128)) for i in range(7)]
        w[5] = jnp.where(zed == low, 0.0, w[5])
        w[6] = jnp.where(zed == upp, 0.0, w[6])
        return w

    def base_forward(b):
        for lane in range(2):
            cols = slice(lane * 128, lane * 128 + 128)
            w = tap_weights(b, cols, 0, 7)
            shift = jnp.broadcast_to(moment[:, cols], (8, 128))

            @pl.loop(0, 4)
            def _(s):
                for x, near in taps(field.at[b], s, cols):
                    total = shift[None]
                    for i in range(7):
                        if near[i] is not None:
                            total = total + w[i][None] * near[i]
                    rows = pl.ds(pl.multiple_of(s * 512 + x * 64, 64), 64)
                    base[rows, cols] = total.reshape(64, 128)

    def with_ghosts(kept, s, x, w):
        total = base[pl.ds(pl.multiple_of(s * 512 + x * 64, 64), 64), :]
        if x == 0:
            total = total + w[0] * ghost[kept, s, 0]
        if x == 7:
            total = total + w[1] * ghost[kept, s, 1]
        edge = slice(x * 8, x * 8 + 8)
        low = total[:8] + w[2] * ghost[kept, s, 2, edge]
        upp = total[56:] + w[3] * ghost[kept, s, 3, edge]
        return jnp.concatenate([low, total[8:56], upp], axis=0)

    def finish_forward(b):
        w = [dw_ref[i, b:b + 1, :] for i in (1, 2, 3, 4)]

        @pl.loop(0, 4)
        def _(s):
            for x in range(8):
                store_plane(act.at[b], s, x, with_ghosts(b, s, x, w))

    mirror = (0, 2, 1, 4, 3, 6, 5)

    def base_backward(b, products):
        dsums[...] = jnp.zeros((7, 8, 256), F32)

        @pl.loop(0, 2)
        def _(h):
            part = pl.ds(pl.multiple_of(h * 512, 512), 512)
            for kind, left, right in products:
                tile = dot(left[...], right[:, part])
                for j in range(2):
                    k1[b, kind, 2 * h + j] = tile[:, j * 256:j * 256 + 256].reshape(2, 128, 256)
                    s1[b, kind, 2 * h + j] = k1[b, kind, 2 * h + j, 1 - core].astype(BF)
            for lane in range(2):
                cols = slice(lane * 128, lane * 128 + 128)
                w = tap_weights(b, cols, 7, 0)
                sums = [dsums[i, :, cols] for i in range(7)]
                for t in range(2):
                    s = 2 * h + t
                    for x, near in taps(dact, s, cols):
                        rows = pl.ds(pl.multiple_of(s * 512 + x * 64, 64), 64)
                        total = load_plane(grad, s, x, cols)
                        value = load_plane(field.at[b], s, x, cols)
                        here = near[0]
                        for i in range(7):
                            if near[mirror[i]] is not None:
                                total = total + w[i][None] * near[mirror[i]]
                                sums[i] = sums[i] + jnp.sum(value * near[mirror[i]], axis=0)
                        if x == 0:
                            sums[1] = sums[1] + jnp.sum(ghost[b, s, 0, :, cols].reshape(8, 8, 128) * here, axis=0)
                        if x == 7:
                            sums[2] = sums[2] + jnp.sum(ghost[b, s, 1, :, cols].reshape(8, 8, 128) * here, axis=0)
                        sums[3] = sums[3] + ghost[b, s, 2, x * 8:x * 8 + 8, cols] * here[0]
                        sums[4] = sums[4] + ghost[b, s, 3, x * 8:x * 8 + 8, cols] * here[7]
                        base[rows, cols] = total.reshape(64, 128)
                for i in range(7):
                    dsums[i, :, cols] = sums[i]

        for kind, left, right in products:
            c1(b, kind).start()
        inside = lax.broadcasted_iota(jnp.int32, (8, 256), 0)
        for i in range(7):
            total = dsums[i]
            if i == 5:
                total = jnp.where(inside == 7, 0.0, total)
            if i == 6:
                total = jnp.where(inside == 0, 0.0, total)
            dacc[7 * b + i:7 * b + i + 1, :] = jnp.sum(total, axis=0, keepdims=True)

    def finish_backward(b):
        w = [dw_ref[i, b:b + 1, :] for i in (2, 1, 4, 3)]

        @pl.loop(0, 4)
        def _(s):
            occ = occupied(s)
            for x in range(8):
                total = with_ghosts(2, s, x, w) * occ
                if b:
                    store_plane(grad, s, x, total)
                else:
                    out_ref[natural(s, x), :] = total.astype(BF)

    def c1(b, kind):
        return remote(s1.at[b, kind], r1.at[b, kind], c1s.at[b, kind], c1r.at[b, kind], twin)

    def weight_grad(b, kind, left, right):
        tile = dot(left[...], right[...])
        for j in range(4):
            k1[b, kind, j] = tile[:, j * 256:j * 256 + 256].reshape(2, 128, 256)
            s1[b, kind, j] = k1[b, kind, j, 1 - core].astype(BF)
        c1(b, kind).start()

    def wait_all(ref, send, recv):
        pltpu.make_async_copy(ref, ref, send).wait()
        pltpu.make_async_copy(ref, ref, recv).wait()

    def c2(b, kind, d):
        to = lax.rem(me_xy + d, 16)
        return remote(s2.at[b, kind, to], r2.at[b, kind, d - 1], c2s.at[b, kind], c2r.at[b, kind], along_xy(d))

    def step2(b, kind):
        c1(b, kind).wait()
        for j in range(4):
            total = k1[b, kind, j, core] + r1[b, kind, j].astype(F32)
            s2[b, kind, 4 * j:4 * j + 4] = total.reshape(4, 32, 256).astype(BF)

        @pl.loop(1, 16)
        def _(d):
            c2(b, kind, d).start()

    def c3(b, kind, d):
        return remote(
            r3.at[b, kind, me_z], r3.at[b, kind, me_z], c3s.at[b, kind, d - 1], c3r.at[b, kind, d - 1], along_z(d)
        )

    def step3(b, kind):
        wait_all(r2.at[b, kind], c2s.at[b, kind], c2r.at[b, kind])
        rows = pl.ds(pl.multiple_of(me_y * 32, 32), 32)
        total = k1[b, kind, me_x, core, rows] + r1[b, kind, me_x, rows].astype(F32)
        for d in range(15):
            total = total + r2[b, kind, d].astype(F32)
        r3[b, kind, me_z] = total.astype(BF)
        for d in (2, 1, 3):
            c3(b, kind, d).start()

    def c5(b, kind, i):
        peers = [twin] + [along_y(d, side) for d in (1, 2, 3) for side in (core, 1 - core)]
        return remote(
            r5.at[b, kind, core, me_y], r5.at[b, kind, core, me_y], c5s.at[b, kind, i], c5r.at[b, kind, i], peers[i]
        )

    def step5(b, kind):
        for d in (1, 2, 3):
            c3(b, kind, d).wait()
        total = r3[b, kind, 0].astype(F32)
        for z in range(1, 4):
            total = total + r3[b, kind, z].astype(F32)
        r5[b, kind, core, me_y] = total.astype(BF)
        for i in (3, 4, 1, 2, 5, 6, 0):
            c5(b, kind, i).start()

    def finish(b, kind):
        for i in range(7):
            c5(b, kind, i).wait()
        for side in range(2):
            at = slice(side * 128, side * 128 + 128)
            total = r5[b, kind, side].reshape(128, 256).astype(F32) * scale
            if kind:
                gup_ref[b, at, :] = total
            else:
                gdn_ref[b, :, at] = total.T

    def e1():
        return remote(ds.at[0], dr1, e_s.at[0], e_r.at[0], twin)

    def e2(d):
        return remote(ds.at[1], dr2.at[0, d - 1], e_s.at[d], e_r.at[d], along_xy(4 * d))

    def e3(d):
        return remote(ds.at[2], dr2.at[1, d - 1], e_s.at[3 + d], e_r.at[3 + d], along_z(d))

    def e4(d):
        return remote(ds.at[3], dr2.at[2, d - 1], e_s.at[6 + d], e_r.at[6 + d], along_y(d, core))

    def taps_start(stage, copy):
        ds[stage] = dacc[...].astype(BF)
        for d in (2, 1, 3):
            copy(d).start()

    def taps_take(stage, copy):
        for d in (1, 2, 3):
            copy(d).wait()
        dacc[...] = dacc[...] + dr2[stage - 1, 0].astype(F32) + dr2[stage - 1, 1].astype(F32) + dr2[stage - 1, 2].astype(F32)

    loads[0].wait()

    pool[0] = jnp.zeros((64, 256), F32)

    @pl.loop(0, 4)
    def _(s):
        occ = occupied(s)
        for x in range(8):
            plane = latv[natural(s, x), :].astype(F32) * occ
            store_plane(field.at[0], s, x, plane)
            if x == 0:
                pool[1 + 4 * s] = plane
            if x == 7:
                pool[2 + 4 * s] = plane
            pool[3 + 4 * s, x * 8:x * 8 + 8] = plane[:8]
            pool[4 + 4 * s, x * 8:x * 8 + 8] = plane[56:]

    pl.semaphore_wait(barrier, 24)
    send_faces(0)
    loads[2].wait()
    table_row = lax.broadcasted_iota(jnp.int32, (1000, 256), 0)
    moment = jnp.sum(jnp.where(table_row == ts_ref[0], tt[...], 0.0), axis=0, keepdims=True)
    base_forward(0)
    loads[1].wait()
    loads[3].wait()
    for b in range(2):
        wut[b] = wu[b].T
        wdt[b] = wd[b].T
    loads[4].wait()

    @pl.loop(0, 4)
    def _(s):
        occ = occupied(s)
        for x in range(8):
            store_plane(grad, s, x, cotv[natural(s, x), :].astype(F32) * occ)

    turn_g[...] = grad[...].T
    take_faces(0, 0)
    finish_forward(0)
    for first, size in ((0, 224), (896, 288)):
        group = slice(first, first + 4 * size)
        for n in range(4):
            part = slice(n * 256, n * 256 + 256)
            hid[0, group, part], slo[group, part] = gelu_pair(dot(act[0, group, :], wu[0, :, part]).astype(BF))
        for s in range(4):
            rows = slice(first + s * size, first + s * size + size)
            total = field[0, rows, :].astype(F32) + dot(hid[0, rows, :], wd[0])
            total = (total * occupied(s)).astype(BF)
            field[1, rows, :] = total
            if first == 0:
                pool_slot(s, total)
        if first == 0:
            send_faces(1)
    base_forward(1)
    for n in range(4):
        part = slice(n * 256, n * 256 + 256)
        dp[:, part] = dot(grad[...], wdt[1, :, part]).astype(BF)
    turn_a[0] = act[0].T
    take_faces(1, 1)
    finish_forward(1)

    turn_a[1] = act[1].T
    for n in range(4):
        part = slice(n * 256, n * 256 + 256)
        hidden, slope = gelu_pair(dot(act[1], wu[1, :, part]).astype(BF))
        hid[1, :, part] = hidden
        dp[:, part] = dp[:, part] * slope
    for s in range(4):
        rows = slice(s * 224, s * 224 + 224)
        total = dot(dp[rows, :], wut[1]).astype(BF)
        dact[rows, :] = total
        pool_slot(s, total)
    send_faces(2)
    dact[896:, :] = dot(dp[896:, :], wut[1]).astype(BF)
    weight_grad(1, 0, turn_g, hid.at[1])
    base_backward(1, ((1, turn_a.at[1], dp),))
    step2(1, 0)
    take_faces(2, 2)
    finish_backward(1)
    step2(1, 1)

    turn_g[...] = grad[...].T
    weight_grad(0, 0, turn_g, hid.at[0])
    for n in range(4):
        part = slice(n * 256, n * 256 + 256)
        dp[:, part] = dot(grad[...], wdt[0, :, part]).astype(BF) * slo[:, part]
    step2(0, 0)
    weight_grad(0, 1, turn_a.at[0], dp)
    for s in range(4):
        rows = slice(s * 224, s * 224 + 224)
        total = dot(dp[rows, :], wut[0]).astype(BF)
        dact[rows, :] = total
        pool_slot(s, total)
    send_faces(3)
    dact[896:, :] = dot(dp[896:, :], wut[0]).astype(BF)
    step2(0, 1)
    step3(1, 0)
    step3(1, 1)
    dacc[14:16] = jnp.zeros((2, 256), F32)
    base_backward(0, ())
    ds[0] = dacc[...].astype(BF)
    e1().start()
    step3(0, 0)
    e1().wait()
    dacc[...] = dacc[...] + dr1[...].astype(F32)
    taps_start(1, e2)
    take_faces(3, 2)
    finish_backward(0)
    step3(0, 1)
    step5(1, 0)
    step5(1, 1)
    step5(0, 0)
    taps_take(1, e2)
    taps_start(2, e3)
    step5(0, 1)
    taps_take(2, e3)
    taps_start(3, e4)
    finish(1, 0)
    finish(1, 1)
    finish(0, 0)
    taps_take(3, e4)
    dsum = dacc[...] * scale
    share = jnp.zeros((16, 64), F32)
    for j in range(4):
        share = jnp.where(me_x == j, dsum[:, j * 64:j * 64 + 64], share)
    for i in range(7):
        dep_ref[i, 0:1] = share[i:i + 1]
        dep_ref[i, 1:2] = share[7 + i:8 + i]
    finish(0, 1)


def store(*refs):
    sems = refs[8]
    copies = [pltpu.make_async_copy(refs[i], refs[4 + i], sems.at[i]) for i in range(4)]
    for copy in copies:
        copy.start()
    for copy in copies:
        copy.wait()


def on_device(latents, cotangent, w_up, w_down, depth_w, time_table, timesteps, brick_counts, send_list, recv_list):
    bricks, voxels, channels = latents.shape
    rows = bricks * voxels
    scale = 1.0 / math.sqrt(rows * lax.axis_size("rep") * lax.axis_size("space"))
    anywhere = pl.BlockSpec(memory_space=pl.ANY)
    vmem = pl.BlockSpec(memory_space=pltpu.VMEM)
    smem = pl.BlockSpec(memory_space=pltpu.SMEM)
    dma = pltpu.SemaphoreType.DMA
    results = pl.pallas_call(
        functools.partial(kernel, scale),
        out_shape=(
            pltpu.VMEM((rows, channels), BF),
            pltpu.VMEM((2, 256, 256), F32),
            pltpu.VMEM((2, 256, 256), F32),
            pltpu.VMEM((7, 2, 64), F32),
        ),
        in_specs=[anywhere] * 4 + [vmem, anywhere] + [smem] * 4,
        out_specs=(vmem, vmem, vmem, vmem),
        scratch_shapes=[
            pltpu.VMEM((rows, 256), BF),
            pltpu.VMEM((rows, 256), BF),
            pltpu.VMEM((2, 256, 1024), BF),
            pltpu.VMEM((2, 1024, 256), BF),
            pltpu.VMEM((1000, 256), F32),
            pltpu.VMEM((2, rows, 256), BF),
            pltpu.VMEM((2, rows, 256), BF),
            pltpu.VMEM((2, rows, 1024), BF),
            pltpu.VMEM((rows, 1024), BF),
            pltpu.VMEM((rows, 1024), BF),
            pltpu.VMEM((rows, 256), BF),
            pltpu.VMEM((256, rows), BF),
            pltpu.VMEM((2, 256, rows), BF),
            pltpu.VMEM((rows, 256), BF),
            pltpu.VMEM((21, 64, 256), F32),
            pltpu.VMEM((3, 4, 4, 64, 256), F32),
            pltpu.VMEM((rows, 256), F32),
            pltpu.VMEM((2, 1024, 256), BF),
            pltpu.VMEM((2, 256, 1024), BF),
            pltpu.VMEM((4, 2, 2, 64, 256), BF),
            pltpu.VMEM((4, 2, 64, 256), BF),
            pltpu.VMEM((4, 2, 64, 256), BF),
            pltpu.VMEM((2, 2, 4, 2, 128, 256), F32),
            pltpu.VMEM((2, 2, 4, 128, 256), BF),
            pltpu.VMEM((2, 2, 4, 128, 256), BF),
            pltpu.VMEM((2, 2, 16, 32, 256), BF),
            pltpu.VMEM((2, 2, 15, 32, 256), BF),
            pltpu.VMEM((2, 2, 4, 32, 256), BF),
            pltpu.VMEM((2, 2, 2, 4, 32, 256), BF),
            pltpu.VMEM((16, 256), F32),
            pltpu.VMEM((7, 8, 256), F32),
            pltpu.VMEM((4, 16, 256), BF),
            pltpu.VMEM((16, 256), BF),
            pltpu.VMEM((3, 3, 16, 256), BF),
            dma((5,)),
            dma((4, 2)),
            dma((4, 2)),
            dma((2, 2)),
            dma((2, 2)),
            dma((2, 2)),
            dma((2, 2)),
            dma((2, 2, 3)),
            dma((2, 2, 3)),
            dma((2, 2, 7)),
            dma((2, 2, 7)),
            dma((10,)),
            dma((10,)),
        ],
        compiler_params=pltpu.CompilerParams(
            collective_id=0, has_side_effects=True, vmem_limit_bytes=58 * 1024 * 1024
        ),
        name="blocks",
    )(
        latents.reshape(rows, channels),
        cotangent.reshape(rows, channels),
        w_up, w_down, depth_w.transpose(1, 0, 2), time_table, timesteps, brick_counts, send_list, recv_list,
    )
    out, up, down, depth = pl.pallas_call(
        store,
        out_shape=[jax.ShapeDtypeStruct(a.shape, a.dtype) for a in results],
        in_specs=[vmem] * 4,
        out_specs=[anywhere] * 4,
        scratch_shapes=[dma((4,))],
        name="store",
    )(*[pltpu.with_memory_space_constraint(a, pltpu.VMEM) for a in results])
    return out.reshape(latents.shape), up, down, depth.transpose(1, 0, 2)


def solution(mesh):
    spread = ("rep", "space")
    return jax.shard_map(
        on_device,
        mesh=mesh,
        in_specs=(
            P(spread, None, None),
            P(spread, None, None),
            P(), P(), P(), P(),
            P("rep"),
            P(spread),
            P(spread, None, None),
            P(spread, None),
        ),
        out_specs=(
            P(spread, None, None),
            P(None, None, "rep"),
            P(None, "rep", None),
            P(None, None, "rep"),
        ),
        check_vma=False,
    )
```

```python
import functools
import math

import jax
import jax.numpy as jnp
from jax import lax
from jax.experimental import pallas as pl
from jax.experimental.pallas import tpu as pltpu
from jax.sharding import PartitionSpec as P

MESH = pl.DeviceIdType.MESH
BF = jnp.bfloat16
F32 = jnp.float32
CUBIC = 0.044715
ROOT = math.sqrt(2.0 / math.pi)
LOG2E = math.log2(math.e)


def gelu_pair(u):
    square = u * u
    power = u * ((-2.0 * ROOT * LOG2E) + (-2.0 * ROOT * CUBIC * LOG2E) * square)
    e = jnp.exp2(jnp.minimum(power, 80.0))
    gate = 1.0 / (1.0 + e)
    hidden = u * gate
    slope = gate + hidden * (e * gate) * ((2.0 * ROOT) + (6.0 * ROOT * CUBIC) * square)
    return hidden, slope


def dot(a, b):
    return jnp.dot(a, b, preferred_element_type=F32)


def kernel(
    scale,
    lat_hbm, cot_hbm, wu_hbm, wd_hbm, dw_ref, tt_hbm, ts_ref, cnt_ref, snd_ref, rcv_ref,
    out_ref, gup_ref, gdn_ref, dep_ref,
    latv, cotv, wu, wd, tt, field, act, hid, slo, dp, dact, turn_g, turn_a, grad, pool, ghost, base, wut, wdt,
    fsend, flow, fupp, k1, s1, r1, s2, r2, r3, r5, dacc, dsums, ds, dr1, dr2,
    in_sem, fs_sem, fr_sem, c1s, c1r, c2s, c2r, c3s, c3r, c5s, c5r, e_s, e_r,
):
    me_x = lax.axis_index("rep")
    me_p = lax.axis_index("space")
    core = lax.rem(me_p, 2)
    twin = {"rep": me_x, "space": me_p + 1 - 2 * core}
    below = {"rep": me_x, "space": lax.rem(me_p + 31, 32)}
    above = {"rep": me_x, "space": lax.rem(me_p + 1, 32)}

    me_z = me_p // 8
    me_y = lax.rem(me_p // 2, 4)
    me_xy = me_x * 4 + me_y

    def along_xy(d):
        to = lax.rem(me_xy + d, 16)
        return {"rep": to // 4, "space": me_z * 8 + lax.rem(to, 4) * 2 + core}

    def along_z(d):
        return {"rep": me_x, "space": lax.rem(me_p + 8 * d, 32)}

    def along_y(d, side):
        return {"rep": me_x, "space": me_z * 8 + lax.rem(me_y + d, 4) * 2 + side}

    loads = [
        pltpu.make_async_copy(a, b, in_sem.at[i])
        for i, (a, b) in enumerate(
            ((lat_hbm, latv), (wu_hbm, wu), (tt_hbm, tt), (wd_hbm, wd), (cot_hbm, cotv))
        )
    ]
    loads[0].start()
    barrier = pltpu.get_barrier_semaphore()

    @pl.loop(1, 16)
    def _(d):
        pl.semaphore_signal(barrier, inc=1, device_id=along_xy(d), device_id_type=MESH)

    for peer in [along_z(d) for d in (2, 1, 3)] + [along_y(d, 1 - core) for d in (2, 1, 3)] + [above, below, twin]:
        pl.semaphore_signal(barrier, inc=1, device_id=peer, device_id_type=MESH)
    for copy in loads[1:]:
        copy.start()

    def occupied(s):
        return jnp.minimum(jnp.maximum(cnt_ref[0] - s, 0), 1).astype(F32)

    def spot(s, x):
        if x in (0, 7):
            return pl.ds(pl.multiple_of(s * 224 + (64 if x else 0), 16), 64), None
        return (
            pl.ds(pl.multiple_of(s * 224 + 112 + 16 * x, 16), 16),
            pl.ds(pl.multiple_of(s * 288 + 848 + 48 * x, 16), 48),
        )

    def load_plane(ref, s, x, cols):
        edge, inner = spot(s, x)
        value = ref[edge, cols].astype(F32)
        width = value.shape[1]
        if inner is None:
            return value.reshape(8, 8, width)
        value = value.reshape(2, 8, width)
        inside = ref[inner, cols].astype(F32).reshape(6, 8, width)
        return jnp.concatenate([value[:1], inside, value[1:]], axis=0)

    def store_plane(ref, s, x, value):
        edge, inner = spot(s, x)
        value = value.reshape(8, 8, 256)
        if inner is None:
            ref[edge, :] = value.reshape(64, 256).astype(BF)
            return
        ref[edge, :] = jnp.concatenate([value[:1], value[7:]], axis=0).reshape(16, 256).astype(BF)
        ref[inner, :] = value[1:7].reshape(48, 256).astype(BF)

    def natural(s, x):
        return pl.ds(pl.multiple_of(s * 512 + x * 64, 64), 64)

    def remote(src, dst, send, recv, peer):
        return pltpu.make_async_remote_copy(
            src_ref=src, dst_ref=dst, send_sem=send, recv_sem=recv, device_id=peer, device_id_type=MESH
        )

    def pool_slot(s, edge):
        v = edge.astype(F32)
        middle = [128 + 16 * x for x in range(6)]
        pool[1 + 4 * s] = v[0:64]
        pool[2 + 4 * s] = v[64:128]
        pool[3 + 4 * s] = jnp.concatenate([v[0:8]] + [v[r:r + 8] for r in middle] + [v[64:72]], axis=0)
        pool[4 + 4 * s] = jnp.concatenate([v[56:64]] + [v[r + 8:r + 16] for r in middle] + [v[120:128]], axis=0)

    def face_copies(turn):
        return (
            remote(fsend.at[turn, 1], flow.at[turn], fs_sem.at[turn, 1], fr_sem.at[turn, 1], above),
            remote(fsend.at[turn, 0], fupp.at[turn], fs_sem.at[turn, 0], fr_sem.at[turn, 0], below),
        )

    def send_faces(turn):
        for k in range(2):
            for e in range(2):
                fsend[turn, k, e] = pool[1 + snd_ref[0, k, e]].astype(BF)
        for copy in face_copies(turn):
            copy.start()

    def take_faces(turn):
        for copy in face_copies(turn):
            copy.wait()
        lower = jnp.where(me_p > 0, 1.0, 0.0).astype(F32)
        upper = jnp.where(me_p < 31, 1.0, 0.0).astype(F32)
        for e in range(2):
            pool[17 + e] = flow[turn, e].astype(F32) * lower
            pool[19 + e] = fupp[turn, e].astype(F32) * upper

    zed = lax.broadcasted_iota(jnp.int32, (8, 128), 0)

    def taps(src, s, cols):
        def plane(x):
            return load_plane(src, s, x, cols)

        blank = jnp.zeros((1, 8, 128), F32)
        before = None
        here = plane(0)
        for x in range(8):
            after = plane(x + 1) if x < 7 else None
            y_low = jnp.concatenate([blank, here[:7]], axis=0)
            y_upp = jnp.concatenate([here[1:], blank], axis=0)
            yield x, (here, before, after, y_low, y_upp, pltpu.roll(here, 1, 1), pltpu.roll(here, 7, 1))
            before, here = here, after

    def tap_weights(b, cols, low, upp):
        w = [jnp.broadcast_to(dw_ref[i, b:b + 1, cols], (8, 128)) for i in range(7)]
        w[5] = jnp.where(zed == low, 0.0, w[5])
        w[6] = jnp.where(zed == upp, 0.0, w[6])
        return w

    def base_forward(b):
        for lane in range(2):
            cols = slice(lane * 128, lane * 128 + 128)
            w = tap_weights(b, cols, 0, 7)
            shift = jnp.broadcast_to(moment[:, cols], (8, 128))

            @pl.loop(0, 4)
            def _(s):
                for x, near in taps(field.at[b], s, cols):
                    total = shift[None]
                    for i in range(7):
                        if near[i] is not None:
                            total = total + w[i][None] * near[i]
                    rows = pl.ds(pl.multiple_of(s * 512 + x * 64, 64), 64)
                    base[rows, cols] = total.reshape(64, 128)

    def with_ghosts(sides, s, x, w):
        total = base[pl.ds(pl.multiple_of(s * 512 + x * 64, 64), 64), :]
        if x == 0:
            total = total + w[0] * sides[0]
        if x == 7:
            total = total + w[1] * sides[1]
        edge = slice(x * 8, x * 8 + 8)
        low = total[:8] + w[2] * sides[2][edge]
        upp = total[56:] + w[3] * sides[3][edge]
        return jnp.concatenate([low, total[8:56], upp], axis=0)

    def finish_forward(b):
        w = [dw_ref[i, b:b + 1, :] for i in (1, 2, 3, 4)]

        @pl.loop(0, 4)
        def _(s):
            sides = [pool[rcv_ref[s, side]] for side in range(4)]
            for side in range(4):
                ghost[b, s, side] = sides[side]
            for x in range(8):
                store_plane(act.at[b], s, x, with_ghosts(sides, s, x, w))

    mirror = (0, 2, 1, 4, 3, 6, 5)

    def base_backward(b, products):
        dsums[...] = jnp.zeros((7, 8, 256), F32)

        @pl.loop(0, 2)
        def _(h):
            part = pl.ds(pl.multiple_of(h * 512, 512), 512)
            for kind, left, right in products:
                tile = dot(left[...], right[:, part])
                for j in range(2):
                    k1[b, kind, 2 * h + j] = tile[:, j * 256:j * 256 + 256].reshape(2, 128, 256)
                    s1[b, kind, 2 * h + j] = k1[b, kind, 2 * h + j, 1 - core].astype(BF)
            for lane in range(2):
                cols = slice(lane * 128, lane * 128 + 128)
                w = tap_weights(b, cols, 7, 0)
                sums = [dsums[i, :, cols] for i in range(7)]
                for t in range(2):
                    s = 2 * h + t
                    for x, near in taps(dact, s, cols):
                        rows = pl.ds(pl.multiple_of(s * 512 + x * 64, 64), 64)
                        total = load_plane(grad, s, x, cols)
                        value = load_plane(field.at[b], s, x, cols)
                        here = near[0]
                        for i in range(7):
                            if near[mirror[i]] is not None:
                                total = total + w[i][None] * near[mirror[i]]
                                sums[i] = sums[i] + jnp.sum(value * near[mirror[i]], axis=0)
                        if x == 0:
                            sums[1] = sums[1] + jnp.sum(ghost[b, s, 0, :, cols].reshape(8, 8, 128) * here, axis=0)
                        if x == 7:
                            sums[2] = sums[2] + jnp.sum(ghost[b, s, 1, :, cols].reshape(8, 8, 128) * here, axis=0)
                        sums[3] = sums[3] + ghost[b, s, 2, x * 8:x * 8 + 8, cols] * here[0]
                        sums[4] = sums[4] + ghost[b, s, 3, x * 8:x * 8 + 8, cols] * here[7]
                        base[rows, cols] = total.reshape(64, 128)
                for i in range(7):
                    dsums[i, :, cols] = sums[i]

        for kind, left, right in products:
            c1(b, kind).start()
        inside = lax.broadcasted_iota(jnp.int32, (8, 256), 0)
        for i in range(7):
            total = dsums[i]
            if i == 5:
                total = jnp.where(inside == 7, 0.0, total)
            if i == 6:
                total = jnp.where(inside == 0, 0.0, total)
            dacc[7 * b + i:7 * b + i + 1, :] = jnp.sum(total, axis=0, keepdims=True)

    def finish_backward(b):
        w = [dw_ref[i, b:b + 1, :] for i in (2, 1, 4, 3)]

        @pl.loop(0, 4)
        def _(s):
            occ = occupied(s)
            sides = [pool[rcv_ref[s, side]] for side in range(4)]
            for x in range(8):
                total = with_ghosts(sides, s, x, w) * occ
                if b:
                    store_plane(grad, s, x, total)
                else:
                    out_ref[natural(s, x), :] = total.astype(BF)

    def c1(b, kind):
        return remote(s1.at[b, kind], r1.at[b, kind], c1s.at[b, kind], c1r.at[b, kind], twin)

    def weight_grad(b, kind, left, right):
        tile = dot(left[...], right[...])
        for j in range(4):
            k1[b, kind, j] = tile[:, j * 256:j * 256 + 256].reshape(2, 128, 256)
            s1[b, kind, j] = k1[b, kind, j, 1 - core].astype(BF)
        c1(b, kind).start()

    def wait_all(ref, send, recv):
        pltpu.make_async_copy(ref, ref, send).wait()
        pltpu.make_async_copy(ref, ref, recv).wait()

    def c2(b, kind, dx, dy):
        x, y = lax.rem(me_x + dx, 4), lax.rem(me_y + dy, 4)
        peer = {"rep": x, "space": me_z * 8 + y * 2 + core}
        return remote(
            s2.at[b, kind, x * 4 + y], r2.at[b, kind, dx * 4 + dy - 1], c2s.at[b, kind], c2r.at[b, kind], peer
        )

    def step2(b, kind):
        c1(b, kind).wait()
        for j in range(4):
            total = k1[b, kind, j, core] + r1[b, kind, j].astype(F32)
            s2[b, kind, 4 * j:4 * j + 4] = total.reshape(4, 32, 256).astype(BF)

        for dx, dy in ((2, 2), (2, 1), (1, 2), (2, 3), (3, 2), (1, 1), (1, 3), (3, 1), (3, 3)):
            c2(b, kind, dx, dy).start()
        for dx, dy in ((2, 0), (0, 2), (1, 0), (0, 1), (3, 0), (0, 3)):
            c2(b, kind, dx, dy).start()

    def c3(b, kind, d):
        return remote(
            r3.at[b, kind, me_z], r3.at[b, kind, me_z], c3s.at[b, kind, d - 1], c3r.at[b, kind, d - 1], along_z(d)
        )

    def step3(b, kind):
        wait_all(r2.at[b, kind], c2s.at[b, kind], c2r.at[b, kind])
        rows = pl.ds(pl.multiple_of(me_y * 32, 32), 32)
        total = k1[b, kind, me_x, core, rows] + r1[b, kind, me_x, rows].astype(F32)
        for d in range(15):
            total = total + r2[b, kind, d].astype(F32)
        r3[b, kind, me_z] = total.astype(BF)
        for d in (2, 1, 3):
            c3(b, kind, d).start()

    def c5(b, kind, i):
        peers = [twin] + [along_y(d, side) for d in (1, 2, 3) for side in (core, 1 - core)]
        return remote(
            r5.at[b, kind, core, me_y], r5.at[b, kind, core, me_y], c5s.at[b, kind, i], c5r.at[b, kind, i], peers[i]
        )

    def step5(b, kind):
        for d in (1, 2, 3):
            c3(b, kind, d).wait()
        total = r3[b, kind, 0].astype(F32)
        for z in range(1, 4):
            total = total + r3[b, kind, z].astype(F32)
        r5[b, kind, core, me_y] = total.astype(BF)
        for i in (3, 4, 1, 2, 5, 6, 0):
            c5(b, kind, i).start()

    def finish(b, kind):
        for i in range(7):
            c5(b, kind, i).wait()
        for side in range(2):
            at = slice(side * 128, side * 128 + 128)
            total = r5[b, kind, side].reshape(128, 256).astype(F32) * scale
            if kind:
                gup_ref[b, at, :] = total
            else:
                gdn_ref[b, :, at] = total.T

    def e1():
        return remote(ds.at[0], dr1, e_s.at[0], e_r.at[0], twin)

    def e2(d):
        return remote(ds.at[1], dr2.at[0, d - 1], e_s.at[d], e_r.at[d], along_xy(4 * d))

    def e3(d):
        return remote(ds.at[2], dr2.at[1, d - 1], e_s.at[3 + d], e_r.at[3 + d], along_z(d))

    def e4(d):
        return remote(ds.at[3], dr2.at[2, d - 1], e_s.at[6 + d], e_r.at[6 + d], along_y(d, core))

    def taps_start(stage, copy):
        ds[stage] = dacc[...].astype(BF)
        for d in (2, 1, 3):
            copy(d).start()

    def taps_take(stage, copy):
        for d in (1, 2, 3):
            copy(d).wait()
        dacc[...] = dacc[...] + dr2[stage - 1, 0].astype(F32) + dr2[stage - 1, 1].astype(F32) + dr2[stage - 1, 2].astype(F32)

    loads[0].wait()

    pool[0] = jnp.zeros((64, 256), F32)

    @pl.loop(0, 4)
    def _(s):
        occ = occupied(s)
        for x in range(8):
            plane = latv[natural(s, x), :].astype(F32) * occ
            store_plane(field.at[0], s, x, plane)
            if x == 0:
                pool[1 + 4 * s] = plane
            if x == 7:
                pool[2 + 4 * s] = plane
            pool[3 + 4 * s, x * 8:x * 8 + 8] = plane[:8]
            pool[4 + 4 * s, x * 8:x * 8 + 8] = plane[56:]

    pl.semaphore_wait(barrier, 24)
    send_faces(0)
    loads[2].wait()
    table_row = lax.broadcasted_iota(jnp.int32, (1000, 256), 0)
    moment = jnp.sum(jnp.where(table_row == ts_ref[0], tt[...], 0.0), axis=0, keepdims=True)
    base_forward(0)
    loads[1].wait()
    loads[3].wait()
    for b in range(2):
        wut[b] = wu[b].T
        wdt[b] = wd[b].T
    loads[4].wait()

    @pl.loop(0, 4)
    def _(s):
        occ = occupied(s)
        for x in range(8):
            store_plane(grad, s, x, cotv[natural(s, x), :].astype(F32) * occ)

    turn_g[...] = grad[...].T
    for n in range(4):
        part = slice(n * 256, n * 256 + 256)
        dp[:, part] = dot(grad[...], wdt[1, :, part]).astype(BF)
    take_faces(0)
    finish_forward(0)
    for first, size in ((0, 224), (896, 288)):
        group = slice(first, first + 4 * size)
        for n in range(4):
            part = slice(n * 256, n * 256 + 256)
            hid[0, group, part], slo[group, part] = gelu_pair(dot(act[0, group, :], wu[0, :, part]).astype(BF))
        for s in range(4):
            rows = slice(first + s * size, first + s * size + size)
            total = field[0, rows, :].astype(F32) + dot(hid[0, rows, :], wd[0])
            total = (total * occupied(s)).astype(BF)
            field[1, rows, :] = total
            if first == 0:
                pool_slot(s, total)
        if first == 0:
            send_faces(1)
    base_forward(1)
    turn_a[0] = act[0].T
    take_faces(1)
    finish_forward(1)

    turn_a[1] = act[1].T
    for n in range(4):
        part = slice(n * 256, n * 256 + 256)
        hidden, slope = gelu_pair(dot(act[1], wu[1, :, part]).astype(BF))
        hid[1, :, part] = hidden
        dp[:, part] = dp[:, part] * slope
    for s in range(4):
        rows = slice(s * 224, s * 224 + 224)
        total = dot(dp[rows, :], wut[1]).astype(BF)
        dact[rows, :] = total
        pool_slot(s, total)
    send_faces(2)
    dact[896:, :] = dot(dp[896:, :], wut[1]).astype(BF)
    weight_grad(1, 0, turn_g, hid.at[1])
    base_backward(1, ((1, turn_a.at[1], dp),))
    step2(1, 0)
    take_faces(2)
    finish_backward(1)
    step2(1, 1)

    turn_g[...] = grad[...].T
    weight_grad(0, 0, turn_g, hid.at[0])
    for n in range(4):
        part = slice(n * 256, n * 256 + 256)
        dp[:, part] = dot(grad[...], wdt[0, :, part]).astype(BF) * slo[:, part]
    step2(0, 0)
    weight_grad(0, 1, turn_a.at[0], dp)
    for s in range(4):
        rows = slice(s * 224, s * 224 + 224)
        total = dot(dp[rows, :], wut[0]).astype(BF)
        dact[rows, :] = total
        pool_slot(s, total)
    send_faces(3)
    dact[896:, :] = dot(dp[896:, :], wut[0]).astype(BF)
    step2(0, 1)
    step3(1, 0)
    step3(1, 1)
    dacc[14:16] = jnp.zeros((2, 256), F32)
    base_backward(0, ())
    ds[0] = dacc[...].astype(BF)
    e1().start()
    step3(0, 0)
    e1().wait()
    dacc[...] = dacc[...] + dr1[...].astype(F32)
    taps_start(1, e2)
    take_faces(3)
    finish_backward(0)
    step3(0, 1)
    step5(1, 0)
    step5(1, 1)
    step5(0, 0)
    taps_take(1, e2)
    taps_start(2, e3)
    step5(0, 1)
    taps_take(2, e3)
    taps_start(3, e4)
    finish(1, 0)
    finish(1, 1)
    finish(0, 0)
    taps_take(3, e4)
    dsum = dacc[...] * scale
    share = jnp.zeros((16, 64), F32)
    for j in range(4):
        share = jnp.where(me_x == j, dsum[:, j * 64:j * 64 + 64], share)
    for i in range(7):
        dep_ref[i, 0:1] = share[i:i + 1]
        dep_ref[i, 1:2] = share[7 + i:8 + i]
    finish(0, 1)


def store(*refs):
    sems = refs[8]
    copies = [pltpu.make_async_copy(refs[i], refs[4 + i], sems.at[i]) for i in range(4)]
    for copy in copies:
        copy.start()
    for copy in copies:
        copy.wait()


def on_device(latents, cotangent, w_up, w_down, depth_w, time_table, timesteps, brick_counts, send_list, recv_list):
    bricks, voxels, channels = latents.shape
    rows = bricks * voxels
    scale = 1.0 / math.sqrt(rows * lax.axis_size("rep") * lax.axis_size("space"))
    anywhere = pl.BlockSpec(memory_space=pl.ANY)
    vmem = pl.BlockSpec(memory_space=pltpu.VMEM)
    smem = pl.BlockSpec(memory_space=pltpu.SMEM)
    dma = pltpu.SemaphoreType.DMA
    results = pl.pallas_call(
        functools.partial(kernel, scale),
        out_shape=(
            pltpu.VMEM((rows, channels), BF),
            pltpu.VMEM((2, 256, 256), F32),
            pltpu.VMEM((2, 256, 256), F32),
            pltpu.VMEM((7, 2, 64), F32),
        ),
        in_specs=[anywhere] * 4 + [vmem, anywhere] + [smem] * 4,
        out_specs=(vmem, vmem, vmem, vmem),
        scratch_shapes=[
            pltpu.VMEM((rows, 256), BF),
            pltpu.VMEM((rows, 256), BF),
            pltpu.VMEM((2, 256, 1024), BF),
            pltpu.VMEM((2, 1024, 256), BF),
            pltpu.VMEM((1000, 256), F32),
            pltpu.VMEM((2, rows, 256), BF),
            pltpu.VMEM((2, rows, 256), BF),
            pltpu.VMEM((2, rows, 1024), BF),
            pltpu.VMEM((rows, 1024), BF),
            pltpu.VMEM((rows, 1024), BF),
            pltpu.VMEM((rows, 256), BF),
            pltpu.VMEM((256, rows), BF),
            pltpu.VMEM((2, 256, rows), BF),
            pltpu.VMEM((rows, 256), BF),
            pltpu.VMEM((21, 64, 256), F32),
            pltpu.VMEM((2, 4, 4, 64, 256), F32),
            pltpu.VMEM((rows, 256), F32),
            pltpu.VMEM((2, 1024, 256), BF),
            pltpu.VMEM((2, 256, 1024), BF),
            pltpu.VMEM((4, 2, 2, 64, 256), BF),
            pltpu.VMEM((4, 2, 64, 256), BF),
            pltpu.VMEM((4, 2, 64, 256), BF),
            pltpu.VMEM((2, 2, 4, 2, 128, 256), F32),
            pltpu.VMEM((2, 2, 4, 128, 256), BF),
            pltpu.VMEM((2, 2, 4, 128, 256), BF),
            pltpu.VMEM((2, 2, 16, 32, 256), BF),
            pltpu.VMEM((2, 2, 15, 32, 256), BF),
            pltpu.VMEM((2, 2, 4, 32, 256), BF),
            pltpu.VMEM((2, 2, 2, 4, 32, 256), BF),
            pltpu.VMEM((16, 256), F32),
            pltpu.VMEM((7, 8, 256), F32),
            pltpu.VMEM((4, 16, 256), BF),
            pltpu.VMEM((16, 256), BF),
            pltpu.VMEM((3, 3, 16, 256), BF),
            dma((5,)),
            dma((4, 2)),
            dma((4, 2)),
            dma((2, 2)),
            dma((2, 2)),
            dma((2, 2)),
            dma((2, 2)),
            dma((2, 2, 3)),
            dma((2, 2, 3)),
            dma((2, 2, 7)),
            dma((2, 2, 7)),
            dma((10,)),
            dma((10,)),
        ],
        compiler_params=pltpu.CompilerParams(
            collective_id=0, has_side_effects=True, vmem_limit_bytes=58 * 1024 * 1024
        ),
        name="blocks",
    )(
        latents.reshape(rows, channels),
        cotangent.reshape(rows, channels),
        w_up, w_down, depth_w.transpose(1, 0, 2), time_table, timesteps, brick_counts, send_list, recv_list,
    )
    out, up, down, depth = pl.pallas_call(
        store,
        out_shape=[jax.ShapeDtypeStruct(a.shape, a.dtype) for a in results],
        in_specs=[vmem] * 4,
        out_specs=[anywhere] * 4,
        scratch_shapes=[dma((4,))],
        name="store",
    )(*[pltpu.with_memory_space_constraint(a, pltpu.VMEM) for a in results])
    return out.reshape(latents.shape), up, down, depth.transpose(1, 0, 2)


def solution(mesh):
    spread = ("rep", "space")
    return jax.shard_map(
        on_device,
        mesh=mesh,
        in_specs=(
            P(spread, None, None),
            P(spread, None, None),
            P(), P(), P(), P(),
            P("rep"),
            P(spread),
            P(spread, None, None),
            P(spread, None),
        ),
        out_specs=(
            P(spread, None, None),
            P(None, None, "rep"),
            P(None, "rep", None),
            P(None, None, "rep"),
        ),
        check_vma=False,
    )
```

```python
import functools
import math

import jax
import jax.numpy as jnp
from jax import lax
from jax.experimental import pallas as pl
from jax.experimental.pallas import tpu as pltpu
from jax.sharding import PartitionSpec as P

MESH = pl.DeviceIdType.MESH
FAR_FIRST = (
    (2, 2), (2, 1), (1, 2), (2, 3), (3, 2), (1, 1), (1, 3), (3, 1), (3, 3), (2, 0), (0, 2), (1, 0), (0, 1), (3, 0), (0, 3),
)
BF = jnp.bfloat16
F32 = jnp.float32
CUBIC = 0.044715
ROOT = math.sqrt(2.0 / math.pi)
LOG2E = math.log2(math.e)


def gelu_pair(u):
    square = u * u
    power = u * ((-2.0 * ROOT * LOG2E) + (-2.0 * ROOT * CUBIC * LOG2E) * square)
    e = jnp.exp2(jnp.minimum(power, 80.0))
    gate = 1.0 / (1.0 + e)
    hidden = u * gate
    slope = gate + hidden * (e * gate) * ((2.0 * ROOT) + (6.0 * ROOT * CUBIC) * square)
    return hidden, slope


def dot(a, b):
    return jnp.dot(a, b, preferred_element_type=F32)


def kernel(
    scale,
    lat_hbm, cot_hbm, wu_hbm, wd_hbm, dw_ref, tt_hbm, ts_ref, cnt_ref, snd_ref, rcv_ref,
    out_ref, gup_ref, gdn_ref, dep_ref,
    latv, cotv, wu, wd, tt, field, act, hid, slo, dp, dact, turn_g, turn_a, grad, pool, ghost, base, wut, wdt,
    fsend, flow, fupp, k1, s1, r1, s2, r2, r3, r5, dacc, dsums, ds, dr1, dr2,
    in_sem, fs_sem, fr_sem, c1s, c1r, c2s, c2r, c3s, c3r, c5s, c5r, e_s, e_r,
):
    me_x = lax.axis_index("rep")
    me_p = lax.axis_index("space")
    core = lax.rem(me_p, 2)
    twin = {"rep": me_x, "space": me_p + 1 - 2 * core}
    below = {"rep": me_x, "space": lax.rem(me_p + 31, 32)}
    above = {"rep": me_x, "space": lax.rem(me_p + 1, 32)}

    me_z = me_p // 8
    me_y = lax.rem(me_p // 2, 4)

    def offset_xy(dx, dy):
        return {"rep": lax.rem(me_x + dx, 4), "space": me_z * 8 + lax.rem(me_y + dy, 4) * 2 + core}

    def along_z(d):
        return {"rep": me_x, "space": lax.rem(me_p + 8 * d, 32)}

    def along_y(d, side):
        return {"rep": me_x, "space": me_z * 8 + lax.rem(me_y + d, 4) * 2 + side}

    loads = [
        pltpu.make_async_copy(a, b, in_sem.at[i])
        for i, (a, b) in enumerate(
            ((lat_hbm, latv), (wu_hbm, wu), (tt_hbm, tt), (wd_hbm, wd), (cot_hbm, cotv))
        )
    ]
    loads[0].start()
    barrier = pltpu.get_barrier_semaphore()

    for dx, dy in FAR_FIRST:
        pl.semaphore_signal(barrier, inc=1, device_id=offset_xy(dx, dy), device_id_type=MESH)
    for peer in [along_z(d) for d in (2, 1, 3)] + [along_y(d, 1 - core) for d in (2, 1, 3)] + [above, below, twin]:
        pl.semaphore_signal(barrier, inc=1, device_id=peer, device_id_type=MESH)
    for copy in loads[1:]:
        copy.start()

    def occupied(s):
        return jnp.minimum(jnp.maximum(cnt_ref[0] - s, 0), 1).astype(F32)

    def spot(s, x):
        if x in (0, 7):
            return pl.ds(pl.multiple_of(s * 224 + (64 if x else 0), 16), 64), None
        return (
            pl.ds(pl.multiple_of(s * 224 + 112 + 16 * x, 16), 16),
            pl.ds(pl.multiple_of(s * 288 + 848 + 48 * x, 16), 48),
        )

    def load_plane(ref, s, x, cols):
        edge, inner = spot(s, x)
        value = ref[edge, cols].astype(F32)
        width = value.shape[1]
        if inner is None:
            return value.reshape(8, 8, width)
        value = value.reshape(2, 8, width)
        inside = ref[inner, cols].astype(F32).reshape(6, 8, width)
        return jnp.concatenate([value[:1], inside, value[1:]], axis=0)

    def store_plane(ref, s, x, value):
        edge, inner = spot(s, x)
        value = value.reshape(8, 8, 256)
        if inner is None:
            ref[edge, :] = value.reshape(64, 256).astype(BF)
            return
        ref[edge, :] = jnp.concatenate([value[:1], value[7:]], axis=0).reshape(16, 256).astype(BF)
        ref[inner, :] = value[1:7].reshape(48, 256).astype(BF)

    def natural(s, x):
        return pl.ds(pl.multiple_of(s * 512 + x * 64, 64), 64)

    def remote(src, dst, send, recv, peer):
        return pltpu.make_async_remote_copy(
            src_ref=src, dst_ref=dst, send_sem=send, recv_sem=recv, device_id=peer, device_id_type=MESH
        )

    def pool_slot(s, edge):
        v = edge.astype(F32)
        middle = [128 + 16 * x for x in range(6)]
        pool[1 + 4 * s] = v[0:64]
        pool[2 + 4 * s] = v[64:128]
        pool[3 + 4 * s] = jnp.concatenate([v[0:8]] + [v[r:r + 8] for r in middle] + [v[64:72]], axis=0)
        pool[4 + 4 * s] = jnp.concatenate([v[56:64]] + [v[r + 8:r + 16] for r in middle] + [v[120:128]], axis=0)

    def face_copies(turn):
        return (
            remote(fsend.at[turn, 1], flow.at[turn], fs_sem.at[turn, 1], fr_sem.at[turn, 1], above),
            remote(fsend.at[turn, 0], fupp.at[turn], fs_sem.at[turn, 0], fr_sem.at[turn, 0], below),
        )

    def send_faces(turn):
        for k in range(2):
            for e in range(2):
                fsend[turn, k, e] = pool[1 + snd_ref[0, k, e]].astype(BF)
        for copy in face_copies(turn):
            copy.start()

    def take_faces(turn):
        for copy in face_copies(turn):
            copy.wait()
        lower = jnp.where(me_p > 0, 1.0, 0.0).astype(F32)
        upper = jnp.where(me_p < 31, 1.0, 0.0).astype(F32)
        for e in range(2):
            pool[17 + e] = flow[turn, e].astype(F32) * lower
            pool[19 + e] = fupp[turn, e].astype(F32) * upper

    zed = lax.broadcasted_iota(jnp.int32, (8, 128), 0)

    def taps(src, s, cols):
        def plane(x):
            return load_plane(src, s, x, cols)

        blank = jnp.zeros((1, 8, 128), F32)
        before = None
        here = plane(0)
        for x in range(8):
            after = plane(x + 1) if x < 7 else None
            y_low = jnp.concatenate([blank, here[:7]], axis=0)
            y_upp = jnp.concatenate([here[1:], blank], axis=0)
            yield x, (here, before, after, y_low, y_upp, pltpu.roll(here, 1, 1), pltpu.roll(here, 7, 1))
            before, here = here, after

    def tap_weights(b, cols, low, upp):
        w = [jnp.broadcast_to(dw_ref[i, b:b + 1, cols], (8, 128)) for i in range(7)]
        w[5] = jnp.where(zed == low, 0.0, w[5])
        w[6] = jnp.where(zed == upp, 0.0, w[6])
        return w

    def base_forward(b):
        for lane in range(2):
            cols = slice(lane * 128, lane * 128 + 128)
            w = tap_weights(b, cols, 0, 7)
            shift = jnp.broadcast_to(moment[:, cols], (8, 128))

            @pl.loop(0, 4)
            def _(s):
                for x, near in taps(field.at[b], s, cols):
                    total = shift[None]
                    for i in range(7):
                        if near[i] is not None:
                            total = total + w[i][None] * near[i]
                    rows = pl.ds(pl.multiple_of(s * 512 + x * 64, 64), 64)
                    base[rows, cols] = total.reshape(64, 128)

    def with_ghosts(sides, s, x, w):
        total = base[pl.ds(pl.multiple_of(s * 512 + x * 64, 64), 64), :]
        if x == 0:
            total = total + w[0] * sides[0]
        if x == 7:
            total = total + w[1] * sides[1]
        edge = slice(x * 8, x * 8 + 8)
        low = total[:8] + w[2] * sides[2][edge]
        upp = total[56:] + w[3] * sides[3][edge]
        return jnp.concatenate([low, total[8:56], upp], axis=0)

    def finish_forward(b):
        w = [dw_ref[i, b:b + 1, :] for i in (1, 2, 3, 4)]

        @pl.loop(0, 4)
        def _(s):
            sides = [pool[rcv_ref[s, side]] for side in range(4)]
            for side in range(4):
                ghost[b, s, side] = sides[side]
            for x in range(8):
                store_plane(act.at[b], s, x, with_ghosts(sides, s, x, w))

    mirror = (0, 2, 1, 4, 3, 6, 5)

    def base_backward(b, products):
        dsums[...] = jnp.zeros((7, 8, 256), F32)

        @pl.loop(0, 2)
        def _(h):
            part = pl.ds(pl.multiple_of(h * 512, 512), 512)
            for kind, left, right in products:
                tile = dot(left[...], right[:, part])
                for j in range(2):
                    k1[b, kind, 2 * h + j] = tile[:, j * 256:j * 256 + 256].reshape(2, 128, 256)
                    s1[b, kind, 2 * h + j] = k1[b, kind, 2 * h + j, 1 - core].astype(BF)
            for lane in range(2):
                cols = slice(lane * 128, lane * 128 + 128)
                w = tap_weights(b, cols, 7, 0)
                sums = [dsums[i, :, cols] for i in range(7)]
                for t in range(2):
                    s = 2 * h + t
                    for x, near in taps(dact, s, cols):
                        rows = pl.ds(pl.multiple_of(s * 512 + x * 64, 64), 64)
                        total = load_plane(grad, s, x, cols)
                        value = load_plane(field.at[b], s, x, cols)
                        here = near[0]
                        for i in range(7):
                            if near[mirror[i]] is not None:
                                total = total + w[i][None] * near[mirror[i]]
                                sums[i] = sums[i] + jnp.sum(value * near[mirror[i]], axis=0)
                        if x == 0:
                            sums[1] = sums[1] + jnp.sum(ghost[b, s, 0, :, cols].reshape(8, 8, 128) * here, axis=0)
                        if x == 7:
                            sums[2] = sums[2] + jnp.sum(ghost[b, s, 1, :, cols].reshape(8, 8, 128) * here, axis=0)
                        sums[3] = sums[3] + ghost[b, s, 2, x * 8:x * 8 + 8, cols] * here[0]
                        sums[4] = sums[4] + ghost[b, s, 3, x * 8:x * 8 + 8, cols] * here[7]
                        base[rows, cols] = total.reshape(64, 128)
                for i in range(7):
                    dsums[i, :, cols] = sums[i]

        for kind, left, right in products:
            c1(b, kind).start()
        inside = lax.broadcasted_iota(jnp.int32, (8, 256), 0)
        for i in range(7):
            total = dsums[i]
            if i == 5:
                total = jnp.where(inside == 7, 0.0, total)
            if i == 6:
                total = jnp.where(inside == 0, 0.0, total)
            dacc[7 * b + i:7 * b + i + 1, :] = jnp.sum(total, axis=0, keepdims=True)

    def finish_backward(b):
        w = [dw_ref[i, b:b + 1, :] for i in (2, 1, 4, 3)]

        @pl.loop(0, 4)
        def _(s):
            occ = occupied(s)
            sides = [pool[rcv_ref[s, side]] for side in range(4)]
            for x in range(8):
                total = with_ghosts(sides, s, x, w) * occ
                if b:
                    store_plane(grad, s, x, total)
                else:
                    out_ref[natural(s, x), :] = total.astype(BF)

    def c1(b, kind):
        return remote(s1.at[b, kind], r1.at[b, kind], c1s.at[b, kind], c1r.at[b, kind], twin)

    def weight_grad(b, kind, left, right):
        tile = dot(left[...], right[...])
        for j in range(4):
            k1[b, kind, j] = tile[:, j * 256:j * 256 + 256].reshape(2, 128, 256)
            s1[b, kind, j] = k1[b, kind, j, 1 - core].astype(BF)
        c1(b, kind).start()

    def wait_all(ref, send, recv):
        pltpu.make_async_copy(ref, ref, send).wait()
        pltpu.make_async_copy(ref, ref, recv).wait()

    def c2(b, kind, dx, dy):
        x, y = lax.rem(me_x + dx, 4), lax.rem(me_y + dy, 4)
        return remote(
            s2.at[b, kind, x * 4 + y], r2.at[b, kind, dx * 4 + dy - 1], c2s.at[b, kind], c2r.at[b, kind],
            offset_xy(dx, dy),
        )

    def step2(b, kind):
        c1(b, kind).wait()
        for j in range(4):
            total = k1[b, kind, j, core] + r1[b, kind, j].astype(F32)
            s2[b, kind, 4 * j:4 * j + 4] = total.reshape(4, 32, 256).astype(BF)

        for dx, dy in FAR_FIRST:
            c2(b, kind, dx, dy).start()

    def c3(b, kind, d):
        return remote(
            r3.at[b, kind, me_z], r3.at[b, kind, me_z], c3s.at[b, kind, d - 1], c3r.at[b, kind, d - 1], along_z(d)
        )

    def step3(b, kind):
        wait_all(r2.at[b, kind], c2s.at[b, kind], c2r.at[b, kind])
        rows = pl.ds(pl.multiple_of(me_y * 32, 32), 32)
        total = k1[b, kind, me_x, core, rows] + r1[b, kind, me_x, rows].astype(F32)
        for d in range(15):
            total = total + r2[b, kind, d].astype(F32)
        r3[b, kind, me_z] = total.astype(BF)
        for d in (2, 1, 3):
            c3(b, kind, d).start()

    def c5(b, kind, i):
        peers = [twin] + [along_y(d, side) for d in (1, 2, 3) for side in (core, 1 - core)]
        return remote(
            r5.at[b, kind, core, me_y], r5.at[b, kind, core, me_y], c5s.at[b, kind, i], c5r.at[b, kind, i], peers[i]
        )

    def step5(b, kind):
        for d in (1, 2, 3):
            c3(b, kind, d).wait()
        total = r3[b, kind, 0].astype(F32)
        for z in range(1, 4):
            total = total + r3[b, kind, z].astype(F32)
        r5[b, kind, core, me_y] = total.astype(BF)
        for i in (3, 4, 1, 2, 5, 6, 0):
            c5(b, kind, i).start()

    def finish(b, kind):
        for i in range(7):
            c5(b, kind, i).wait()
        for side in range(2):
            at = slice(side * 128, side * 128 + 128)
            total = r5[b, kind, side].reshape(128, 256).astype(F32) * scale
            if kind:
                gup_ref[b, at, :] = total
            else:
                gdn_ref[b, :, at] = total.T

    def e1():
        return remote(ds.at[0], dr1, e_s.at[0], e_r.at[0], twin)

    def e2(d):
        return remote(ds.at[1], dr2.at[0, d - 1], e_s.at[d], e_r.at[d], offset_xy(d, 0))

    def e3(d):
        return remote(ds.at[2], dr2.at[1, d - 1], e_s.at[3 + d], e_r.at[3 + d], along_z(d))

    def e4(d):
        return remote(ds.at[3], dr2.at[2, d - 1], e_s.at[6 + d], e_r.at[6 + d], along_y(d, core))

    def taps_start(stage, copy):
        ds[stage] = dacc[...].astype(BF)
        for d in (2, 1, 3):
            copy(d).start()

    def taps_take(stage, copy):
        for d in (1, 2, 3):
            copy(d).wait()
        dacc[...] = dacc[...] + dr2[stage - 1, 0].astype(F32) + dr2[stage - 1, 1].astype(F32) + dr2[stage - 1, 2].astype(F32)

    loads[0].wait()

    pool[0] = jnp.zeros((64, 256), F32)

    @pl.loop(0, 4)
    def _(s):
        occ = occupied(s)
        for x in range(8):
            plane = latv[natural(s, x), :].astype(F32) * occ
            store_plane(field.at[0], s, x, plane)
            if x == 0:
                pool[1 + 4 * s] = plane
            if x == 7:
                pool[2 + 4 * s] = plane
            pool[3 + 4 * s, x * 8:x * 8 + 8] = plane[:8]
            pool[4 + 4 * s, x * 8:x * 8 + 8] = plane[56:]

    pl.semaphore_wait(barrier, 24)
    send_faces(0)
    loads[2].wait()
    table_row = lax.broadcasted_iota(jnp.int32, (1000, 256), 0)
    moment = jnp.sum(jnp.where(table_row == ts_ref[0], tt[...], 0.0), axis=0, keepdims=True)
    base_forward(0)
    loads[1].wait()
    loads[3].wait()
    for b in range(2):
        wut[b] = wu[b].T
        wdt[b] = wd[b].T
    loads[4].wait()

    @pl.loop(0, 4)
    def _(s):
        occ = occupied(s)
        for x in range(8):
            store_plane(grad, s, x, cotv[natural(s, x), :].astype(F32) * occ)

    turn_g[...] = grad[...].T
    for n in range(4):
        part = slice(n * 256, n * 256 + 256)
        dp[:, part] = dot(grad[...], wdt[1, :, part]).astype(BF)
    take_faces(0)
    finish_forward(0)
    for first, size in ((0, 224), (896, 288)):
        group = slice(first, first + 4 * size)
        for n in range(4):
            part = slice(n * 256, n * 256 + 256)
            hid[0, group, part], slo[group, part] = gelu_pair(dot(act[0, group, :], wu[0, :, part]).astype(BF))
        for s in range(4):
            rows = slice(first + s * size, first + s * size + size)
            total = field[0, rows, :].astype(F32) + dot(hid[0, rows, :], wd[0])
            total = (total * occupied(s)).astype(BF)
            field[1, rows, :] = total
            if first == 0:
                pool_slot(s, total)
        if first == 0:
            send_faces(1)
    base_forward(1)
    turn_a[0] = act[0].T
    take_faces(1)
    finish_forward(1)

    turn_a[1] = act[1].T
    for n in range(4):
        part = slice(n * 256, n * 256 + 256)
        hidden, slope = gelu_pair(dot(act[1], wu[1, :, part]).astype(BF))
        hid[1, :, part] = hidden
        dp[:, part] = dp[:, part] * slope
    for s in range(4):
        rows = slice(s * 224, s * 224 + 224)
        total = dot(dp[rows, :], wut[1]).astype(BF)
        dact[rows, :] = total
        pool_slot(s, total)
    send_faces(2)
    dact[896:, :] = dot(dp[896:, :], wut[1]).astype(BF)
    weight_grad(1, 0, turn_g, hid.at[1])
    base_backward(1, ((1, turn_a.at[1], dp),))
    step2(1, 0)
    take_faces(2)
    finish_backward(1)
    step2(1, 1)

    turn_g[...] = grad[...].T
    weight_grad(0, 0, turn_g, hid.at[0])
    for n in range(4):
        part = slice(n * 256, n * 256 + 256)
        dp[:, part] = dot(grad[...], wdt[0, :, part]).astype(BF) * slo[:, part]
    step2(0, 0)
    weight_grad(0, 1, turn_a.at[0], dp)
    for s in range(4):
        rows = slice(s * 224, s * 224 + 224)
        total = dot(dp[rows, :], wut[0]).astype(BF)
        dact[rows, :] = total
        pool_slot(s, total)
    send_faces(3)
    dact[896:, :] = dot(dp[896:, :], wut[0]).astype(BF)
    step2(0, 1)
    step3(1, 0)
    step3(1, 1)
    dacc[14:16] = jnp.zeros((2, 256), F32)
    base_backward(0, ())
    ds[0] = dacc[...].astype(BF)
    e1().start()
    step3(0, 0)
    e1().wait()
    dacc[...] = dacc[...] + dr1[...].astype(F32)
    taps_start(1, e2)
    take_faces(3)
    finish_backward(0)
    step3(0, 1)
    step5(1, 0)
    step5(1, 1)
    step5(0, 0)
    taps_take(1, e2)
    taps_start(2, e3)
    step5(0, 1)
    taps_take(2, e3)
    taps_start(3, e4)
    finish(1, 0)
    finish(1, 1)
    finish(0, 0)
    taps_take(3, e4)
    dsum = dacc[...] * scale
    share = jnp.zeros((16, 64), F32)
    for j in range(4):
        share = jnp.where(me_x == j, dsum[:, j * 64:j * 64 + 64], share)
    for i in range(7):
        dep_ref[i, 0:1] = share[i:i + 1]
        dep_ref[i, 1:2] = share[7 + i:8 + i]
    finish(0, 1)


def store(*refs):
    sems = refs[8]
    copies = [pltpu.make_async_copy(refs[i], refs[4 + i], sems.at[i]) for i in range(4)]
    for copy in copies:
        copy.start()
    for copy in copies:
        copy.wait()


def on_device(latents, cotangent, w_up, w_down, depth_w, time_table, timesteps, brick_counts, send_list, recv_list):
    bricks, voxels, channels = latents.shape
    rows = bricks * voxels
    scale = 1.0 / math.sqrt(rows * lax.axis_size("rep") * lax.axis_size("space"))
    anywhere = pl.BlockSpec(memory_space=pl.ANY)
    vmem = pl.BlockSpec(memory_space=pltpu.VMEM)
    smem = pl.BlockSpec(memory_space=pltpu.SMEM)
    dma = pltpu.SemaphoreType.DMA
    results = pl.pallas_call(
        functools.partial(kernel, scale),
        out_shape=(
            pltpu.VMEM((rows, channels), BF),
            pltpu.VMEM((2, 256, 256), F32),
            pltpu.VMEM((2, 256, 256), F32),
            pltpu.VMEM((7, 2, 64), F32),
        ),
        in_specs=[anywhere] * 4 + [vmem, anywhere] + [smem] * 4,
        out_specs=(vmem, vmem, vmem, vmem),
        scratch_shapes=[
            pltpu.VMEM((rows, 256), BF),
            pltpu.VMEM((rows, 256), BF),
            pltpu.VMEM((2, 256, 1024), BF),
            pltpu.VMEM((2, 1024, 256), BF),
            pltpu.VMEM((1000, 256), F32),
            pltpu.VMEM((2, rows, 256), BF),
            pltpu.VMEM((2, rows, 256), BF),
            pltpu.VMEM((2, rows, 1024), BF),
            pltpu.VMEM((rows, 1024), BF),
            pltpu.VMEM((rows, 1024), BF),
            pltpu.VMEM((rows, 256), BF),
            pltpu.VMEM((256, rows), BF),
            pltpu.VMEM((2, 256, rows), BF),
            pltpu.VMEM((rows, 256), BF),
            pltpu.VMEM((21, 64, 256), F32),
            pltpu.VMEM((2, 4, 4, 64, 256), F32),
            pltpu.VMEM((rows, 256), F32),
            pltpu.VMEM((2, 1024, 256), BF),
            pltpu.VMEM((2, 256, 1024), BF),
            pltpu.VMEM((4, 2, 2, 64, 256), BF),
            pltpu.VMEM((4, 2, 64, 256), BF),
            pltpu.VMEM((4, 2, 64, 256), BF),
            pltpu.VMEM((2, 2, 4, 2, 128, 256), F32),
            pltpu.VMEM((2, 2, 4, 128, 256), BF),
            pltpu.VMEM((2, 2, 4, 128, 256), BF),
            pltpu.VMEM((2, 2, 16, 32, 256), BF),
            pltpu.VMEM((2, 2, 15, 32, 256), BF),
            pltpu.VMEM((2, 2, 4, 32, 256), BF),
            pltpu.VMEM((2, 2, 2, 4, 32, 256), BF),
            pltpu.VMEM((16, 256), F32),
            pltpu.VMEM((7, 8, 256), F32),
            pltpu.VMEM((4, 16, 256), BF),
            pltpu.VMEM((16, 256), BF),
            pltpu.VMEM((3, 3, 16, 256), BF),
            dma((5,)),
            dma((4, 2)),
            dma((4, 2)),
            dma((2, 2)),
            dma((2, 2)),
            dma((2, 2)),
            dma((2, 2)),
            dma((2, 2, 3)),
            dma((2, 2, 3)),
            dma((2, 2, 7)),
            dma((2, 2, 7)),
            dma((10,)),
            dma((10,)),
        ],
        compiler_params=pltpu.CompilerParams(
            collective_id=0, has_side_effects=True, vmem_limit_bytes=58 * 1024 * 1024
        ),
        name="blocks",
    )(
        latents.reshape(rows, channels),
        cotangent.reshape(rows, channels),
        w_up, w_down, depth_w.transpose(1, 0, 2), time_table, timesteps, brick_counts, send_list, recv_list,
    )
    out, up, down, depth = pl.pallas_call(
        store,
        out_shape=[jax.ShapeDtypeStruct(a.shape, a.dtype) for a in results],
        in_specs=[vmem] * 4,
        out_specs=[anywhere] * 4,
        scratch_shapes=[dma((4,))],
        name="store",
    )(*[pltpu.with_memory_space_constraint(a, pltpu.VMEM) for a in results])
    return out.reshape(latents.shape), up, down, depth.transpose(1, 0, 2)


def solution(mesh):
    spread = ("rep", "space")
    return jax.shard_map(
        on_device,
        mesh=mesh,
        in_specs=(
            P(spread, None, None),
            P(spread, None, None),
            P(), P(), P(), P(),
            P("rep"),
            P(spread),
            P(spread, None, None),
            P(spread, None),
        ),
        out_specs=(
            P(spread, None, None),
            P(None, None, "rep"),
            P(None, "rep", None),
            P(None, None, "rep"),
        ),
        check_vma=False,
    )
```
